512 devices in a mesh: row: 64 (over y_lo, z, core), grp: 8 (over y_hi, x).
Axes of the slice: x: 4, y: 4 (y_hi: 2, y_lo: 2; y = y_hi * 2 + y_lo), z: 16, core: 2. Of those that a mesh axis runs over, the one named last changes fastest.
Arguments:
- pair: bfloat16 [448, 448, 128], P('row', 'grp'), may hold values from -6 to 6
- pair_mask: int32 [448, 448], P('row', 'grp'), may hold values 0 or 1
- w_ab: bfloat16 [2, 128, 512], replicated, may hold values from -0.5 to 0.5
- w_gate: bfloat16 [2, 128, 128], replicated, may hold values from -0.5 to 0.5
- w_out: bfloat16 [2, 128, 128], replicated, may hold values from -0.5 to 0.5
Outputs:
- pair_out: bfloat16 [448, 448, 128], P('row', 'grp')
The draws below stay inside these ranges and needn't reach their ends.
All inputs are finite; a program needn't handle non-finite values. No bound on the sum of `pair_mask` on one device may be relied on, other than what follows from the above.
Results may differ from the reference program's by a relative error of at most 0.017.
Values may be sent and summed in bfloat16 or wider, within the bound.
A program may use at most 64 MiB of HBM per device.

```python
import jax
import jax.numpy as jnp
from jax import lax

C = 128
N_TOK = 448


def with_ends(drawn, key, smallest, largest):
    longest = drawn.shape.index(max(drawn.shape))
    spots = []
    for shift in (0, 1):
        where = [jax.random.randint(jax.random.fold_in(key, axis), (), 0, length) for axis, length in enumerate(drawn.shape)]
        where[longest] = (where[longest] + shift) % drawn.shape[longest]
        spots.append(tuple(where))
    return drawn.at[spots[0]].set(smallest).at[spots[1]].set(largest)


def level_of(stream_key, shape, shards, low, high):
    loudness = 1.0
    for dim, parts in shards:
        draws = jax.random.uniform(jax.random.fold_in(jax.random.fold_in(stream_key, 6), dim), (parts,), jnp.float32, low / len(shards), high / len(shards))
        loudness = loudness * jnp.repeat(jnp.exp(draws), shape[dim] // parts).reshape((-1,) + (1,) * (len(shape) - 1 - dim))
    return loudness


def scatter_about(stream_key, shape, scale, limit, split=(), held_as=jnp.bfloat16):
    level = level_of(stream_key, shape, split, -0.22, 0.18) if split else 1.0
    values = jax.random.normal(stream_key, shape, jnp.float32) * scale * level
    return jnp.minimum(jnp.maximum(values, -limit), limit).astype(held_as)


def setup_inputs(seed: int = 0) -> dict:
    splits = jax.random.split(jax.random.key(seed), 6)
    pair = scatter_about(splits[0], (N_TOK, N_TOK, C), 1.0, 6.0, ((0, 64), (1, 8)))
    pair_mask = with_ends((jax.random.randint(splits[1], (N_TOK, N_TOK), 0, 8) < 7).astype(jnp.int32), jax.random.fold_in(splits[1], 1), 0, 1)
    w_ab = scatter_about(splits[2], (2, C, 4 * C), C ** -0.5, 0.5)
    w_gate = scatter_about(splits[3], (2, C, C), C ** -0.5, 0.5)
    w_out = scatter_about(splits[4], (2, C, C), C ** -0.5, 0.5)
    return {"pair": pair, "pair_mask": pair_mask, "w_ab": w_ab, "w_gate": w_gate, "w_out": w_out}


def normalize(values, axis):
    mean = lax.optimization_barrier(jnp.mean(values, axis=axis, keepdims=True))
    centered = values - mean
    var = lax.optimization_barrier(jnp.mean(centered * centered, axis=axis, keepdims=True))
    return centered * jax.lax.rsqrt(var + 1e-05)

def update(pair, keep, w_ab, w_gate, w_out, incoming):
    width = pair.shape[2]
    pair_f = pair.astype(jnp.float32)
    normed = normalize(pair_f, 2).astype(jnp.bfloat16)
    proj = jnp.einsum('ijc,cf->fij', normed.astype(jnp.float32), w_ab.astype(jnp.float32))
    left = (jax.nn.sigmoid(proj[:width]) * proj[width:2 * width] * keep).astype(jnp.bfloat16)
    right = (jax.nn.sigmoid(proj[2 * width:3 * width]) * proj[3 * width:] * keep).astype(jnp.bfloat16)
    gate = jax.nn.sigmoid(jnp.einsum('ijc,cd->ijd', normed.astype(jnp.float32), w_gate.astype(jnp.float32)))
    if incoming:
        tri = jnp.einsum('cki,ckj->cij', left.astype(jnp.float32), right.astype(jnp.float32))
    else:
        tri = jnp.einsum('cik,cjk->cij', left.astype(jnp.float32), right.astype(jnp.float32))
    tri = tri.astype(jnp.bfloat16)
    tnorm = normalize(tri.astype(jnp.float32), 0).astype(jnp.bfloat16)
    out = jnp.einsum('cij,cd->ijd', tnorm.astype(jnp.float32), w_out.astype(jnp.float32))
    return (pair_f + gate * out).astype(jnp.bfloat16)

def reference(pair, pair_mask, w_ab, w_gate, w_out):
    keep = pair_mask.astype(jnp.float32)
    first = update(pair, keep, w_ab[0], w_gate[0], w_out[0], False)
    return update(first, keep, w_ab[1], w_gate[1], w_out[1], True)
```

```python
import jax
import jax.numpy as jnp
from jax import lax
from jax.experimental import pallas as pl
from jax.experimental.pallas import tpu as pltpu
from jax.sharding import PartitionSpec as P

MESH = pl.DeviceIdType.MESH
F32, BF16 = jnp.float32, jnp.bfloat16
NZ, NG, ROWS, COLS, RS, MS, CH = 16, 8, 7, 56, 8, 64, 128
TOK = RS * MS
HALF = TOK // 2
AROUND = (8, 7, 9, 6, 10, 5, 11, 4, 12, 3, 13, 2, 14, 1, 15)
EARLY, LATE = 0, 1
F1, F2, MATE, B1, B2, STAGES = 0, 2, 4, 5, 7, 9


def mm(a, b, ca=1, cb=0):
    return lax.dot_general(a, b, (((ca,), (cb,)), ((), ())), preferred_element_type=F32)


def iota2(shape):
    return lax.broadcasted_iota(jnp.int32, shape, 0), lax.broadcasted_iota(jnp.int32, shape, 1)


def one_hot(hit):
    return jnp.where(hit, 1.0, 0.0).astype(BF16)


def normalize(x, axes):
    count = 1
    for a in axes:
        count *= x.shape[a]
    mean = jnp.sum(x, axis=axes, keepdims=True) * (1.0 / count)
    cen = x - mean
    var = jnp.sum(cen * cen, axis=axes, keepdims=True) * (1.0 / count)
    return cen * lax.rsqrt(var + 1e-05)


def sigmoid(x):
    return 0.5 * jnp.tanh(0.5 * x) + 0.5


def swap_halves(a, b):
    low = lax.broadcasted_iota(jnp.int32, a.shape, a.ndim - 1) < 64
    return jnp.where(low, a, pltpu.roll(b, 64, a.ndim - 1)), jnp.where(low, pltpu.roll(a, 64, a.ndim - 1), b)


def kernel(
    pair_hbm, mask_hbm, wab_hbm, wg_hbm, wo_hbm, out_ref,
    pair_ref, mask_ref, wab_ref, wg_ref, wo_ref, wabt, wgt, wot, perm, cols,
    ztok, zt, zn, gate, sides, s1, r1, s2, r2, y0, y1, e0, e1, s3, r3, s4, r4, insem, ssem, rsem,
):
    loads = [
        pltpu.make_async_copy(src, dst, insem.at[n])
        for n, (src, dst) in enumerate(
            ((pair_hbm, pair_ref), (wab_hbm, wab_ref), (mask_hbm, mask_ref), (wg_hbm, wg_ref), (wo_hbm, wo_ref))
        )
    ]
    for load in loads:
        load.start()

    row, g = lax.axis_index("row"), lax.axis_index("grp")
    core = lax.rem(row, 2)
    z = lax.rem(row // 2, NZ)
    yl = row // (2 * NZ)

    mate = 1 - core

    def dev(yl_, z_, core_, g_):
        return (yl_ * (2 * NZ) + z_ * 2 + core_, g_)

    barrier = pltpu.get_barrier_semaphore()

    def greet(device):
        pl.semaphore_signal(barrier, inc=1, device_id=device, device_id_type=MESH)

    for d in AROUND:
        greet(dev(yl, lax.rem(z + d, NZ), core, g))

    def send(src, dst, u, stage, device, is_self=None):
        def remote():
            pltpu.make_async_remote_copy(
                src_ref=src, dst_ref=dst, send_sem=ssem.at[u, stage], recv_sem=rsem.at[u, stage],
                device_id=device, device_id_type=MESH,
            ).start()

        if is_self is None:
            remote()
            return

        @pl.when(is_self)
        def _():
            pltpu.make_async_copy(src, dst, rsem.at[u, stage]).start()

        pl.when(jnp.logical_not(is_self))(remote)

    def send_z(src, dst, u, stage):
        for d in AROUND:
            to = lax.rem(z + d, NZ)
            send(src.at[to], dst.at[z], u, stage, dev(yl, to, core, g))
        pltpu.make_async_copy(src.at[z], dst.at[z], rsem.at[u, stage]).start()

    def wait_all(ref, sem):
        pltpu.make_async_copy(ref, ref, sem).wait()

    ztok[...] = jnp.zeros_like(ztok)
    loads[0].wait()
    for r in range(ROWS):
        ztok[pl.ds(r * MS, COLS), :] = pair_ref[r].astype(F32)
    zt[...] = ztok[...].T
    for dy in range(2):
        for dc in range(2):
            for dg in range(NG):
                if dy or dc or dg:
                    greet(dev(yl if dy == 0 else 1 - yl, z, core if dc == 0 else mate, lax.rem(g + dg, NG)))
    for load in loads[1:]:
        load.wait()
    wabt[0] = wab_ref[0].T

    k, l = iota2((COLS, TOK))
    spread = mm(mask_ref[...].astype(F32).astype(BF16), one_hot(lax.rem(l, MS) == k))
    k, l = iota2((ROWS, TOK))
    keep = jnp.sum(jnp.where(l // MS == k, spread, 0.0), axis=0, keepdims=True)

    def lanes(h):
        return slice(HALF * h, HALF * h + HALF)

    def norm(h):
        zn[:, lanes(h)] = normalize(zt[:, lanes(h)], (0,)).astype(BF16)

    def project(u, h, e):
        base = 0 if u != e else 2 * CH
        p = mm(wabt[u, base : base + 2 * CH, :], zn[:, lanes(h)])
        value = sigmoid(p[:CH]) * p[CH:] * keep[:, lanes(h)]
        sides[e, :, NG * h : NG * h + NG, :] = value.reshape(NZ, NG, HALF)

    def push(u, e):
        s1[u, e] = sides[e].astype(BF16)
        send_z(s1.at[u, e], r1.at[u, e], u, F1 + e)

    def constants():
        wgt[0], wgt[1] = wg_ref[0].T, wg_ref[1].T
        wot[0], wot[1] = wo_ref[0].T, wo_ref[1].T
        wabt[1] = wab_ref[1].T
        o, i = iota2((256, 256))
        perm[...] = one_hot(i == lax.rem(o, 16) * 16 + o // 16)
        i, l = iota2((224, 256))
        zi, n = lax.rem(i, NZ), i // NZ
        ci = jnp.where(n < 8, n // 4, (n - 8) // 3)
        ri = jnp.where(n < 8, lax.rem(n, 4), 4 + lax.rem(n - 8, 3))
        cols[...] = one_hot(l == zi // 4 * MS + lax.rem(zi, 4) * 14 + ci * 7 + ri)

    def channels_apart(u, e):
        x = mm(perm[...], r1[u, e].reshape(256, HALF)).astype(BF16)
        for h in range(2):
            s2[u, e, :, :, lanes(h)] = x[128 * h : 128 * h + 128].reshape(NG, NZ, HALF)

    def send_early(u, a, slot):
        for d in (4, 3, 5, 2, 6, 1, 7, 0):
            h = lax.rem(g + d, NG)
            for yl_to in (yl, 1 - yl):
                send(
                    s2.at[u, EARLY, h], r2.at[u, EARLY, slot], u, F2 + EARLY, dev(yl_to, z, a, h),
                    a == core if d == 0 and yl_to is yl else None,
                )

    def send_late(u, a, slot):
        for d in (4, 3, 5, 2, 6, 1, 7, 0):
            h = lax.rem(g + d, NG)
            send(
                s2.at[u, LATE, h], r2.at[u, LATE, slot], u, F2 + LATE, dev(a, z, core, h), a == yl if d == 0 else None
            )

    def assemble(u, e, cs):
        n_src, n_g = (1, 8) if u == 0 else (2, 4)
        for s in range(n_src):
            for q in range(n_g // 2):
                for t in range(4):
                    at = slice(128 * t, 128 * t + 128)
                    slot = cs * NG + s * n_g + 2 * q
                    lo, hi = swap_halves(r2[u, e, slot, :, at], r2[u, e, slot + 1, :, at])
                    to_lanes = slice(128 * q, 128 * q + 128)
                    for r, x in ((2 * t, lo), (2 * t + 1, hi)):
                        if r == ROWS:
                            continue
                        if u == 1:
                            block = (cs * 2 + s) * ROWS + r
                        elif r < 4:
                            block = cs * 4 + r
                        else:
                            block = 8 + cs * 3 + r - 4
                        to_rows = pl.ds(pl.multiple_of(block * NZ, NZ), NZ) if cs is core or cs is mate else pl.ds(block * NZ, NZ)
                        if u == 0:
                            y0[e, to_rows, to_lanes] = x
                        else:
                            y1[e, to_rows, to_lanes] = x

    def finish(u, h):
        x = r4[u, h].astype(F32).reshape(NZ, 2, NG, 128)
        tn = jnp.concatenate([normalize(x[:, t], (0, 1)).reshape(CH, 128) for t in range(2)], axis=1).astype(BF16)
        out = mm(wot[u], tn)
        zt[:, lanes(h)] = (zt[:, lanes(h)] + gate[:, lanes(h)] * out).astype(BF16).astype(F32)

    for u in range(2):
        a = yl if u == 0 else g // 4
        slot = core * NG + g if u == 0 else (core * 2 + yl) * 4 + lax.rem(g, 4)
        if u == 0:
            norm(0)
            norm(1)
            project(u, 0, EARLY)
            project(u, 1, EARLY)
            pl.semaphore_wait(barrier, NZ - 1 + 4 * NG - 1)
            push(u, EARLY)
            project(u, 0, LATE)
            project(u, 1, LATE)
            push(u, LATE)
            constants()
        else:
            project(u, 1, EARLY)
            push(u, EARLY)
            project(u, 1, LATE)
            push(u, LATE)
        gate[...] = sigmoid(mm(wgt[u], zn[...]))

        wait_all(r1.at[u, EARLY], rsem.at[u, F1 + EARLY])
        channels_apart(u, EARLY)
        send_early(u, a, slot)
        wait_all(r1.at[u, LATE], rsem.at[u, F1 + LATE])
        channels_apart(u, LATE)
        send_late(u, a, slot)

        wait_all(r2.at[u, EARLY], rsem.at[u, F2 + EARLY])
        assemble(u, EARLY, 0)
        assemble(u, EARLY, 1)
        if u == 0:
            e0[...] = mm(y0[EARLY], cols[...], 0, 0).astype(BF16)
        else:
            e1[...] = mm(cols[...], y1[EARLY], 1, 1).astype(BF16)

        own = r2.at[u, LATE, pl.ds(core * NG, NG)]
        wait_all(own, rsem.at[u, F2 + LATE])
        hand = pltpu.make_async_remote_copy(
            src_ref=own, dst_ref=own, send_sem=ssem.at[u, MATE], recv_sem=rsem.at[u, MATE],
            device_id=dev(yl, z, mate, g), device_id_type=MESH,
        )
        hand.start()
        assemble(u, LATE, core)
        hand.wait_recv()
        assemble(u, LATE, mate)

        i_half, j_half = (yl, core) if u == 0 else (core, yl)
        for h in range(2):
            n_r = 4 - h
            rows = slice(128 * h, 128 * h + 32 * n_r)
            if u == 0:
                tri = mm(y0[LATE, rows, :], e0[...]).astype(BF16)
            else:
                tri = mm(e1[rows, :], y1[LATE]).astype(BF16)
            for ci in range(2):
                for t in range(2):
                    for q in range(2):
                        at = slice(128 * q, 128 * q + 128)
                        base = (ci * n_r + 2 * t) * NZ
                        c0 = tri[base : base + NZ, at]
                        c1 = tri[base + NZ : base + 2 * NZ, at] if 2 * t + 1 < n_r else jnp.zeros_like(c0)
                        lo, hi = swap_halves(c0, c1)
                        s3[u, h, ci * 4 + 2 * q, :, 128 * t : 128 * t + 128] = lo
                        s3[u, h, ci * 4 + 2 * q + 1, :, 128 * t : 128 * t + 128] = hi

            for d in (2, 1, 3, 0):
                q = lax.rem(g + d, 4)
                to = 4 * j_half + q
                for ci in (mate, core):
                    send(
                        s3.at[u, h, ci * 4 + q], r3.at[u, h, g], u, B1 + h, dev(i_half, z, ci, to),
                        (i_half == yl) & (to == g) if d == 0 and ci is core else None,
                    )

        for h in range(2):
            wait_all(r3.at[u, h], rsem.at[u, B1 + h])
            x = r3[u, h].reshape(NG * NZ, HALF)
            x = jnp.concatenate([x[:, :128], x[:, 128:]], axis=0)
            s4[u, h] = mm(perm[...], x).astype(BF16).reshape(NZ, 16, 128)
            send_z(s4.at[u, h], r4.at[u, h], u, B2 + h)
        for h in range(2):
            wait_all(r4.at[u, h], rsem.at[u, B2 + h])
            finish(u, h)
            if u == 0:
                norm(h)
                if h == 0:
                    project(1, h, EARLY)
                    project(1, h, LATE)

    ztok[...] = zt[...].T
    for r in range(ROWS):
        out_ref[r] = ztok[pl.ds(r * MS, COLS), :].astype(BF16)

    def wait_sent(u, stage, ref, count, less):
        @pl.when(less)
        def _():
            wait_all(ref.at[pl.ds(0, count - 1)], ssem.at[u, stage])

        @pl.when(jnp.logical_not(less))
        def _():
            wait_all(ref.at[pl.ds(0, count)], ssem.at[u, stage])

    for u in range(2):
        a = yl if u == 0 else g // 4
        for e in (EARLY, LATE):
            wait_all(s1.at[u, e, pl.ds(0, NZ - 1)], ssem.at[u, F1 + e])
        wait_sent(u, F2 + EARLY, r2.at[u, EARLY], 2 * NG, a == core)
        wait_sent(u, F2 + LATE, s2.at[u, LATE], NG, a == yl)
        wait_all(r2.at[u, LATE, pl.ds(0, NG)], ssem.at[u, MATE])
        for h in range(2):
            wait_sent(u, B1 + h, s3.at[u, h], 8, g // 4 == core if u == 0 else (core == yl) & (g // 4 == yl))
            wait_all(s4.at[u, h, pl.ds(0, NZ - 1)], ssem.at[u, B2 + h])


def body(pair, pair_mask, w_ab, w_gate, w_out):
    return pl.pallas_call(
        kernel,
        out_shape=pltpu.VMEM(pair.shape, pair.dtype),
        in_specs=[pl.BlockSpec(memory_space=pltpu.HBM)] * 5,
        out_specs=pl.BlockSpec(memory_space=pltpu.VMEM),
        scratch_shapes=[
            pltpu.VMEM((ROWS, COLS, CH), BF16),
            pltpu.VMEM((ROWS, COLS), jnp.int32),
            pltpu.VMEM((2, CH, 4 * CH), BF16),
            pltpu.VMEM((2, CH, CH), BF16),
            pltpu.VMEM((2, CH, CH), BF16),
            pltpu.VMEM((2, 4 * CH, CH), BF16),
            pltpu.VMEM((2, CH, CH), BF16),
            pltpu.VMEM((2, CH, CH), BF16),
            pltpu.VMEM((256, 256), BF16),
            pltpu.VMEM((224, 256), BF16),
            pltpu.VMEM((TOK, CH), F32),
            pltpu.VMEM((CH, TOK), F32),
            pltpu.VMEM((CH, TOK), BF16),
            pltpu.VMEM((CH, TOK), F32),
            pltpu.VMEM((2, NZ, 16, HALF), F32),
            pltpu.VMEM((2, 2, NZ, 16, HALF), BF16),
            pltpu.VMEM((2, 2, NZ, 16, HALF), BF16),
            pltpu.VMEM((2, 2, NG, NZ, TOK), BF16),
            pltpu.VMEM((2, 2, 16, NZ, TOK), BF16),
            pltpu.VMEM((2, 224, 512), BF16),
            pltpu.VMEM((2, 448, 256), BF16),
            pltpu.VMEM((512, 256), BF16),
            pltpu.VMEM((224, 448), BF16),
            pltpu.VMEM((2, 2, 8, NZ, HALF), BF16),
            pltpu.VMEM((2, 2, 8, NZ, HALF), BF16),
            pltpu.VMEM((2, 2, NZ, 16, 128), BF16),
            pltpu.VMEM((2, 2, NZ, 16, 128), BF16),
            pltpu.SemaphoreType.DMA((5,)),
            pltpu.SemaphoreType.DMA((2, STAGES)),
            pltpu.SemaphoreType.DMA((2, STAGES)),
        ],
        compiler_params=pltpu.CompilerParams(
            collective_id=0, has_side_effects=True, vmem_limit_bytes=32 * 1024 * 1024
        ),
        name="triangle",
    )(*(pltpu.with_memory_space_constraint(x, pltpu.HBM) for x in (pair, pair_mask, w_ab, w_gate, w_out)))


def solution(mesh):
    return jax.shard_map(
        body,
        mesh=mesh,
        in_specs=(P("row", "grp", None), P("row", "grp"), P(), P(), P()),
        out_specs=P("row", "grp", None),
        check_vma=False,
    )
```

```python
import jax
import jax.numpy as jnp
from jax import lax
from jax.experimental import pallas as pl
from jax.experimental.pallas import tpu as pltpu
from jax.sharding import PartitionSpec as P

MESH = pl.DeviceIdType.MESH
F32, BF16 = jnp.float32, jnp.bfloat16
NZ, NG, ROWS, COLS, RS, MS, CH = 16, 8, 7, 56, 8, 64, 128
TOK = RS * MS
HALF = TOK // 2
AROUND = (8, 7, 9, 6, 10, 5, 11, 4, 12, 3, 13, 2, 14, 1, 15)
EARLY, LATE = 0, 1
F1, F2, MATE, B1, B2, STAGES = 0, 1, 3, 4, 5, 6


def mm(a, b, ca=1, cb=0):
    return lax.dot_general(a, b, (((ca,), (cb,)), ((), ())), preferred_element_type=F32)


def iota2(shape):
    return lax.broadcasted_iota(jnp.int32, shape, 0), lax.broadcasted_iota(jnp.int32, shape, 1)


def one_hot(hit):
    return jnp.where(hit, 1.0, 0.0).astype(BF16)


def normalize(x, axes):
    count = 1
    for a in axes:
        count *= x.shape[a]
    mean = jnp.sum(x, axis=axes, keepdims=True) * (1.0 / count)
    cen = x - mean
    var = jnp.sum(cen * cen, axis=axes, keepdims=True) * (1.0 / count)
    return cen * lax.rsqrt(var + 1e-05)


def sigmoid(x):
    return 0.5 * jnp.tanh(0.5 * x) + 0.5


def swap_halves(a, b):
    low = lax.broadcasted_iota(jnp.int32, a.shape, a.ndim - 1) < 64
    return jnp.where(low, a, pltpu.roll(b, 64, a.ndim - 1)), jnp.where(low, pltpu.roll(a, 64, a.ndim - 1), b)


def kernel(
    pair_hbm, mask_hbm, wab_hbm, wg_hbm, wo_hbm, out_ref,
    pair_ref, mask_ref, wab_ref, wg_ref, wo_ref, wabt, wgt, wot, perm, cols,
    ztok, zt, zn, gate, sides, s1, r1, s2, r2, y0, y1, e0, e1, s3, r3, s4, r4, insem, ssem, rsem,
):
    loads = [
        pltpu.make_async_copy(src, dst, insem.at[n])
        for n, (src, dst) in enumerate(
            ((pair_hbm, pair_ref), (wab_hbm, wab_ref), (mask_hbm, mask_ref), (wg_hbm, wg_ref), (wo_hbm, wo_ref))
        )
    ]
    for load in loads:
        load.start()

    row, g = lax.axis_index("row"), lax.axis_index("grp")
    core = lax.rem(row, 2)
    z = lax.rem(row // 2, NZ)
    yl = row // (2 * NZ)

    mate = 1 - core

    def dev(yl_, z_, core_, g_):
        return (yl_ * (2 * NZ) + z_ * 2 + core_, g_)

    barrier = pltpu.get_barrier_semaphore()

    def greet(device):
        pl.semaphore_signal(barrier, inc=1, device_id=device, device_id_type=MESH)

    for d in AROUND:
        greet(dev(yl, lax.rem(z + d, NZ), core, g))

    def send(src, dst, u, stage, device, is_self=None):
        def remote():
            pltpu.make_async_remote_copy(
                src_ref=src, dst_ref=dst, send_sem=ssem.at[u, stage], recv_sem=rsem.at[u, stage],
                device_id=device, device_id_type=MESH,
            ).start()

        if is_self is None:
            remote()
            return

        @pl.when(is_self)
        def _():
            pltpu.make_async_copy(src, dst, rsem.at[u, stage]).start()

        pl.when(jnp.logical_not(is_self))(remote)

    def send_z(src, dst, u, stage):
        for d in AROUND:
            to = lax.rem(z + d, NZ)
            send(src.at[to], dst.at[z], u, stage, dev(yl, to, core, g))
        pltpu.make_async_copy(src.at[z], dst.at[z], rsem.at[u, stage]).start()

    def wait_all(ref, sem):
        pltpu.make_async_copy(ref, ref, sem).wait()

    ztok[...] = jnp.zeros_like(ztok)
    loads[0].wait()
    for r in range(ROWS):
        ztok[pl.ds(r * MS, COLS), :] = pair_ref[r].astype(F32)
    zt[...] = ztok[...].T
    for dy in range(2):
        for dc in range(2):
            for dg in range(NG):
                if dy or dc or dg:
                    greet(dev(yl if dy == 0 else 1 - yl, z, core if dc == 0 else mate, lax.rem(g + dg, NG)))
    for load in loads[1:]:
        load.wait()
    wabt[0] = wab_ref[0].T

    k, l = iota2((COLS, TOK))
    spread = mm(mask_ref[...].astype(F32).astype(BF16), one_hot(lax.rem(l, MS) == k))
    k, l = iota2((ROWS, TOK))
    keep = jnp.sum(jnp.where(l // MS == k, spread, 0.0), axis=0, keepdims=True)

    def lanes(h):
        return slice(HALF * h, HALF * h + HALF)

    def norm(h):
        zn[:, lanes(h)] = normalize(zt[:, lanes(h)], (0,)).astype(BF16)

    def project(u, h, e):
        base = 0 if u != e else 2 * CH
        p = mm(wabt[u, base : base + 2 * CH, :], zn[:, lanes(h)])
        value = sigmoid(p[:CH]) * p[CH:] * keep[:, lanes(h)]
        sides[e, :, NG * h : NG * h + NG, :] = value.reshape(NZ, NG, HALF)

    def push(u):
        s1[u] = jnp.concatenate([sides[EARLY], sides[LATE]], axis=1).astype(BF16)
        send_z(s1.at[u], r1.at[u], u, F1)

    def constants():
        wgt[0], wgt[1] = wg_ref[0].T, wg_ref[1].T
        wot[0], wot[1] = wo_ref[0].T, wo_ref[1].T
        wabt[1] = wab_ref[1].T
        o, i = iota2((256, 256))
        perm[...] = one_hot(i == lax.rem(o, 16) * 16 + o // 16)
        i, l = iota2((224, 256))
        zi, n = lax.rem(i, NZ), i // NZ
        ci = jnp.where(n < 8, n // 4, (n - 8) // 3)
        ri = jnp.where(n < 8, lax.rem(n, 4), 4 + lax.rem(n - 8, 3))
        cols[...] = one_hot(l == zi // 4 * MS + lax.rem(zi, 4) * 14 + ci * 7 + ri)

    def channels_apart(u, e):
        x = mm(perm[...], r1[u, :, 16 * e : 16 * e + 16, :].reshape(256, HALF)).astype(BF16)
        for h in range(2):
            s2[u, e, :, :, lanes(h)] = x[128 * h : 128 * h + 128].reshape(NG, NZ, HALF)

    def send_early(u, a, slot):
        for d in (4, 3, 5, 2, 6, 1, 7, 0):
            h = lax.rem(g + d, NG)
            for yl_to in (yl, 1 - yl):
                send(
                    s2.at[u, EARLY, h], r2.at[u, EARLY, slot], u, F2 + EARLY, dev(yl_to, z, a, h),
                    a == core if d == 0 and yl_to is yl else None,
                )

    def send_late(u, a, slot):
        for d in (4, 3, 5, 2, 6, 1, 7, 0):
            h = lax.rem(g + d, NG)
            send(
                s2.at[u, LATE, h], r2.at[u, LATE, slot], u, F2 + LATE, dev(a, z, core, h), a == yl if d == 0 else None
            )

    def assemble(u, e, cs):
        n_src, n_g = (1, 8) if u == 0 else (2, 4)
        for s in range(n_src):
            for q in range(n_g // 2):
                for t in range(4):
                    at = slice(128 * t, 128 * t + 128)
                    slot = cs * NG + s * n_g + 2 * q
                    lo, hi = swap_halves(r2[u, e, slot, :, at], r2[u, e, slot + 1, :, at])
                    to_lanes = slice(128 * q, 128 * q + 128)
                    for r, x in ((2 * t, lo), (2 * t + 1, hi)):
                        if r == ROWS:
                            continue
                        if u == 1:
                            block = (cs * 2 + s) * ROWS + r
                        elif r < 4:
                            block = cs * 4 + r
                        else:
                            block = 8 + cs * 3 + r - 4
                        to_rows = pl.ds(pl.multiple_of(block * NZ, NZ), NZ) if cs is core or cs is mate else pl.ds(block * NZ, NZ)
                        if u == 0:
                            y0[e, to_rows, to_lanes] = x
                        else:
                            y1[e, to_rows, to_lanes] = x

    def finish(u, h):
        x = r4[u, :, 16 * h : 16 * h + 16, :].astype(F32).reshape(NZ, 2, NG, 128)
        tn = jnp.concatenate([normalize(x[:, t], (0, 1)).reshape(CH, 128) for t in range(2)], axis=1).astype(BF16)
        out = mm(wot[u], tn)
        zt[:, lanes(h)] = (zt[:, lanes(h)] + gate[:, lanes(h)] * out).astype(BF16).astype(F32)

    for u in range(2):
        a = yl if u == 0 else g // 4
        slot = core * NG + g if u == 0 else (core * 2 + yl) * 4 + lax.rem(g, 4)
        if u == 0:
            norm(0)
            norm(1)
        for h in range(2):
            project(u, h, EARLY)
            project(u, h, LATE)
        if u == 0:
            pl.semaphore_wait(barrier, NZ - 1 + 4 * NG - 1)
        push(u)
        if u == 0:
            constants()
        gate[...] = sigmoid(mm(wgt[u], zn[...]))

        wait_all(r1.at[u], rsem.at[u, F1])
        channels_apart(u, EARLY)
        send_early(u, a, slot)
        channels_apart(u, LATE)
        send_late(u, a, slot)

        wait_all(r2.at[u, EARLY], rsem.at[u, F2 + EARLY])
        assemble(u, EARLY, 0)
        assemble(u, EARLY, 1)
        if u == 0:
            e0[...] = mm(y0[EARLY], cols[...], 0, 0).astype(BF16)
        else:
            e1[...] = mm(cols[...], y1[EARLY], 1, 1).astype(BF16)

        own = r2.at[u, LATE, pl.ds(core * NG, NG)]
        wait_all(own, rsem.at[u, F2 + LATE])
        hand = pltpu.make_async_remote_copy(
            src_ref=own, dst_ref=own, send_sem=ssem.at[u, MATE], recv_sem=rsem.at[u, MATE],
            device_id=dev(yl, z, mate, g), device_id_type=MESH,
        )
        hand.start()
        assemble(u, LATE, core)
        hand.wait_recv()
        assemble(u, LATE, mate)

        i_half, j_half = (yl, core) if u == 0 else (core, yl)
        for h in range(2):
            n_r = 4 - h
            rows = slice(128 * h, 128 * h + 32 * n_r)
            if u == 0:
                tri = mm(y0[LATE, rows, :], e0[...]).astype(BF16)
            else:
                tri = mm(e1[rows, :], y1[LATE]).astype(BF16)
            for ci in range(2):
                for t in range(2):
                    for q in range(2):
                        at = slice(128 * q, 128 * q + 128)
                        base = (ci * n_r + 2 * t) * NZ
                        c0 = tri[base : base + NZ, at]
                        c1 = tri[base + NZ : base + 2 * NZ, at] if 2 * t + 1 < n_r else jnp.zeros_like(c0)
                        lo, hi = swap_halves(c0, c1)
                        tile = slice(HALF * h + 128 * t, HALF * h + 128 * t + 128)
                        s3[u, ci * 4 + 2 * q, :, tile] = lo
                        s3[u, ci * 4 + 2 * q + 1, :, tile] = hi

        for d in (2, 1, 3, 0):
            q = lax.rem(g + d, 4)
            to = 4 * j_half + q
            for ci in (mate, core):
                send(
                    s3.at[u, ci * 4 + q], r3.at[u, g], u, B1, dev(i_half, z, ci, to),
                    (i_half == yl) & (to == g) if d == 0 and ci is core else None,
                )

        wait_all(r3.at[u], rsem.at[u, B1])
        x = r3[u].reshape(NG * NZ, TOK)
        x = jnp.concatenate(
            [
                jnp.concatenate([x[:, :128], x[:, 256:384]], axis=1),
                jnp.concatenate([x[:, 128:256], x[:, 384:]], axis=1),
            ],
            axis=0,
        )
        x = mm(perm[...], x).astype(BF16).reshape(NZ, 16, 256)
        s4[u] = jnp.concatenate([x[:, :, :128], x[:, :, 128:]], axis=1)
        send_z(s4.at[u], r4.at[u], u, B2)
        wait_all(r4.at[u], rsem.at[u, B2])
        for h in range(2):
            finish(u, h)
            if u == 0:
                norm(h)

    ztok[...] = zt[...].T
    for r in range(ROWS):
        out_ref[r] = ztok[pl.ds(r * MS, COLS), :].astype(BF16)

    def wait_sent(u, stage, ref, count, less):
        @pl.when(less)
        def _():
            wait_all(ref.at[pl.ds(0, count - 1)], ssem.at[u, stage])

        @pl.when(jnp.logical_not(less))
        def _():
            wait_all(ref.at[pl.ds(0, count)], ssem.at[u, stage])

    for u in range(2):
        a = yl if u == 0 else g // 4
        wait_all(s1.at[u, pl.ds(0, NZ - 1)], ssem.at[u, F1])
        wait_sent(u, F2 + EARLY, r2.at[u, EARLY], 2 * NG, a == core)
        wait_sent(u, F2 + LATE, s2.at[u, LATE], NG, a == yl)
        wait_all(r2.at[u, LATE, pl.ds(0, NG)], ssem.at[u, MATE])
        wait_sent(u, B1, s3.at[u], 8, g // 4 == core if u == 0 else (core == yl) & (g // 4 == yl))
        wait_all(s4.at[u, pl.ds(0, NZ - 1)], ssem.at[u, B2])


def body(pair, pair_mask, w_ab, w_gate, w_out):
    return pl.pallas_call(
        kernel,
        out_shape=pltpu.VMEM(pair.shape, pair.dtype),
        in_specs=[pl.BlockSpec(memory_space=pltpu.HBM)] * 5,
        out_specs=pl.BlockSpec(memory_space=pltpu.VMEM),
        scratch_shapes=[
            pltpu.VMEM((ROWS, COLS, CH), BF16),
            pltpu.VMEM((ROWS, COLS), jnp.int32),
            pltpu.VMEM((2, CH, 4 * CH), BF16),
            pltpu.VMEM((2, CH, CH), BF16),
            pltpu.VMEM((2, CH, CH), BF16),
            pltpu.VMEM((2, 4 * CH, CH), BF16),
            pltpu.VMEM((2, CH, CH), BF16),
            pltpu.VMEM((2, CH, CH), BF16),
            pltpu.VMEM((256, 256), BF16),
            pltpu.VMEM((224, 256), BF16),
            pltpu.VMEM((TOK, CH), F32),
            pltpu.VMEM((CH, TOK), F32),
            pltpu.VMEM((CH, TOK), BF16),
            pltpu.VMEM((CH, TOK), F32),
            pltpu.VMEM((2, NZ, 16, HALF), F32),
            pltpu.VMEM((2, NZ, 32, HALF), BF16),
            pltpu.VMEM((2, NZ, 32, HALF), BF16),
            pltpu.VMEM((2, 2, NG, NZ, TOK), BF16),
            pltpu.VMEM((2, 2, 16, NZ, TOK), BF16),
            pltpu.VMEM((2, 224, 512), BF16),
            pltpu.VMEM((2, 448, 256), BF16),
            pltpu.VMEM((512, 256), BF16),
            pltpu.VMEM((224, 448), BF16),
            pltpu.VMEM((2, 8, NZ, TOK), BF16),
            pltpu.VMEM((2, 8, NZ, TOK), BF16),
            pltpu.VMEM((2, NZ, 32, 128), BF16),
            pltpu.VMEM((2, NZ, 32, 128), BF16),
            pltpu.SemaphoreType.DMA((5,)),
            pltpu.SemaphoreType.DMA((2, STAGES)),
            pltpu.SemaphoreType.DMA((2, STAGES)),
        ],
        compiler_params=pltpu.CompilerParams(
            collective_id=0, has_side_effects=True, vmem_limit_bytes=32 * 1024 * 1024
        ),
        name="triangle",
    )(*(pltpu.with_memory_space_constraint(x, pltpu.HBM) for x in (pair, pair_mask, w_ab, w_gate, w_out)))


def solution(mesh):
    return jax.shard_map(
        body,
        mesh=mesh,
        in_specs=(P("row", "grp", None), P("row", "grp"), P(), P(), P()),
        out_specs=P("row", "grp", None),
        check_vma=False,
    )
```

```python
import jax
import jax.numpy as jnp
from jax import lax
from jax.experimental import pallas as pl
from jax.experimental.pallas import tpu as pltpu
from jax.sharding import PartitionSpec as P

MESH = pl.DeviceIdType.MESH
F32, BF16 = jnp.float32, jnp.bfloat16
NZ, NG, ROWS, COLS, RS, MS, CH = 16, 8, 7, 56, 8, 64, 128
TOK = RS * MS
HALF = TOK // 2
AROUND = (8, 7, 9, 6, 10, 5, 11, 4, 12, 3, 13, 2, 14, 1, 15)
FAR = (6, 5, 7, 2, 4, 1, 3, 0)
EARLY, LATE = 0, 1
F1, F2, B1, B2, STAGES = 0, 2, 4, 6, 8


def mm(a, b, ca=1, cb=0):
    return lax.dot_general(a, b, (((ca,), (cb,)), ((), ())), preferred_element_type=F32)


def iota2(shape):
    return lax.broadcasted_iota(jnp.int32, shape, 0), lax.broadcasted_iota(jnp.int32, shape, 1)


def one_hot(hit):
    return jnp.where(hit, 1.0, 0.0).astype(BF16)


def normalize(x, axes):
    count = 1
    for a in axes:
        count *= x.shape[a]
    mean = jnp.sum(x, axis=axes, keepdims=True) * (1.0 / count)
    cen = x - mean
    var = jnp.sum(cen * cen, axis=axes, keepdims=True) * (1.0 / count)
    return cen * lax.rsqrt(var + 1e-05)


def sigmoid(x):
    return 0.5 * jnp.tanh(0.5 * x) + 0.5


def kernel(
    pair_hbm, mask_hbm, wab_hbm, wg_hbm, wo_hbm, out_ref,
    pair_ref, mask_ref, wab_ref, wg_ref, wo_ref, wabt, wgt, wot, perm, cols,
    ztok, zt, zn, gate, s1, r1, s2, r2, y0, y1, e0, e1, s3, r3, s4, r4, insem, ssem, rsem,
):
    loads = [
        pltpu.make_async_copy(src, dst, insem.at[n])
        for n, (src, dst) in enumerate(
            (
                (pair_hbm, pair_ref), (wab_hbm.at[0], wab_ref.at[0]), (mask_hbm, mask_ref), (wab_hbm.at[1], wab_ref.at[1]),
                (wg_hbm, wg_ref), (wo_hbm, wo_ref),
            )
        )
    ]
    for load in loads:
        load.start()

    row, g = lax.axis_index("row"), lax.axis_index("grp")
    core = lax.rem(row, 2)
    z = lax.rem(row // 2, NZ)
    yl = row // (2 * NZ)

    mate = 1 - core
    odd = lax.rem(g, 2)

    def dev(yl_, z_, core_, g_):
        return (yl_ * (2 * NZ) + z_ * 2 + core_, g_)

    barrier = pltpu.get_barrier_semaphore()

    def greet(device):
        pl.semaphore_signal(barrier, inc=1, device_id=device, device_id_type=MESH)

    for d in AROUND:
        greet(dev(yl, lax.rem(z + d, NZ), core, g))
    for d in FAR:
        for yl_to in (yl, 1 - yl):
            for core_to in (core, mate):
                if d or yl_to is not yl or core_to is not core:
                    greet(dev(yl_to, z, core_to, lax.rem(g + d, NG)))

    def send(src, dst, u, stage, device, is_self=None):
        def remote():
            pltpu.make_async_remote_copy(
                src_ref=src, dst_ref=dst, send_sem=ssem.at[u, stage], recv_sem=rsem.at[u, stage],
                device_id=device, device_id_type=MESH,
            ).start()

        if is_self is None:
            remote()
            return

        @pl.when(is_self)
        def _():
            pltpu.make_async_copy(src, dst, rsem.at[u, stage]).start()

        pl.when(jnp.logical_not(is_self))(remote)

    def send_z(src, dst, u, stage):
        for d in AROUND:
            to = lax.rem(z + d, NZ)
            send(src.at[to], dst.at[z], u, stage, dev(yl, to, core, g))
        pltpu.make_async_copy(src.at[z], dst.at[z], rsem.at[u, stage]).start()

    def wait_all(ref, sem):
        pltpu.make_async_copy(ref, ref, sem).wait()

    def slot_rows(r):
        return pl.ds(pl.multiple_of((r + odd * (1 - 2 * (r % 2))) * MS, MS), COLS)

    low = lax.broadcasted_iota(jnp.int32, (NZ, 128), 1) < 64
    ztok[...] = jnp.zeros_like(ztok)

    k, l = iota2((COLS, TOK))
    places = one_hot(lax.rem(l, MS) == k)
    k, l = iota2((ROWS, TOK))
    loads[2].wait()
    spread = mm(mask_ref[...].astype(F32).astype(BF16), places)
    keep = jnp.sum(jnp.where(l // MS == k + odd * (1 - 2 * lax.rem(k, 2)), spread, 0.0), axis=0, keepdims=True)

    loads[1].wait()
    wabt[0] = wab_ref[0].T
    loads[0].wait()
    for r in range(ROWS):
        ztok[slot_rows(r), :] = pair_ref[r].astype(F32)
    zt[...] = ztok[...].T

    def lanes(h):
        return slice(HALF * h, HALF * h + HALF)

    def norm(h):
        zn[:, lanes(h)] = normalize(zt[:, lanes(h)], (0,)).astype(BF16)

    def push(u, h):
        def side(base):
            p = mm(wabt[u, base : base + 2 * CH, :], zn[:, lanes(h)])
            return (sigmoid(p[:CH]) * p[CH:] * keep[:, lanes(h)]).reshape(NZ, NG, HALF)

        left, right = side(0), side(2 * CH)
        s1[u, h] = jnp.concatenate([right, left] if u == 0 else [left, right], axis=1).astype(BF16)
        send_z(s1.at[u, h], r1.at[u, h], u, F1 + h)

    def constants():
        for load in loads[3:]:
            load.wait()
        wgt[0], wgt[1] = wg_ref[0].T, wg_ref[1].T
        wot[0], wot[1] = wo_ref[0].T, wo_ref[1].T
        wabt[1] = wab_ref[1].T
        o, i = iota2((256, 256))
        perm[...] = one_hot(i == lax.rem(o, 16) * 16 + o // 16)
        i, l = iota2((224, 256))
        zi, n = lax.rem(i, NZ), i // NZ
        ci = jnp.where(n < 8, n // 4, (n - 8) // 3)
        ri = jnp.where(n < 8, lax.rem(n, 4), 4 + lax.rem(n - 8, 3))
        cols[...] = one_hot(l == zi // 4 * MS + lax.rem(zi, 4) * 14 + ci * 7 + ri)

    def channels_apart(u, h):
        x = mm(perm[...], r1[u, h].reshape(256, HALF)).astype(BF16)
        for e in (EARLY, LATE):
            s2[u, e, :, :, lanes(h)] = x[128 * e : 128 * e + 128].reshape(NG, NZ, HALF)

    def send_early(u, a, slot):
        for d in FAR:
            h = lax.rem(g + d, NG)
            for yl_to in (yl, 1 - yl):
                send(
                    s2.at[u, EARLY, h], r2.at[u, EARLY, slot], u, F2 + EARLY, dev(yl_to, z, a, h),
                    a == core if d == 0 and yl_to is yl else None,
                )

    def send_late(u, a, slot):
        for d in FAR:
            h = lax.rem(g + d, NG)
            for core_to in (core, mate):
                send(
                    s2.at[u, LATE, h], r2.at[u, LATE, slot], u, F2 + LATE, dev(a, z, core_to, h),
                    a == yl if d == 0 and core_to is core else None,
                )

    def assemble(u, e, cs):
        n_src, n_g = (1, 8) if u == 0 else (2, 4)
        for s in range(n_src):
            for q in range(n_g // 2):
                for t in range(4):
                    at = slice(128 * t, 128 * t + 128)
                    slot = cs * NG + s * n_g + 2 * q
                    even, other = r2[u, e, slot, :, at], r2[u, e, slot + 1, :, at]
                    lo = jnp.where(low, even, other)
                    hi = pltpu.roll(jnp.where(low, other, even), 64, 1) if t < 3 else None
                    to_lanes = slice(128 * q, 128 * q + 128)
                    for r, x in ((2 * t, lo), (2 * t + 1, hi)):
                        if r == ROWS:
                            continue
                        if u == 1:
                            block = (cs * 2 + s) * ROWS + r
                        elif r < 4:
                            block = cs * 4 + r
                        else:
                            block = 8 + cs * 3 + r - 4
                        to_rows = slice(block * NZ, block * NZ + NZ)
                        if u == 0:
                            y0[e, to_rows, to_lanes] = x
                        else:
                            y1[e, to_rows, to_lanes] = x

    def finish(u, h):
        x = r4[u, h].astype(F32).reshape(NZ, 2, NG, 128)
        tn = jnp.concatenate([normalize(x[:, t], (0, 1)).reshape(CH, 128) for t in range(2)], axis=1).astype(BF16)
        out = mm(wot[u], tn)
        zt[:, lanes(h)] = (zt[:, lanes(h)] + gate[:, lanes(h)] * out).astype(BF16).astype(F32)

    for u in range(2):
        a = yl if u == 0 else g // 4
        slot = core * NG + g if u == 0 else (core * 2 + yl) * 4 + lax.rem(g, 4)
        if u == 0:
            norm(0)
            pl.semaphore_wait(barrier, NZ - 1 + 4 * NG - 1)
            push(u, 0)
            norm(1)
            push(u, 1)
            constants()
        gate[...] = sigmoid(mm(wgt[u], zn[...]))

        for h in range(2):
            wait_all(r1.at[u, h], rsem.at[u, F1 + h])
            channels_apart(u, h)
        send_early(u, a, slot)
        send_late(u, a, slot)

        wait_all(r2.at[u, EARLY], rsem.at[u, F2 + EARLY])
        assemble(u, EARLY, 0)
        assemble(u, EARLY, 1)
        if u == 0:
            e0[...] = mm(y0[EARLY], cols[...], 0, 0).astype(BF16)
        else:
            e1[...] = mm(cols[...], y1[EARLY], 1, 1).astype(BF16)

        wait_all(r2.at[u, LATE], rsem.at[u, F2 + LATE])
        assemble(u, LATE, 0)
        assemble(u, LATE, 1)

        i_half, j_half = (yl, core) if u == 0 else (core, yl)
        for h in range(2):
            n_r = 4 - h
            rows = slice(128 * h, 128 * h + 32 * n_r)
            if u == 0:
                tri = mm(y0[LATE, rows, :], e0[...]).astype(BF16)
            else:
                tri = mm(e1[rows, :], y1[LATE]).astype(BF16)
            for ci in range(2):
                for t in range(2):
                    for q in range(2):
                        at = slice(128 * q, 128 * q + 128)
                        base = (ci * n_r + 2 * t) * NZ
                        c0 = tri[base : base + NZ, at]
                        c1 = tri[base + NZ : base + 2 * NZ, at] if 2 * t + 1 < n_r else jnp.zeros_like(c0)
                        c1 = pltpu.roll(c1, 64, 1)
                        s3[u, h, ci * 4 + 2 * q, :, 128 * t : 128 * t + 128] = jnp.where(low, c0, c1)
                        s3[u, h, ci * 4 + 2 * q + 1, :, 128 * t : 128 * t + 128] = jnp.where(low, c1, c0)

            for d in (2, 1, 3, 0):
                q = lax.rem(g + d, 4)
                to = 4 * j_half + q
                for ci in (mate, core):
                    send(
                        s3.at[u, h, ci * 4 + q], r3.at[u, h, g], u, B1 + h, dev(i_half, z, ci, to),
                        (i_half == yl) & (to == g) if d == 0 and ci is core else None,
                    )

        for h in range(2):
            wait_all(r3.at[u, h], rsem.at[u, B1 + h])
            x = r3[u, h].reshape(NG * NZ, HALF)
            x = jnp.concatenate([x[:, :128], x[:, 128:]], axis=0)
            s4[u, h] = mm(perm[...], x).astype(BF16).reshape(NZ, 16, 128)
            send_z(s4.at[u, h], r4.at[u, h], u, B2 + h)
        for h in range(2):
            wait_all(r4.at[u, h], rsem.at[u, B2 + h])
            finish(u, h)
            if u == 0:
                norm(h)
                push(1, h)

    ztok[...] = zt[...].T
    for r in range(ROWS):
        out_ref[r] = ztok[slot_rows(r), :].astype(BF16)

    def wait_sent(u, stage, ref, count, less):
        @pl.when(less)
        def _():
            wait_all(ref.at[pl.ds(0, count - 1)], ssem.at[u, stage])

        @pl.when(jnp.logical_not(less))
        def _():
            wait_all(ref.at[pl.ds(0, count)], ssem.at[u, stage])

    for u in range(2):
        a = yl if u == 0 else g // 4
        for h in range(2):
            wait_all(s1.at[u, h, pl.ds(0, NZ - 1)], ssem.at[u, F1 + h])
        wait_sent(u, F2 + EARLY, r2.at[u, EARLY], 2 * NG, a == core)
        wait_sent(u, F2 + LATE, r2.at[u, LATE], 2 * NG, a == yl)
        for h in range(2):
            wait_sent(u, B1 + h, s3.at[u, h], 8, g // 4 == core if u == 0 else (core == yl) & (g // 4 == yl))
            wait_all(s4.at[u, h, pl.ds(0, NZ - 1)], ssem.at[u, B2 + h])


def body(pair, pair_mask, w_ab, w_gate, w_out):
    return pl.pallas_call(
        kernel,
        out_shape=pltpu.VMEM(pair.shape, pair.dtype),
        in_specs=[pl.BlockSpec(memory_space=pltpu.HBM)] * 5,
        out_specs=pl.BlockSpec(memory_space=pltpu.VMEM),
        scratch_shapes=[
            pltpu.VMEM((ROWS, COLS, CH), BF16),
            pltpu.VMEM((ROWS, COLS), jnp.int32),
            pltpu.VMEM((2, CH, 4 * CH), BF16),
            pltpu.VMEM((2, CH, CH), BF16),
            pltpu.VMEM((2, CH, CH), BF16),
            pltpu.VMEM((2, 4 * CH, CH), BF16),
            pltpu.VMEM((2, CH, CH), BF16),
            pltpu.VMEM((2, CH, CH), BF16),
            pltpu.VMEM((256, 256), BF16),
            pltpu.VMEM((224, 256), BF16),
            pltpu.VMEM((TOK, CH), F32),
            pltpu.VMEM((CH, TOK), F32),
            pltpu.VMEM((CH, TOK), BF16),
            pltpu.VMEM((CH, TOK), F32),
            pltpu.VMEM((2, 2, NZ, 16, HALF), BF16),
            pltpu.VMEM((2, 2, NZ, 16, HALF), BF16),
            pltpu.VMEM((2, 2, NG, NZ, TOK), BF16),
            pltpu.VMEM((2, 2, 16, NZ, TOK), BF16),
            pltpu.VMEM((2, 224, 512), BF16),
            pltpu.VMEM((2, 448, 256), BF16),
            pltpu.VMEM((512, 256), BF16),
            pltpu.VMEM((224, 448), BF16),
            pltpu.VMEM((2, 2, 8, NZ, HALF), BF16),
            pltpu.VMEM((2, 2, 8, NZ, HALF), BF16),
            pltpu.VMEM((2, 2, NZ, 16, 128), BF16),
            pltpu.VMEM((2, 2, NZ, 16, 128), BF16),
            pltpu.SemaphoreType.DMA((6,)),
            pltpu.SemaphoreType.DMA((2, STAGES)),
            pltpu.SemaphoreType.DMA((2, STAGES)),
        ],
        compiler_params=pltpu.CompilerParams(
            collective_id=0, has_side_effects=True, vmem_limit_bytes=32 * 1024 * 1024
        ),
        name="triangle",
    )(*(pltpu.with_memory_space_constraint(x, pltpu.HBM) for x in (pair, pair_mask, w_ab, w_gate, w_out)))


def solution(mesh):
    return jax.shard_map(
        body,
        mesh=mesh,
        in_specs=(P("row", "grp", None), P("row", "grp"), P(), P(), P()),
        out_specs=P("row", "grp", None),
        check_vma=False,
    )
```

```python
import jax
import jax.numpy as jnp
from jax import lax
from jax.experimental import pallas as pl
from jax.experimental.pallas import tpu as pltpu
from jax.sharding import PartitionSpec as P

MESH = pl.DeviceIdType.MESH
F32, BF16 = jnp.float32, jnp.bfloat16
NZ, NG, ROWS, COLS, RS, MS, CH = 16, 8, 7, 56, 8, 64, 128
TOK = RS * MS
HALF = TOK // 2
AROUND = (8, 7, 9, 6, 10, 5, 11, 4, 12, 3, 13, 2, 14, 1, 15)
FAR = (6, 5, 7, 2, 4, 1, 3, 0)
EARLY, LATE = 0, 1
F1, F2, B1, B2, STAGES = 0, 2, 6, 8, 10


def mm(a, b, ca=1, cb=0):
    return lax.dot_general(a, b, (((ca,), (cb,)), ((), ())), preferred_element_type=F32)


def iota2(shape):
    return lax.broadcasted_iota(jnp.int32, shape, 0), lax.broadcasted_iota(jnp.int32, shape, 1)


def one_hot(hit):
    return jnp.where(hit, 1.0, 0.0).astype(BF16)


def normalize(x, axes):
    count = 1
    for a in axes:
        count *= x.shape[a]
    mean = jnp.sum(x, axis=axes, keepdims=True) * (1.0 / count)
    cen = x - mean
    var = jnp.sum(cen * cen, axis=axes, keepdims=True) * (1.0 / count)
    return cen * lax.rsqrt(var + 1e-05)


def sigmoid(x):
    return 0.5 * jnp.tanh(0.5 * x) + 0.5


def kernel(
    pair_hbm, mask_hbm, wab_hbm, wg_hbm, wo_hbm, out_ref,
    pair_ref, mask_ref, wab_ref, wg_ref, wo_ref, wabt, wgt, wot, perm, cols,
    ztok, zt, zn, gate, s1, r1, s2, r2, y0, y1, e0, e1, s3, r3, s4, r4, insem, ssem, rsem,
):
    loads = [
        pltpu.make_async_copy(src, dst, insem.at[n])
        for n, (src, dst) in enumerate(
            (
                (pair_hbm, pair_ref), (wab_hbm.at[0], wab_ref.at[0]), (mask_hbm, mask_ref), (wab_hbm.at[1], wab_ref.at[1]),
                (wg_hbm, wg_ref), (wo_hbm, wo_ref),
            )
        )
    ]
    for load in loads:
        load.start()

    row, g = lax.axis_index("row"), lax.axis_index("grp")
    core = lax.rem(row, 2)
    z = lax.rem(row // 2, NZ)
    yl = row // (2 * NZ)

    mate = 1 - core
    odd = lax.rem(g, 2)

    def dev(yl_, z_, core_, g_):
        return (yl_ * (2 * NZ) + z_ * 2 + core_, g_)

    barrier = pltpu.get_barrier_semaphore()

    def greet(device):
        pl.semaphore_signal(barrier, inc=1, device_id=device, device_id_type=MESH)

    for d in AROUND:
        greet(dev(yl, lax.rem(z + d, NZ), core, g))
    for d in FAR:
        for yl_to in (yl, 1 - yl):
            for core_to in (core, mate):
                if d or yl_to is not yl or core_to is not core:
                    greet(dev(yl_to, z, core_to, lax.rem(g + d, NG)))

    def send(src, dst, u, stage, device, is_self=None):
        def remote():
            pltpu.make_async_remote_copy(
                src_ref=src, dst_ref=dst, send_sem=ssem.at[u, stage], recv_sem=rsem.at[u, stage],
                device_id=device, device_id_type=MESH,
            ).start()

        if is_self is None:
            remote()
            return

        @pl.when(is_self)
        def _():
            pltpu.make_async_copy(src, dst, rsem.at[u, stage]).start()

        pl.when(jnp.logical_not(is_self))(remote)

    def send_z(src, dst, u, stage):
        for d in AROUND:
            to = lax.rem(z + d, NZ)
            send(src.at[to], dst.at[z], u, stage, dev(yl, to, core, g))
        pltpu.make_async_copy(src.at[z], dst.at[z], rsem.at[u, stage]).start()

    def wait_all(ref, sem):
        pltpu.make_async_copy(ref, ref, sem).wait()

    def slot_rows(r):
        return pl.ds(pl.multiple_of((r + odd * (1 - 2 * (r % 2))) * MS, MS), COLS)

    low = lax.broadcasted_iota(jnp.int32, (NZ, 128), 1) < 64
    ztok[...] = jnp.zeros_like(ztok)

    k, l = iota2((COLS, TOK))
    places = one_hot(lax.rem(l, MS) == k)
    k, l = iota2((ROWS, TOK))
    loads[2].wait()
    spread = mm(mask_ref[...].astype(F32).astype(BF16), places)
    keep = jnp.sum(jnp.where(l // MS == k + odd * (1 - 2 * lax.rem(k, 2)), spread, 0.0), axis=0, keepdims=True)

    loads[1].wait()
    wabt[0] = wab_ref[0].T
    loads[0].wait()
    for r in range(ROWS):
        ztok[slot_rows(r), :] = pair_ref[r].astype(F32)
    zt[...] = ztok[...].T

    def lanes(h):
        return slice(HALF * h, HALF * h + HALF)

    def norm(h):
        zn[:, lanes(h)] = normalize(zt[:, lanes(h)], (0,)).astype(BF16)

    def push(u, h):
        def side(base):
            p = mm(wabt[u, base : base + 2 * CH, :], zn[:, lanes(h)])
            return (sigmoid(p[:CH]) * p[CH:] * keep[:, lanes(h)]).reshape(NZ, NG, HALF)

        left, right = side(0), side(2 * CH)
        s1[u, h] = jnp.concatenate([right, left] if u == 0 else [left, right], axis=1).astype(BF16)
        send_z(s1.at[u, h], r1.at[u, h], u, F1 + h)

    def constants():
        for load in loads[3:]:
            load.wait()
        wgt[0], wgt[1] = wg_ref[0].T, wg_ref[1].T
        wot[0], wot[1] = wo_ref[0].T, wo_ref[1].T
        wabt[1] = wab_ref[1].T
        o, i = iota2((256, 256))
        perm[...] = one_hot(i == lax.rem(o, 16) * 16 + o // 16)
        i, l = iota2((224, 256))
        zi, n = lax.rem(i, NZ), i // NZ
        ci = jnp.where(n < 8, n // 4, (n - 8) // 3)
        ri = jnp.where(n < 8, lax.rem(n, 4), 4 + lax.rem(n - 8, 3))
        cols[...] = one_hot(l == zi // 4 * MS + lax.rem(zi, 4) * 14 + ci * 7 + ri)

    def channels_apart(u, h):
        x = mm(perm[...], r1[u, h].reshape(256, HALF)).astype(BF16)
        for e in (EARLY, LATE):
            s2[u, e, h] = x[128 * e : 128 * e + 128].reshape(NG, NZ, HALF)

    def send_early(u, t, a, slot):
        for d in FAR:
            h = lax.rem(g + d, NG)
            for yl_to in (yl, 1 - yl):
                send(
                    s2.at[u, EARLY, t, h], r2.at[u, EARLY, t, slot], u, F2 + t, dev(yl_to, z, a, h),
                    a == core if d == 0 and yl_to is yl else None,
                )

    def send_late(u, t, a, slot):
        for d in FAR:
            h = lax.rem(g + d, NG)
            for core_to in (core, mate):
                send(
                    s2.at[u, LATE, t, h], r2.at[u, LATE, t, slot], u, F2 + 2 + t, dev(a, z, core_to, h),
                    a == yl if d == 0 and core_to is core else None,
                )

    def assemble(u, e, h):
        n_src, n_g = (2, 8) if u == 0 else (4, 4)
        to = y0 if u == 0 else y1
        for s in range(n_src):
            for q in range(n_g // 2):
                for t in range(2):
                    at = slice(128 * t, 128 * t + 128)
                    even, other = r2[u, e, h, s * n_g + 2 * q, :, at], r2[u, e, h, s * n_g + 2 * q + 1, :, at]
                    r = 4 * h + 2 * t
                    if u == 1:
                        row = (s * ROWS + r) * NZ
                    else:
                        row = (s * 4 + r if h == 0 else 8 + s * 3 + r - 4) * NZ
                    to_lanes = slice(128 * q, 128 * q + 128)
                    to[e, row : row + NZ, to_lanes] = jnp.where(low, even, other)
                    if r + 1 < ROWS:
                        to[e, row + NZ : row + 2 * NZ, to_lanes] = pltpu.roll(jnp.where(low, other, even), 64, 1)

    def finish(u, h):
        x = r4[u, h].astype(F32).reshape(NZ, 2, NG, 128)
        tn = jnp.concatenate([normalize(x[:, t], (0, 1)).reshape(CH, 128) for t in range(2)], axis=1).astype(BF16)
        out = mm(wot[u], tn)
        zt[:, lanes(h)] = (zt[:, lanes(h)] + gate[:, lanes(h)] * out).astype(BF16).astype(F32)

    for u in range(2):
        a = yl if u == 0 else g // 4
        slot = core * NG + g if u == 0 else (core * 2 + yl) * 4 + lax.rem(g, 4)
        if u == 0:
            norm(0)
            pl.semaphore_wait(barrier, NZ - 1 + 4 * NG - 1)
            push(u, 0)
            norm(1)
            constants()
        gate[...] = sigmoid(mm(wgt[u], zn[...]))
        if u == 0:
            push(u, 1)

        for h in range(2):
            wait_all(r1.at[u, h], rsem.at[u, F1 + h])
            channels_apart(u, h)
            send_early(u, h, a, slot)
            send_late(u, h, a, slot)

        for e in (EARLY, LATE):
            wait_all(r2.at[u, e, 0], rsem.at[u, F2 + 2 * e])
            assemble(u, e, 0)
        wait_all(r2.at[u, EARLY, 1], rsem.at[u, F2 + 1])
        assemble(u, EARLY, 1)
        if u == 0:
            e0[...] = mm(y0[EARLY], cols[...], 0, 0).astype(BF16)
        else:
            e1[...] = mm(cols[...], y1[EARLY], 1, 1).astype(BF16)

        wait_all(r2.at[u, LATE, 1], rsem.at[u, F2 + 3])
        assemble(u, LATE, 1)

        i_half, j_half = (yl, core) if u == 0 else (core, yl)
        for h in range(2):
            n_r = 4 - h
            rows = slice(128 * h, 128 * h + 32 * n_r)
            if u == 0:
                tri = mm(y0[LATE, rows, :], e0[...]).astype(BF16)
            else:
                tri = mm(e1[rows, :], y1[LATE]).astype(BF16)
            for ci in range(2):
                for t in range(2):
                    for q in range(2):
                        at = slice(128 * q, 128 * q + 128)
                        base = (ci * n_r + 2 * t) * NZ
                        c0 = tri[base : base + NZ, at]
                        c1 = tri[base + NZ : base + 2 * NZ, at] if 2 * t + 1 < n_r else jnp.zeros_like(c0)
                        c1 = pltpu.roll(c1, 64, 1)
                        s3[u, h, ci * 4 + 2 * q, :, 128 * t : 128 * t + 128] = jnp.where(low, c0, c1)
                        s3[u, h, ci * 4 + 2 * q + 1, :, 128 * t : 128 * t + 128] = jnp.where(low, c1, c0)

            for d in (2, 1, 3, 0):
                q = lax.rem(g + d, 4)
                to = 4 * j_half + q
                for ci in (mate, core):
                    send(
                        s3.at[u, h, ci * 4 + q], r3.at[u, h, g], u, B1 + h, dev(i_half, z, ci, to),
                        (i_half == yl) & (to == g) if d == 0 and ci is core else None,
                    )

        for h in range(2):
            wait_all(r3.at[u, h], rsem.at[u, B1 + h])
            x = r3[u, h].reshape(NG * NZ, HALF)
            x = jnp.concatenate([x[:, :128], x[:, 128:]], axis=0)
            s4[u, h] = mm(perm[...], x).astype(BF16).reshape(NZ, 16, 128)
            send_z(s4.at[u, h], r4.at[u, h], u, B2 + h)
        for h in range(2):
            wait_all(r4.at[u, h], rsem.at[u, B2 + h])
            finish(u, h)
            if u == 0:
                norm(h)
                push(1, h)

    ztok[...] = zt[...].T
    for r in range(ROWS):
        out_ref[r] = ztok[slot_rows(r), :].astype(BF16)

    def wait_sent(u, stage, ref, count, less):
        @pl.when(less)
        def _():
            wait_all(ref.at[pl.ds(0, count - 1)], ssem.at[u, stage])

        @pl.when(jnp.logical_not(less))
        def _():
            wait_all(ref.at[pl.ds(0, count)], ssem.at[u, stage])

    for u in range(2):
        a = yl if u == 0 else g // 4
        for h in range(2):
            wait_all(s1.at[u, h, pl.ds(0, NZ - 1)], ssem.at[u, F1 + h])
        for h in range(2):
            wait_sent(u, F2 + h, r2.at[u, EARLY, h], 2 * NG, a == core)
            wait_sent(u, F2 + 2 + h, r2.at[u, LATE, h], 2 * NG, a == yl)
            wait_sent(u, B1 + h, s3.at[u, h], 8, g // 4 == core if u == 0 else (core == yl) & (g // 4 == yl))
            wait_all(s4.at[u, h, pl.ds(0, NZ - 1)], ssem.at[u, B2 + h])


def body(pair, pair_mask, w_ab, w_gate, w_out):
    return pl.pallas_call(
        kernel,
        out_shape=pltpu.VMEM(pair.shape, pair.dtype),
        in_specs=[pl.BlockSpec(memory_space=pltpu.HBM)] * 5,
        out_specs=pl.BlockSpec(memory_space=pltpu.VMEM),
        scratch_shapes=[
            pltpu.VMEM((ROWS, COLS, CH), BF16),
            pltpu.VMEM((ROWS, COLS), jnp.int32),
            pltpu.VMEM((2, CH, 4 * CH), BF16),
            pltpu.VMEM((2, CH, CH), BF16),
            pltpu.VMEM((2, CH, CH), BF16),
            pltpu.VMEM((2, 4 * CH, CH), BF16),
            pltpu.VMEM((2, CH, CH), BF16),
            pltpu.VMEM((2, CH, CH), BF16),
            pltpu.VMEM((256, 256), BF16),
            pltpu.VMEM((224, 256), BF16),
            pltpu.VMEM((TOK, CH), F32),
            pltpu.VMEM((CH, TOK), F32),
            pltpu.VMEM((CH, TOK), BF16),
            pltpu.VMEM((CH, TOK), F32),
            pltpu.VMEM((2, 2, NZ, 16, HALF), BF16),
            pltpu.VMEM((2, 2, NZ, 16, HALF), BF16),
            pltpu.VMEM((2, 2, 2, NG, NZ, HALF), BF16),
            pltpu.VMEM((2, 2, 2, 16, NZ, HALF), BF16),
            pltpu.VMEM((2, 224, 512), BF16),
            pltpu.VMEM((2, 448, 256), BF16),
            pltpu.VMEM((512, 256), BF16),
            pltpu.VMEM((224, 448), BF16),
            pltpu.VMEM((2, 2, 8, NZ, HALF), BF16),
            pltpu.VMEM((2, 2, 8, NZ, HALF), BF16),
            pltpu.VMEM((2, 2, NZ, 16, 128), BF16),
            pltpu.VMEM((2, 2, NZ, 16, 128), BF16),
            pltpu.SemaphoreType.DMA((6,)),
            pltpu.SemaphoreType.DMA((2, STAGES)),
            pltpu.SemaphoreType.DMA((2, STAGES)),
        ],
        compiler_params=pltpu.CompilerParams(
            collective_id=0, has_side_effects=True, vmem_limit_bytes=32 * 1024 * 1024
        ),
        name="triangle",
    )(*(pltpu.with_memory_space_constraint(x, pltpu.HBM) for x in (pair, pair_mask, w_ab, w_gate, w_out)))


def solution(mesh):
    return jax.shard_map(
        body,
        mesh=mesh,
        in_specs=(P("row", "grp", None), P("row", "grp"), P(), P(), P()),
        out_specs=P("row", "grp", None),
        check_vma=False,
    )
```

```python
import jax
import jax.numpy as jnp
from jax import lax
from jax.experimental import pallas as pl
from jax.experimental.pallas import tpu as pltpu
from jax.sharding import PartitionSpec as P

MESH = pl.DeviceIdType.MESH
F32, BF16 = jnp.float32, jnp.bfloat16
NZ, NG, ROWS, COLS, RS, MS, CH = 16, 8, 7, 56, 8, 64, 128
TOK = RS * MS
HALF = TOK // 2
AROUND = (8, 7, 9, 6, 10, 5, 11, 4, 12, 3, 13, 2, 14, 1, 15)
FAR = (6, 5, 7, 2, 4, 1, 3, 0)
EARLY, LATE = 0, 1
PIECES = ((0, 2), (2, 1), (3, 1))
F1, F2, B1, B2, STAGES = 0, 3, 9, 11, 13


def mm(a, b, ca=1, cb=0):
    return lax.dot_general(a, b, (((ca,), (cb,)), ((), ())), preferred_element_type=F32)


def iota2(shape):
    return lax.broadcasted_iota(jnp.int32, shape, 0), lax.broadcasted_iota(jnp.int32, shape, 1)


def one_hot(hit):
    return jnp.where(hit, 1.0, 0.0).astype(BF16)


def normalize(x, axes):
    count = 1
    for a in axes:
        count *= x.shape[a]
    mean = jnp.sum(x, axis=axes, keepdims=True) * (1.0 / count)
    cen = x - mean
    var = jnp.sum(cen * cen, axis=axes, keepdims=True) * (1.0 / count)
    return cen * lax.rsqrt(var + 1e-05)


def sigmoid(x):
    return 0.5 * jnp.tanh(0.5 * x) + 0.5


def kernel(
    pair_hbm, mask_hbm, wab_hbm, wg_hbm, wo_hbm, out_ref,
    pair_ref, mask_ref, wab_ref, wg_ref, wo_ref, wabt, wgt, wot, perm, cols,
    ztok, zt, zn, gate, s1a, s1b, s1c, r1a, r1b, r1c, s2a, s2b, s2c, r2a, r2b, r2c, y0, y1, e0, e1, s3, r3, s4, r4, insem, ssem, rsem,
):
    loads = [
        pltpu.make_async_copy(src, dst, insem.at[n])
        for n, (src, dst) in enumerate(
            (
                (pair_hbm, pair_ref), (wab_hbm.at[0], wab_ref.at[0]), (mask_hbm, mask_ref), (wab_hbm.at[1], wab_ref.at[1]),
                (wg_hbm, wg_ref), (wo_hbm, wo_ref),
            )
        )
    ]
    for load in loads:
        load.start()

    row, g = lax.axis_index("row"), lax.axis_index("grp")
    core = lax.rem(row, 2)
    z = lax.rem(row // 2, NZ)
    yl = row // (2 * NZ)

    mate = 1 - core
    odd = lax.rem(g, 2)

    def dev(yl_, z_, core_, g_):
        return (yl_ * (2 * NZ) + z_ * 2 + core_, g_)

    barrier = pltpu.get_barrier_semaphore()

    s1, r1, s2, r2 = (s1a, s1b, s1c), (r1a, r1b, r1c), (s2a, s2b, s2c), (r2a, r2b, r2c)

    def greet(device):
        pl.semaphore_signal(barrier, inc=1, device_id=device, device_id_type=MESH)

    for d in AROUND:
        greet(dev(yl, lax.rem(z + d, NZ), core, g))
    for d in FAR:
        for yl_to in (yl, 1 - yl):
            for core_to in (core, mate):
                if d or yl_to is not yl or core_to is not core:
                    greet(dev(yl_to, z, core_to, lax.rem(g + d, NG)))

    def send(src, dst, u, stage, device, is_self=None):
        def remote():
            pltpu.make_async_remote_copy(
                src_ref=src, dst_ref=dst, send_sem=ssem.at[u, stage], recv_sem=rsem.at[u, stage],
                device_id=device, device_id_type=MESH,
            ).start()

        if is_self is None:
            remote()
            return

        @pl.when(is_self)
        def _():
            pltpu.make_async_copy(src, dst, rsem.at[u, stage]).start()

        pl.when(jnp.logical_not(is_self))(remote)

    def send_z(src, dst, u, stage):
        for d in AROUND:
            to = lax.rem(z + d, NZ)
            send(src.at[to], dst.at[z], u, stage, dev(yl, to, core, g))
        pltpu.make_async_copy(src.at[z], dst.at[z], rsem.at[u, stage]).start()

    def wait_all(ref, sem):
        pltpu.make_async_copy(ref, ref, sem).wait()

    def slot_rows(r):
        return pl.ds(pl.multiple_of((r + odd * (1 - 2 * (r % 2))) * MS, MS), COLS)

    low = lax.broadcasted_iota(jnp.int32, (NZ, 128), 1) < 64
    ztok[...] = jnp.zeros_like(ztok)

    k, l = iota2((COLS, TOK))
    places = one_hot(lax.rem(l, MS) == k)
    k, l = iota2((ROWS, TOK))
    loads[2].wait()
    spread = mm(mask_ref[...].astype(F32).astype(BF16), places)
    keep = jnp.sum(jnp.where(l // MS == k + odd * (1 - 2 * lax.rem(k, 2)), spread, 0.0), axis=0, keepdims=True)

    loads[1].wait()
    wabt[0] = wab_ref[0].T
    loads[0].wait()
    for r in range(ROWS):
        ztok[slot_rows(r), :] = pair_ref[r].astype(F32)
    zt[...] = ztok[...].T

    def lanes(h):
        return slice(HALF * h, HALF * h + HALF)

    def norm(h):
        zn[:, lanes(h)] = normalize(zt[:, lanes(h)], (0,)).astype(BF16)

    def push(u, h):
        def side(base):
            p = mm(wabt[u, base : base + 2 * CH, :], zn[:, lanes(h)])
            return (sigmoid(p[:CH]) * p[CH:] * keep[:, lanes(h)]).reshape(NZ, NG, HALF)

        left, right = side(0), side(2 * CH)
        x = jnp.concatenate([right, left] if u == 0 else [left, right], axis=1).astype(BF16)
        for p, (t, n) in enumerate(PIECES):
            if t // 2 == h:
                s1[p][u] = x[:, :, 128 * (t - 2 * h) : 128 * (t - 2 * h + n)]
                send_z(s1[p].at[u], r1[p].at[u], u, F1 + p)

    def constants():
        for load in loads[3:]:
            load.wait()
        wgt[0], wgt[1] = wg_ref[0].T, wg_ref[1].T
        wot[0], wot[1] = wo_ref[0].T, wo_ref[1].T
        wabt[1] = wab_ref[1].T
        o, i = iota2((256, 256))
        perm[...] = one_hot(i == lax.rem(o, 16) * 16 + o // 16)
        i, l = iota2((224, 256))
        zi, n = lax.rem(i, NZ), i // NZ
        ci = jnp.where(n < 8, n // 4, (n - 8) // 3)
        ri = jnp.where(n < 8, lax.rem(n, 4), 4 + lax.rem(n - 8, 3))
        cols[...] = one_hot(l == zi // 4 * MS + lax.rem(zi, 4) * 14 + ci * 7 + ri)

    def channels_apart(u, p):
        width = 128 * PIECES[p][1]
        x = mm(perm[...], r1[p][u].reshape(256, width)).astype(BF16)
        for e in (EARLY, LATE):
            s2[p][u, e] = x[128 * e : 128 * e + 128].reshape(NG, NZ, width)

    def send_early(u, p, a, slot):
        for d in FAR:
            h = lax.rem(g + d, NG)
            for yl_to in (yl, 1 - yl):
                send(
                    s2[p].at[u, EARLY, h], r2[p].at[u, EARLY, slot], u, F2 + p, dev(yl_to, z, a, h),
                    a == core if d == 0 and yl_to is yl else None,
                )

    def send_late(u, p, a, slot):
        for d in FAR:
            h = lax.rem(g + d, NG)
            for core_to in (core, mate):
                send(
                    s2[p].at[u, LATE, h], r2[p].at[u, LATE, slot], u, F2 + 3 + p, dev(a, z, core_to, h),
                    a == yl if d == 0 and core_to is core else None,
                )

    def assemble(u, e, p):
        n_src, n_g = (2, 8) if u == 0 else (4, 4)
        to = y0 if u == 0 else y1
        for s in range(n_src):
            for q in range(n_g // 2):
                for t in range(PIECES[p][1]):
                    at = slice(128 * t, 128 * t + 128)
                    even, other = r2[p][u, e, s * n_g + 2 * q, :, at], r2[p][u, e, s * n_g + 2 * q + 1, :, at]
                    r = 2 * (PIECES[p][0] + t)
                    if u == 1:
                        row = (s * ROWS + r) * NZ
                    else:
                        row = (s * 4 + r if r < 4 else 8 + s * 3 + r - 4) * NZ
                    to_lanes = slice(128 * q, 128 * q + 128)
                    to[e, row : row + NZ, to_lanes] = jnp.where(low, even, other)
                    if r + 1 < ROWS:
                        to[e, row + NZ : row + 2 * NZ, to_lanes] = pltpu.roll(jnp.where(low, other, even), 64, 1)

    def finish(u, h):
        x = r4[u, h].astype(F32).reshape(NZ, 2, NG, 128)
        tn = jnp.concatenate([normalize(x[:, t], (0, 1)).reshape(CH, 128) for t in range(2)], axis=1).astype(BF16)
        out = mm(wot[u], tn)
        zt[:, lanes(h)] = (zt[:, lanes(h)] + gate[:, lanes(h)] * out).astype(BF16).astype(F32)

    for u in range(2):
        a = yl if u == 0 else g // 4
        slot = core * NG + g if u == 0 else (core * 2 + yl) * 4 + lax.rem(g, 4)
        if u == 0:
            norm(0)
            pl.semaphore_wait(barrier, NZ - 1 + 4 * NG - 1)
            push(u, 0)
            norm(1)
            constants()
        gate[...] = sigmoid(mm(wgt[u], zn[...]))
        if u == 0:
            push(u, 1)

        for p in range(3):
            wait_all(r1[p].at[u], rsem.at[u, F1 + p])
            channels_apart(u, p)
            send_early(u, p, a, slot)
            send_late(u, p, a, slot)

        for p in range(2):
            for e in (EARLY, LATE):
                wait_all(r2[p].at[u, e], rsem.at[u, F2 + 3 * e + p])
                assemble(u, e, p)
        wait_all(r2[2].at[u, EARLY], rsem.at[u, F2 + 2])
        assemble(u, EARLY, 2)
        if u == 0:
            e0[...] = mm(y0[EARLY], cols[...], 0, 0).astype(BF16)
        else:
            e1[...] = mm(cols[...], y1[EARLY], 1, 1).astype(BF16)

        wait_all(r2[2].at[u, LATE], rsem.at[u, F2 + 5])
        assemble(u, LATE, 2)

        i_half, j_half = (yl, core) if u == 0 else (core, yl)
        for h in range(2):
            n_r = 4 - h
            rows = slice(128 * h, 128 * h + 32 * n_r)
            if u == 0:
                tri = mm(y0[LATE, rows, :], e0[...]).astype(BF16)
            else:
                tri = mm(e1[rows, :], y1[LATE]).astype(BF16)
            for ci in range(2):
                for t in range(2):
                    for q in range(2):
                        at = slice(128 * q, 128 * q + 128)
                        base = (ci * n_r + 2 * t) * NZ
                        c0 = tri[base : base + NZ, at]
                        c1 = tri[base + NZ : base + 2 * NZ, at] if 2 * t + 1 < n_r else jnp.zeros_like(c0)
                        c1 = pltpu.roll(c1, 64, 1)
                        s3[u, h, ci * 4 + 2 * q, :, 128 * t : 128 * t + 128] = jnp.where(low, c0, c1)
                        s3[u, h, ci * 4 + 2 * q + 1, :, 128 * t : 128 * t + 128] = jnp.where(low, c1, c0)

            for d in (2, 1, 3, 0):
                q = lax.rem(g + d, 4)
                to = 4 * j_half + q
                for ci in (mate, core):
                    send(
                        s3.at[u, h, ci * 4 + q], r3.at[u, h, g], u, B1 + h, dev(i_half, z, ci, to),
                        (i_half == yl) & (to == g) if d == 0 and ci is core else None,
                    )

        for h in range(2):
            wait_all(r3.at[u, h], rsem.at[u, B1 + h])
            x = r3[u, h].reshape(NG * NZ, HALF)
            x = jnp.concatenate([x[:, :128], x[:, 128:]], axis=0)
            s4[u, h] = mm(perm[...], x).astype(BF16).reshape(NZ, 16, 128)
            send_z(s4.at[u, h], r4.at[u, h], u, B2 + h)
        for h in range(2):
            wait_all(r4.at[u, h], rsem.at[u, B2 + h])
            finish(u, h)
            if u == 0:
                norm(h)
                push(1, h)
            else:
                ztok[lanes(h), :] = zt[:, lanes(h)].T
                for r in range(4 * h, min(4 * h + 4, ROWS)):
                    out_ref[r] = ztok[slot_rows(r), :].astype(BF16)

    def wait_sent(u, stage, ref, count, less):
        @pl.when(less)
        def _():
            wait_all(ref.at[pl.ds(0, count - 1)], ssem.at[u, stage])

        @pl.when(jnp.logical_not(less))
        def _():
            wait_all(ref.at[pl.ds(0, count)], ssem.at[u, stage])

    for u in range(2):
        a = yl if u == 0 else g // 4
        for p in range(3):
            wait_all(s1[p].at[u, pl.ds(0, NZ - 1)], ssem.at[u, F1 + p])
            wait_sent(u, F2 + p, r2[p].at[u, EARLY], 2 * NG, a == core)
            wait_sent(u, F2 + 3 + p, r2[p].at[u, LATE], 2 * NG, a == yl)
        for h in range(2):
            wait_sent(u, B1 + h, s3.at[u, h], 8, g // 4 == core if u == 0 else (core == yl) & (g // 4 == yl))
            wait_all(s4.at[u, h, pl.ds(0, NZ - 1)], ssem.at[u, B2 + h])


def body(pair, pair_mask, w_ab, w_gate, w_out):
    return pl.pallas_call(
        kernel,
        out_shape=pltpu.VMEM(pair.shape, pair.dtype),
        in_specs=[pl.BlockSpec(memory_space=pltpu.HBM)] * 5,
        out_specs=pl.BlockSpec(memory_space=pltpu.VMEM),
        scratch_shapes=[
            pltpu.VMEM((ROWS, COLS, CH), BF16),
            pltpu.VMEM((ROWS, COLS), jnp.int32),
            pltpu.VMEM((2, CH, 4 * CH), BF16),
            pltpu.VMEM((2, CH, CH), BF16),
            pltpu.VMEM((2, CH, CH), BF16),
            pltpu.VMEM((2, 4 * CH, CH), BF16),
            pltpu.VMEM((2, CH, CH), BF16),
            pltpu.VMEM((2, CH, CH), BF16),
            pltpu.VMEM((256, 256), BF16),
            pltpu.VMEM((224, 256), BF16),
            pltpu.VMEM((TOK, CH), F32),
            pltpu.VMEM((CH, TOK), F32),
            pltpu.VMEM((CH, TOK), BF16),
            pltpu.VMEM((CH, TOK), F32),
            *(pltpu.VMEM((2, NZ, 16, 128 * n), BF16) for _, n in PIECES),
            *(pltpu.VMEM((2, NZ, 16, 128 * n), BF16) for _, n in PIECES),
            *(pltpu.VMEM((2, 2, NG, NZ, 128 * n), BF16) for _, n in PIECES),
            *(pltpu.VMEM((2, 2, 16, NZ, 128 * n), BF16) for _, n in PIECES),
            pltpu.VMEM((2, 224, 512), BF16),
            pltpu.VMEM((2, 448, 256), BF16),
            pltpu.VMEM((512, 256), BF16),
            pltpu.VMEM((224, 448), BF16),
            pltpu.VMEM((2, 2, 8, NZ, HALF), BF16),
            pltpu.VMEM((2, 2, 8, NZ, HALF), BF16),
            pltpu.VMEM((2, 2, NZ, 16, 128), BF16),
            pltpu.VMEM((2, 2, NZ, 16, 128), BF16),
            pltpu.SemaphoreType.DMA((6,)),
            pltpu.SemaphoreType.DMA((2, STAGES)),
            pltpu.SemaphoreType.DMA((2, STAGES)),
        ],
        compiler_params=pltpu.CompilerParams(
            collective_id=0, has_side_effects=True, vmem_limit_bytes=32 * 1024 * 1024
        ),
        name="triangle",
    )(*(pltpu.with_memory_space_constraint(x, pltpu.HBM) for x in (pair, pair_mask, w_ab, w_gate, w_out)))


def solution(mesh):
    return jax.shard_map(
        body,
        mesh=mesh,
        in_specs=(P("row", "grp", None), P("row", "grp"), P(), P(), P()),
        out_specs=P("row", "grp", None),
        check_vma=False,
    )
```

```python
import jax
import jax.numpy as jnp
from jax import lax
from jax.experimental import pallas as pl
from jax.experimental.pallas import tpu as pltpu
from jax.sharding import PartitionSpec as P

MESH = pl.DeviceIdType.MESH
F32, BF16 = jnp.float32, jnp.bfloat16
NZ, NG, ROWS, COLS, RS, MS, CH = 16, 8, 7, 56, 8, 64, 128
TOK = RS * MS
HALF = TOK // 2
AROUND = (8, 7, 9, 6, 10, 5, 11, 4, 12, 3, 13, 2, 14, 1, 15)
FAR = (6, 5, 7, 2, 4, 1, 3, 0)
EARLY, LATE = 0, 1
F1, F2, B1, B2, STAGES = 0, 2, 6, 8, 10


def mm(a, b, ca=1, cb=0):
    return lax.dot_general(a, b, (((ca,), (cb,)), ((), ())), preferred_element_type=F32)


def iota2(shape):
    return lax.broadcasted_iota(jnp.int32, shape, 0), lax.broadcasted_iota(jnp.int32, shape, 1)


def one_hot(hit):
    return jnp.where(hit, 1.0, 0.0).astype(BF16)


def normalize(x, axes):
    count = 1
    for a in axes:
        count *= x.shape[a]
    mean = jnp.sum(x, axis=axes, keepdims=True) * (1.0 / count)
    cen = x - mean
    var = jnp.sum(cen * cen, axis=axes, keepdims=True) * (1.0 / count)
    return cen * lax.rsqrt(var + 1e-05)


def sigmoid(x):
    return 0.5 * jnp.tanh(0.5 * x) + 0.5


def kernel(
    pair_hbm, mask_hbm, wab_hbm, wg_hbm, wo_hbm, out_ref,
    pair_ref, mask_ref, wab_ref, wg_ref, wo_ref, wabt, wgt, wot, perm, cols,
    ztok, zt, zn, gate, s1, r1, s2, r2, y0, y1, e0, e1, part0, part1, s3, r3, s4, r4, insem, ssem, rsem,
):
    loads = [
        pltpu.make_async_copy(src, dst, insem.at[n])
        for n, (src, dst) in enumerate(
            (
                (pair_hbm, pair_ref), (wab_hbm.at[0], wab_ref.at[0]), (mask_hbm, mask_ref), (wab_hbm.at[1], wab_ref.at[1]),
                (wg_hbm, wg_ref), (wo_hbm, wo_ref),
            )
        )
    ]
    for load in loads:
        load.start()

    row, g = lax.axis_index("row"), lax.axis_index("grp")
    core = lax.rem(row, 2)
    z = lax.rem(row // 2, NZ)
    yl = row // (2 * NZ)

    mate = 1 - core
    odd = lax.rem(g, 2)

    def dev(yl_, z_, core_, g_):
        return (yl_ * (2 * NZ) + z_ * 2 + core_, g_)

    barrier = pltpu.get_barrier_semaphore()

    def greet(device):
        pl.semaphore_signal(barrier, inc=1, device_id=device, device_id_type=MESH)

    for d in AROUND:
        greet(dev(yl, lax.rem(z + d, NZ), core, g))
    for d in FAR:
        for yl_to in (yl, 1 - yl):
            for core_to in (core, mate):
                if d or yl_to is not yl or core_to is not core:
                    greet(dev(yl_to, z, core_to, lax.rem(g + d, NG)))

    def send(src, dst, u, stage, device, is_self=None):
        def remote():
            pltpu.make_async_remote_copy(
                src_ref=src, dst_ref=dst, send_sem=ssem.at[u, stage], recv_sem=rsem.at[u, stage],
                device_id=device, device_id_type=MESH,
            ).start()

        if is_self is None:
            remote()
            return

        @pl.when(is_self)
        def _():
            pltpu.make_async_copy(src, dst, rsem.at[u, stage]).start()

        pl.when(jnp.logical_not(is_self))(remote)

    def send_z(src, dst, u, stage):
        for d in AROUND:
            to = lax.rem(z + d, NZ)
            send(src.at[to], dst.at[z], u, stage, dev(yl, to, core, g))
        pltpu.make_async_copy(src.at[z], dst.at[z], rsem.at[u, stage]).start()

    def wait_all(ref, sem):
        pltpu.make_async_copy(ref, ref, sem).wait()

    def slot_rows(r):
        return pl.ds(pl.multiple_of((r + odd * (1 - 2 * (r % 2))) * MS, MS), COLS)

    low = lax.broadcasted_iota(jnp.int32, (NZ, 128), 1) < 64
    ztok[...] = jnp.zeros_like(ztok)

    k, l = iota2((COLS, TOK))
    places = one_hot(lax.rem(l, MS) == k)
    k, l = iota2((ROWS, TOK))
    loads[2].wait()
    spread = mm(mask_ref[...].astype(F32).astype(BF16), places)
    keep = jnp.sum(jnp.where(l // MS == k + odd * (1 - 2 * lax.rem(k, 2)), spread, 0.0), axis=0, keepdims=True)

    loads[1].wait()
    wabt[0] = wab_ref[0].T
    loads[0].wait()
    for r in range(ROWS):
        ztok[slot_rows(r), :] = pair_ref[r].astype(F32)
    zt[...] = ztok[...].T

    def lanes(h):
        return slice(HALF * h, HALF * h + HALF)

    def norm(h):
        zn[:, lanes(h)] = normalize(zt[:, lanes(h)], (0,)).astype(BF16)

    def push(u, h):
        def side(base):
            p = mm(wabt[u, base : base + 2 * CH, :], zn[:, lanes(h)])
            return (sigmoid(p[:CH]) * p[CH:] * keep[:, lanes(h)]).reshape(NZ, NG, HALF)

        left, right = side(0), side(2 * CH)
        s1[u, h] = jnp.concatenate([right, left] if u == 0 else [left, right], axis=1).astype(BF16)
        send_z(s1.at[u, h], r1.at[u, h], u, F1 + h)

    def constants():
        for load in loads[3:]:
            load.wait()
        wgt[0], wgt[1] = wg_ref[0].T, wg_ref[1].T
        wot[0], wot[1] = wo_ref[0].T, wo_ref[1].T
        wabt[1] = wab_ref[1].T
        o, i = iota2((256, 256))
        perm[...] = one_hot(i == lax.rem(o, 16) * 16 + o // 16)
        i, l = iota2((224, 256))
        zi, n = lax.rem(i, NZ), i // NZ
        ci = jnp.where(n < 8, n // 4, (n - 8) // 3)
        ri = jnp.where(n < 8, lax.rem(n, 4), 4 + lax.rem(n - 8, 3))
        cols[...] = one_hot(l == zi // 4 * MS + lax.rem(zi, 4) * 14 + ci * 7 + ri)

    def channels_apart(u, h):
        x = mm(perm[...], r1[u, h].reshape(256, HALF)).astype(BF16)
        for e in (EARLY, LATE):
            s2[u, e, h] = x[128 * e : 128 * e + 128].reshape(NG, NZ, HALF)

    def send_early(u, t, a, slot):
        for d in FAR:
            h = lax.rem(g + d, NG)
            for yl_to in (yl, 1 - yl):
                send(
                    s2.at[u, EARLY, t, h], r2.at[u, EARLY, t, slot], u, F2 + t, dev(yl_to, z, a, h),
                    a == core if d == 0 and yl_to is yl else None,
                )

    def send_late(u, t, a, slot):
        for d in FAR:
            h = lax.rem(g + d, NG)
            for core_to in (core, mate):
                send(
                    s2.at[u, LATE, t, h], r2.at[u, LATE, t, slot], u, F2 + 2 + t, dev(a, z, core_to, h),
                    a == yl if d == 0 and core_to is core else None,
                )

    def assemble(u, e, h):
        n_src, n_g = (2, 8) if u == 0 else (4, 4)
        to = y0 if u == 0 else y1
        for s in range(n_src):
            for q in range(n_g // 2):
                for t in range(2):
                    at = slice(128 * t, 128 * t + 128)
                    even, other = r2[u, e, h, s * n_g + 2 * q, :, at], r2[u, e, h, s * n_g + 2 * q + 1, :, at]
                    r = 4 * h + 2 * t
                    row = (s * 4 + r if h == 0 else n_src * 4 + s * 3 + r - 4) * NZ
                    to_lanes = slice(128 * q, 128 * q + 128)
                    to[e, row : row + NZ, to_lanes] = jnp.where(low, even, other)
                    if r + 1 < ROWS:
                        to[e, row + NZ : row + 2 * NZ, to_lanes] = pltpu.roll(jnp.where(low, other, even), 64, 1)

    def finish(u, h):
        x = r4[u, h].astype(F32).reshape(NZ, 2, NG, 128)
        tn = jnp.concatenate([normalize(x[:, t], (0, 1)).reshape(CH, 128) for t in range(2)], axis=1).astype(BF16)
        out = mm(wot[u], tn)
        zt[:, lanes(h)] = (zt[:, lanes(h)] + gate[:, lanes(h)] * out).astype(BF16).astype(F32)

    for u in range(2):
        a = yl if u == 0 else g // 4
        slot = core * NG + g if u == 0 else (core * 2 + yl) * 4 + lax.rem(g, 4)
        if u == 0:
            norm(0)
            pl.semaphore_wait(barrier, NZ - 1 + 4 * NG - 1)
            push(u, 0)
            norm(1)
            constants()
        gate[...] = sigmoid(mm(wgt[u], zn[...]))
        if u == 0:
            push(u, 1)

        for h in range(2):
            wait_all(r1.at[u, h], rsem.at[u, F1 + h])
            channels_apart(u, h)
            send_early(u, h, a, slot)
            send_late(u, h, a, slot)

        for e in (EARLY, LATE):
            wait_all(r2.at[u, e, 0], rsem.at[u, F2 + 2 * e])
            assemble(u, e, 0)
        if u == 0:
            part0[...] = mm(y0[EARLY, :128], cols[:128], 0, 0)
        else:
            e1[:, :256] = mm(cols[...], y1[EARLY, :256], 1, 1).astype(BF16)
            part1[...] = mm(e1[:, :256], y1[LATE, :256])
        wait_all(r2.at[u, EARLY, 1], rsem.at[u, F2 + 1])
        assemble(u, EARLY, 1)
        if u == 0:
            e0[...] = (part0[...] + mm(y0[EARLY, 128:], cols[128:], 0, 0)).astype(BF16)
        else:
            e1[:, 256:] = mm(cols[...], y1[EARLY, 256:], 1, 1).astype(BF16)

        i_half, j_half = (yl, core) if u == 0 else (core, yl)
        for h in range(2):
            n_r = 4 - h
            rows = slice(128 * h, 128 * h + 32 * n_r)
            if h == 1 - u:
                wait_all(r2.at[u, LATE, 1], rsem.at[u, F2 + 3])
                assemble(u, LATE, 1)
            if u == 0:
                tri = mm(y0[LATE, rows, :], e0[...]).astype(BF16)
            else:
                tri = (part1[rows, :] + mm(e1[rows, 256:], y1[LATE, 256:])).astype(BF16)
            for ci in range(2):
                for t in range(2):
                    for q in range(2):
                        at = slice(128 * q, 128 * q + 128)
                        base = (ci * n_r + 2 * t) * NZ
                        c0 = tri[base : base + NZ, at]
                        c1 = tri[base + NZ : base + 2 * NZ, at] if 2 * t + 1 < n_r else jnp.zeros_like(c0)
                        c1 = pltpu.roll(c1, 64, 1)
                        s3[u, h, ci * 4 + 2 * q, :, 128 * t : 128 * t + 128] = jnp.where(low, c0, c1)
                        s3[u, h, ci * 4 + 2 * q + 1, :, 128 * t : 128 * t + 128] = jnp.where(low, c1, c0)

            for d in (2, 1, 3, 0):
                q = lax.rem(g + d, 4)
                to = 4 * j_half + q
                for ci in (mate, core):
                    send(
                        s3.at[u, h, ci * 4 + q], r3.at[u, h, g], u, B1 + h, dev(i_half, z, ci, to),
                        (i_half == yl) & (to == g) if d == 0 and ci is core else None,
                    )

        for h in range(2):
            wait_all(r3.at[u, h], rsem.at[u, B1 + h])
            x = r3[u, h].reshape(NG * NZ, HALF)
            x = jnp.concatenate([x[:, :128], x[:, 128:]], axis=0)
            s4[u, h] = mm(perm[...], x).astype(BF16).reshape(NZ, 16, 128)
            send_z(s4.at[u, h], r4.at[u, h], u, B2 + h)
        for h in range(2):
            wait_all(r4.at[u, h], rsem.at[u, B2 + h])
            finish(u, h)
            if u == 0:
                norm(h)
                push(1, h)
            else:
                ztok[lanes(h), :] = zt[:, lanes(h)].T
                for r in range(4 * h, min(4 * h + 4, ROWS)):
                    out_ref[r] = ztok[slot_rows(r), :].astype(BF16)

    def wait_sent(u, stage, ref, count, less):
        @pl.when(less)
        def _():
            wait_all(ref.at[pl.ds(0, count - 1)], ssem.at[u, stage])

        @pl.when(jnp.logical_not(less))
        def _():
            wait_all(ref.at[pl.ds(0, count)], ssem.at[u, stage])

    for u in range(2):
        a = yl if u == 0 else g // 4
        for h in range(2):
            wait_all(s1.at[u, h, pl.ds(0, NZ - 1)], ssem.at[u, F1 + h])
        for h in range(2):
            wait_sent(u, F2 + h, r2.at[u, EARLY, h], 2 * NG, a == core)
            wait_sent(u, F2 + 2 + h, r2.at[u, LATE, h], 2 * NG, a == yl)
            wait_sent(u, B1 + h, s3.at[u, h], 8, g // 4 == core if u == 0 else (core == yl) & (g // 4 == yl))
            wait_all(s4.at[u, h, pl.ds(0, NZ - 1)], ssem.at[u, B2 + h])


def body(pair, pair_mask, w_ab, w_gate, w_out):
    return pl.pallas_call(
        kernel,
        out_shape=pltpu.VMEM(pair.shape, pair.dtype),
        in_specs=[pl.BlockSpec(memory_space=pltpu.HBM)] * 5,
        out_specs=pl.BlockSpec(memory_space=pltpu.VMEM),
        scratch_shapes=[
            pltpu.VMEM((ROWS, COLS, CH), BF16),
            pltpu.VMEM((ROWS, COLS), jnp.int32),
            pltpu.VMEM((2, CH, 4 * CH), BF16),
            pltpu.VMEM((2, CH, CH), BF16),
            pltpu.VMEM((2, CH, CH), BF16),
            pltpu.VMEM((2, 4 * CH, CH), BF16),
            pltpu.VMEM((2, CH, CH), BF16),
            pltpu.VMEM((2, CH, CH), BF16),
            pltpu.VMEM((256, 256), BF16),
            pltpu.VMEM((224, 256), BF16),
            pltpu.VMEM((TOK, CH), F32),
            pltpu.VMEM((CH, TOK), F32),
            pltpu.VMEM((CH, TOK), BF16),
            pltpu.VMEM((CH, TOK), F32),
            pltpu.VMEM((2, 2, NZ, 16, HALF), BF16),
            pltpu.VMEM((2, 2, NZ, 16, HALF), BF16),
            pltpu.VMEM((2, 2, 2, NG, NZ, HALF), BF16),
            pltpu.VMEM((2, 2, 2, 16, NZ, HALF), BF16),
            pltpu.VMEM((2, 224, 512), BF16),
            pltpu.VMEM((2, 448, 256), BF16),
            pltpu.VMEM((512, 256), BF16),
            pltpu.VMEM((224, 448), BF16),
            pltpu.VMEM((512, 256), F32),
            pltpu.VMEM((224, 256), F32),
            pltpu.VMEM((2, 2, 8, NZ, HALF), BF16),
            pltpu.VMEM((2, 2, 8, NZ, HALF), BF16),
            pltpu.VMEM((2, 2, NZ, 16, 128), BF16),
            pltpu.VMEM((2, 2, NZ, 16, 128), BF16),
            pltpu.SemaphoreType.DMA((6,)),
            pltpu.SemaphoreType.DMA((2, STAGES)),
            pltpu.SemaphoreType.DMA((2, STAGES)),
        ],
        compiler_params=pltpu.CompilerParams(
            collective_id=0, has_side_effects=True, vmem_limit_bytes=32 * 1024 * 1024
        ),
        name="triangle",
    )(*(pltpu.with_memory_space_constraint(x, pltpu.HBM) for x in (pair, pair_mask, w_ab, w_gate, w_out)))


def solution(mesh):
    return jax.shard_map(
        body,
        mesh=mesh,
        in_specs=(P("row", "grp", None), P("row", "grp"), P(), P(), P()),
        out_specs=P("row", "grp", None),
        check_vma=False,
    )
```

```python
import jax
import jax.numpy as jnp
from jax import lax
from jax.experimental import pallas as pl
from jax.experimental.pallas import tpu as pltpu
from jax.sharding import PartitionSpec as P

MESH = pl.DeviceIdType.MESH
F32, BF16 = jnp.float32, jnp.bfloat16
NZ, NG, ROWS, COLS, RS, MS, CH = 16, 8, 7, 56, 8, 64, 128
TOK = RS * MS
HALF = TOK // 2
AROUND = (8, 7, 9, 6, 10, 5, 11, 4, 12, 3, 13, 2, 14, 1, 15)
FAR = (6, 5, 7, 2, 4, 1, 3, 0)
EARLY, LATE = 0, 1
F1, F2, MATE, B1, B2, STAGES = 0, 2, 6, 8, 10, 12


def mm(a, b, ca=1, cb=0):
    return lax.dot_general(a, b, (((ca,), (cb,)), ((), ())), preferred_element_type=F32)


def iota2(shape):
    return lax.broadcasted_iota(jnp.int32, shape, 0), lax.broadcasted_iota(jnp.int32, shape, 1)


def one_hot(hit):
    return jnp.where(hit, 1.0, 0.0).astype(BF16)


def normalize(x, axes):
    count = 1
    for a in axes:
        count *= x.shape[a]
    mean = jnp.sum(x, axis=axes, keepdims=True) * (1.0 / count)
    cen = x - mean
    var = jnp.sum(cen * cen, axis=axes, keepdims=True) * (1.0 / count)
    return cen * lax.rsqrt(var + 1e-05)


def sigmoid(x):
    return 0.5 * jnp.tanh(0.5 * x) + 0.5


def kernel(
    pair_hbm, mask_hbm, wab_hbm, wg_hbm, wo_hbm, out_ref,
    pair_ref, mask_ref, wab_ref, wg_ref, wo_ref, wabt, wgt, wot, perm, cols,
    ztok, zt, zn, gate, s1, r1, s2, r2, y0, y1, e0, e1, part0, part1, s3, r3, s4, r4, insem, ssem, rsem,
):
    loads = [
        pltpu.make_async_copy(src, dst, insem.at[n])
        for n, (src, dst) in enumerate(
            (
                (pair_hbm, pair_ref), (wab_hbm.at[0], wab_ref.at[0]), (mask_hbm, mask_ref), (wab_hbm.at[1], wab_ref.at[1]),
                (wg_hbm, wg_ref), (wo_hbm, wo_ref),
            )
        )
    ]
    for load in loads:
        load.start()

    row, g = lax.axis_index("row"), lax.axis_index("grp")
    core = lax.rem(row, 2)
    z = lax.rem(row // 2, NZ)
    yl = row // (2 * NZ)

    mate = 1 - core
    odd = lax.rem(g, 2)

    def dev(yl_, z_, core_, g_):
        return (yl_ * (2 * NZ) + z_ * 2 + core_, g_)

    barrier = pltpu.get_barrier_semaphore()

    def greet(device):
        pl.semaphore_signal(barrier, inc=1, device_id=device, device_id_type=MESH)

    for d in AROUND:
        greet(dev(yl, lax.rem(z + d, NZ), core, g))
    for d in FAR:
        for yl_to in (yl, 1 - yl):
            for core_to in (core, mate):
                if d or yl_to is not yl or core_to is not core:
                    greet(dev(yl_to, z, core_to, lax.rem(g + d, NG)))

    def send(src, dst, u, stage, device, is_self=None):
        def remote():
            pltpu.make_async_remote_copy(
                src_ref=src, dst_ref=dst, send_sem=ssem.at[u, stage], recv_sem=rsem.at[u, stage],
                device_id=device, device_id_type=MESH,
            ).start()

        if is_self is None:
            remote()
            return

        @pl.when(is_self)
        def _():
            pltpu.make_async_copy(src, dst, rsem.at[u, stage]).start()

        pl.when(jnp.logical_not(is_self))(remote)

    def send_z(src, dst, u, stage):
        for d in AROUND:
            to = lax.rem(z + d, NZ)
            send(src.at[to], dst.at[z], u, stage, dev(yl, to, core, g))
        pltpu.make_async_copy(src.at[z], dst.at[z], rsem.at[u, stage]).start()

    def wait_all(ref, sem):
        pltpu.make_async_copy(ref, ref, sem).wait()

    def slot_rows(r):
        return pl.ds(pl.multiple_of((r + odd * (1 - 2 * (r % 2))) * MS, MS), COLS)

    low = lax.broadcasted_iota(jnp.int32, (NZ, 128), 1) < 64
    ztok[...] = jnp.zeros_like(ztok)

    k, l = iota2((COLS, TOK))
    places = one_hot(lax.rem(l, MS) == k)
    k, l = iota2((ROWS, TOK))
    loads[2].wait()
    spread = mm(mask_ref[...].astype(F32).astype(BF16), places)
    keep = jnp.sum(jnp.where(l // MS == k + odd * (1 - 2 * lax.rem(k, 2)), spread, 0.0), axis=0, keepdims=True)

    loads[1].wait()
    wabt[0] = wab_ref[0].T
    loads[0].wait()
    for r in range(ROWS):
        ztok[slot_rows(r), :] = pair_ref[r].astype(F32)
    zt[...] = ztok[...].T

    def lanes(h):
        return slice(HALF * h, HALF * h + HALF)

    def norm(h):
        zn[:, lanes(h)] = normalize(zt[:, lanes(h)], (0,)).astype(BF16)

    def push(u, h):
        def side(base):
            p = mm(wabt[u, base : base + 2 * CH, :], zn[:, lanes(h)])
            return (sigmoid(p[:CH]) * p[CH:] * keep[:, lanes(h)]).reshape(NZ, NG, HALF)

        left, right = side(0), side(2 * CH)
        s1[u, h] = jnp.concatenate([right, left] if u == 0 else [left, right], axis=1).astype(BF16)
        send_z(s1.at[u, h], r1.at[u, h], u, F1 + h)

    def constants():
        for load in loads[3:]:
            load.wait()
        wgt[0], wgt[1] = wg_ref[0].T, wg_ref[1].T
        wot[0], wot[1] = wo_ref[0].T, wo_ref[1].T
        wabt[1] = wab_ref[1].T
        o, i = iota2((256, 256))
        perm[...] = one_hot(i == lax.rem(o, 16) * 16 + o // 16)
        i, l = iota2((224, 256))
        zi, n = lax.rem(i, NZ), i // NZ
        ci = jnp.where(n < 8, n // 4, (n - 8) // 3)
        ri = jnp.where(n < 8, lax.rem(n, 4), 4 + lax.rem(n - 8, 3))
        cols[...] = one_hot(l == zi // 4 * MS + lax.rem(zi, 4) * 14 + ci * 7 + ri)

    def channels_apart(u, h):
        x = mm(perm[...], r1[u, h].reshape(256, HALF)).astype(BF16)
        for e in (EARLY, LATE):
            s2[u, e, h] = x[128 * e : 128 * e + 128].reshape(NG, NZ, HALF)

    def send_early(u, t, a, slot):
        for d in FAR:
            h = lax.rem(g + d, NG)
            for yl_to in (yl, 1 - yl):
                send(
                    s2.at[u, EARLY, t, h], r2.at[u, EARLY, t, slot], u, F2 + t, dev(yl_to, z, a, h),
                    a == core if d == 0 and yl_to is yl else None,
                )

    def send_late(u, t, a, slot):
        for d in FAR:
            h = lax.rem(g + d, NG)
            send(
                s2.at[u, LATE, t, h], r2.at[u, LATE, t, slot], u, F2 + 2 + t, dev(a, z, core, h),
                a == yl if d == 0 else None,
            )

    def hand_over(u, t):
        own = r2.at[u, LATE, t, pl.ds(core * NG, NG)]
        wait_all(own, rsem.at[u, F2 + 2 + t])
        send(own, own, u, MATE + t, dev(yl, z, mate, g))

    def assemble(u, e, h, cs):
        n_src, n_g = (1, 8) if u == 0 else (2, 4)
        to = y0 if u == 0 else y1
        for s in range(n_src):
            for q in range(n_g // 2):
                for t in range(2):
                    at = slice(128 * t, 128 * t + 128)
                    slot, source = cs * NG + s * n_g + 2 * q, cs * n_src + s
                    even, other = r2[u, e, h, slot, :, at], r2[u, e, h, slot + 1, :, at]
                    r = 4 * h + 2 * t
                    row = (source * 4 + r if h == 0 else n_src * 8 + source * 3 + r - 4) * NZ
                    to_lanes = slice(128 * q, 128 * q + 128)
                    if not isinstance(cs, int):
                        row = pl.multiple_of(row, NZ)
                    to[e, pl.ds(row, NZ), to_lanes] = jnp.where(low, even, other)
                    if r + 1 < ROWS:
                        to[e, pl.ds(row + NZ, NZ), to_lanes] = pltpu.roll(jnp.where(low, other, even), 64, 1)

    def finish(u, h):
        x = r4[u, h].astype(F32).reshape(NZ, 2, NG, 128)
        tn = jnp.concatenate([normalize(x[:, t], (0, 1)).reshape(CH, 128) for t in range(2)], axis=1).astype(BF16)
        out = mm(wot[u], tn)
        zt[:, lanes(h)] = (zt[:, lanes(h)] + gate[:, lanes(h)] * out).astype(BF16).astype(F32)

    for u in range(2):
        a = yl if u == 0 else g // 4
        slot = core * NG + g if u == 0 else (core * 2 + yl) * 4 + lax.rem(g, 4)
        if u == 0:
            norm(0)
            pl.semaphore_wait(barrier, NZ - 1 + 4 * NG - 1)
            push(u, 0)
            norm(1)
            constants()
        gate[...] = sigmoid(mm(wgt[u], zn[...]))
        if u == 0:
            push(u, 1)

        for h in range(2):
            wait_all(r1.at[u, h], rsem.at[u, F1 + h])
            channels_apart(u, h)
            send_early(u, h, a, slot)
            send_late(u, h, a, slot)

        hand_over(u, 0)
        wait_all(r2.at[u, EARLY, 0], rsem.at[u, F2])
        assemble(u, EARLY, 0, 0)
        assemble(u, EARLY, 0, 1)
        wait_all(r2.at[u, LATE, 0, pl.ds(0, NG)], rsem.at[u, MATE])
        assemble(u, LATE, 0, 0)
        assemble(u, LATE, 0, 1)
        if u == 0:
            part0[...] = mm(y0[EARLY, :128], cols[:128], 0, 0)
        else:
            e1[:, :256] = mm(cols[...], y1[EARLY, :256], 1, 1).astype(BF16)
            part1[...] = mm(e1[:, :256], y1[LATE, :256])
        wait_all(r2.at[u, EARLY, 1], rsem.at[u, F2 + 1])
        assemble(u, EARLY, 1, 0)
        assemble(u, EARLY, 1, 1)
        if u == 0:
            e0[...] = (part0[...] + mm(y0[EARLY, 128:], cols[128:], 0, 0)).astype(BF16)
        else:
            e1[:, 256:] = mm(cols[...], y1[EARLY, 256:], 1, 1).astype(BF16)

        i_half, j_half = (yl, core) if u == 0 else (core, yl)
        for h in range(2):
            n_r = 4 - h
            rows = slice(128 * h, 128 * h + 32 * n_r)
            if h == 1 - u:
                hand_over(u, 1)
                assemble(u, LATE, 1, core)
                wait_all(r2.at[u, LATE, 1, pl.ds(0, NG)], rsem.at[u, MATE + 1])
                assemble(u, LATE, 1, mate)
            if u == 0:
                tri = mm(y0[LATE, rows, :], e0[...]).astype(BF16)
            else:
                tri = (part1[rows, :] + mm(e1[rows, 256:], y1[LATE, 256:])).astype(BF16)
            for ci in range(2):
                for t in range(2):
                    for q in range(2):
                        at = slice(128 * q, 128 * q + 128)
                        base = (ci * n_r + 2 * t) * NZ
                        c0 = tri[base : base + NZ, at]
                        c1 = tri[base + NZ : base + 2 * NZ, at] if 2 * t + 1 < n_r else jnp.zeros_like(c0)
                        c1 = pltpu.roll(c1, 64, 1)
                        s3[u, h, ci * 4 + 2 * q, :, 128 * t : 128 * t + 128] = jnp.where(low, c0, c1)
                        s3[u, h, ci * 4 + 2 * q + 1, :, 128 * t : 128 * t + 128] = jnp.where(low, c1, c0)

            for d in (2, 1, 3, 0):
                q = lax.rem(g + d, 4)
                to = 4 * j_half + q
                for ci in (mate, core):
                    send(
                        s3.at[u, h, ci * 4 + q], r3.at[u, h, g], u, B1 + h, dev(i_half, z, ci, to),
                        (i_half == yl) & (to == g) if d == 0 and ci is core else None,
                    )

        for h in range(2):
            wait_all(r3.at[u, h], rsem.at[u, B1 + h])
            x = r3[u, h].reshape(NG * NZ, HALF)
            x = jnp.concatenate([x[:, :128], x[:, 128:]], axis=0)
            s4[u, h] = mm(perm[...], x).astype(BF16).reshape(NZ, 16, 128)
            send_z(s4.at[u, h], r4.at[u, h], u, B2 + h)
        for h in range(2):
            wait_all(r4.at[u, h], rsem.at[u, B2 + h])
            finish(u, h)
            if u == 0:
                norm(h)
                push(1, h)
            else:
                ztok[lanes(h), :] = zt[:, lanes(h)].T
                for r in range(4 * h, min(4 * h + 4, ROWS)):
                    out_ref[r] = ztok[slot_rows(r), :].astype(BF16)

    def wait_sent(u, stage, ref, count, less):
        @pl.when(less)
        def _():
            wait_all(ref.at[pl.ds(0, count - 1)], ssem.at[u, stage])

        @pl.when(jnp.logical_not(less))
        def _():
            wait_all(ref.at[pl.ds(0, count)], ssem.at[u, stage])

    for u in range(2):
        a = yl if u == 0 else g // 4
        for h in range(2):
            wait_all(s1.at[u, h, pl.ds(0, NZ - 1)], ssem.at[u, F1 + h])
        for h in range(2):
            wait_sent(u, F2 + h, r2.at[u, EARLY, h], 2 * NG, a == core)
            wait_sent(u, F2 + 2 + h, r2.at[u, LATE, h], NG, a == yl)
            wait_all(r2.at[u, LATE, h, pl.ds(0, NG)], ssem.at[u, MATE + h])
            wait_sent(u, B1 + h, s3.at[u, h], 8, g // 4 == core if u == 0 else (core == yl) & (g // 4 == yl))
            wait_all(s4.at[u, h, pl.ds(0, NZ - 1)], ssem.at[u, B2 + h])


def body(pair, pair_mask, w_ab, w_gate, w_out):
    return pl.pallas_call(
        kernel,
        out_shape=pltpu.VMEM(pair.shape, pair.dtype),
        in_specs=[pl.BlockSpec(memory_space=pltpu.HBM)] * 5,
        out_specs=pl.BlockSpec(memory_space=pltpu.VMEM),
        scratch_shapes=[
            pltpu.VMEM((ROWS, COLS, CH), BF16),
            pltpu.VMEM((ROWS, COLS), jnp.int32),
            pltpu.VMEM((2, CH, 4 * CH), BF16),
            pltpu.VMEM((2, CH, CH), BF16),
            pltpu.VMEM((2, CH, CH), BF16),
            pltpu.VMEM((2, 4 * CH, CH), BF16),
            pltpu.VMEM((2, CH, CH), BF16),
            pltpu.VMEM((2, CH, CH), BF16),
            pltpu.VMEM((256, 256), BF16),
            pltpu.VMEM((224, 256), BF16),
            pltpu.VMEM((TOK, CH), F32),
            pltpu.VMEM((CH, TOK), F32),
            pltpu.VMEM((CH, TOK), BF16),
            pltpu.VMEM((CH, TOK), F32),
            pltpu.VMEM((2, 2, NZ, 16, HALF), BF16),
            pltpu.VMEM((2, 2, NZ, 16, HALF), BF16),
            pltpu.VMEM((2, 2, 2, NG, NZ, HALF), BF16),
            pltpu.VMEM((2, 2, 2, 16, NZ, HALF), BF16),
            pltpu.VMEM((2, 224, 512), BF16),
            pltpu.VMEM((2, 448, 256), BF16),
            pltpu.VMEM((512, 256), BF16),
            pltpu.VMEM((224, 448), BF16),
            pltpu.VMEM((512, 256), F32),
            pltpu.VMEM((224, 256), F32),
            pltpu.VMEM((2, 2, 8, NZ, HALF), BF16),
            pltpu.VMEM((2, 2, 8, NZ, HALF), BF16),
            pltpu.VMEM((2, 2, NZ, 16, 128), BF16),
            pltpu.VMEM((2, 2, NZ, 16, 128), BF16),
            pltpu.SemaphoreType.DMA((6,)),
            pltpu.SemaphoreType.DMA((2, STAGES)),
            pltpu.SemaphoreType.DMA((2, STAGES)),
        ],
        compiler_params=pltpu.CompilerParams(
            collective_id=0, has_side_effects=True, vmem_limit_bytes=32 * 1024 * 1024
        ),
        name="triangle",
    )(*(pltpu.with_memory_space_constraint(x, pltpu.HBM) for x in (pair, pair_mask, w_ab, w_gate, w_out)))


def solution(mesh):
    return jax.shard_map(
        body,
        mesh=mesh,
        in_specs=(P("row", "grp", None), P("row", "grp"), P(), P(), P()),
        out_specs=P("row", "grp", None),
        check_vma=False,
    )
```

```python
import jax
import jax.numpy as jnp
from jax import lax
from jax.experimental import pallas as pl
from jax.experimental.pallas import tpu as pltpu
from jax.sharding import PartitionSpec as P

MESH = pl.DeviceIdType.MESH
F32, BF16 = jnp.float32, jnp.bfloat16
NZ, NG, ROWS, COLS, RS, MS, CH = 16, 8, 7, 56, 8, 64, 128
TOK = RS * MS
HALF = TOK // 2
AROUND = (8, 7, 9, 6, 10, 5, 11, 4, 12, 3, 13, 2, 14, 1, 15)
FAR = (6, 5, 7, 2, 4, 1, 3, 0)
EARLY, LATE = 0, 1
F1, F2, MATE, B1, B2, STAGES = 0, 2, 6, 8, 10, 12


def mm(a, b, ca=1, cb=0):
    return lax.dot_general(a, b, (((ca,), (cb,)), ((), ())), preferred_element_type=F32)


def iota2(shape):
    return lax.broadcasted_iota(jnp.int32, shape, 0), lax.broadcasted_iota(jnp.int32, shape, 1)


def one_hot(hit):
    return jnp.where(hit, 1.0, 0.0).astype(BF16)


def normalize(x, axes):
    count = 1
    for a in axes:
        count *= x.shape[a]
    mean = jnp.sum(x, axis=axes, keepdims=True) * (1.0 / count)
    cen = x - mean
    var = jnp.sum(cen * cen, axis=axes, keepdims=True) * (1.0 / count)
    return cen * lax.rsqrt(var + 1e-05)


def sigmoid(x):
    return 0.5 * jnp.tanh(0.5 * x) + 0.5


def kernel(
    pair_hbm, mask_hbm, wab_hbm, wg_hbm, wo_hbm, out_ref,
    pair_ref, mask_ref, wab_ref, wg_ref, wo_ref, wabt, wgt, wot, perm, cols,
    ztok, zt, zn, gate, s1, r1, s2, r2, y0, y1, e0, e1, part0, part1, s3, r3, s4, r4, insem, ssem, rsem,
):
    loads = [
        pltpu.make_async_copy(src, dst, insem.at[n])
        for n, (src, dst) in enumerate(
            (
                (pair_hbm, pair_ref), (wab_hbm.at[0], wab_ref.at[0]), (mask_hbm, mask_ref), (wab_hbm.at[1], wab_ref.at[1]),
                (wg_hbm, wg_ref), (wo_hbm, wo_ref),
            )
        )
    ]
    for load in loads:
        load.start()

    row, g = lax.axis_index("row"), lax.axis_index("grp")
    core = lax.rem(row, 2)
    z = lax.rem(row // 2, NZ)
    yl = row // (2 * NZ)

    mate = 1 - core
    odd = lax.rem(g, 2)

    def dev(yl_, z_, core_, g_):
        return (yl_ * (2 * NZ) + z_ * 2 + core_, g_)

    barrier = pltpu.get_barrier_semaphore()

    def greet(device):
        pl.semaphore_signal(barrier, inc=1, device_id=device, device_id_type=MESH)

    for d in AROUND:
        greet(dev(yl, lax.rem(z + d, NZ), core, g))
    for d in FAR:
        for yl_to in (yl, 1 - yl):
            for core_to in (core, mate):
                if d or yl_to is not yl or core_to is not core:
                    greet(dev(yl_to, z, core_to, lax.rem(g + d, NG)))

    def send(src, dst, u, stage, device, is_self=None):
        def remote():
            pltpu.make_async_remote_copy(
                src_ref=src, dst_ref=dst, send_sem=ssem.at[u, stage], recv_sem=rsem.at[u, stage],
                device_id=device, device_id_type=MESH,
            ).start()

        if is_self is None:
            remote()
            return

        @pl.when(is_self)
        def _():
            pltpu.make_async_copy(src, dst, rsem.at[u, stage]).start()

        pl.when(jnp.logical_not(is_self))(remote)

    def send_z(src, dst, u, stage):
        for d in AROUND:
            to = lax.rem(z + d, NZ)
            send(src.at[to], dst.at[z], u, stage, dev(yl, to, core, g))
        pltpu.make_async_copy(src.at[z], dst.at[z], rsem.at[u, stage]).start()

    def wait_all(ref, sem):
        pltpu.make_async_copy(ref, ref, sem).wait()

    def slot_rows(r):
        return pl.ds(pl.multiple_of((r + odd * (1 - 2 * (r % 2))) * MS, MS), COLS)

    low = lax.broadcasted_iota(jnp.int32, (NZ, 128), 1) < 64
    ztok[...] = jnp.zeros_like(ztok)

    k, l = iota2((COLS, TOK))
    places = one_hot(lax.rem(l, MS) == k)
    k, l = iota2((ROWS, TOK))
    loads[2].wait()
    spread = mm(mask_ref[...].astype(F32).astype(BF16), places)
    keep = jnp.sum(jnp.where(l // MS == k + odd * (1 - 2 * lax.rem(k, 2)), spread, 0.0), axis=0, keepdims=True)

    loads[1].wait()
    wabt[0] = wab_ref[0].T
    loads[0].wait()
    for r in range(ROWS):
        ztok[slot_rows(r), :] = pair_ref[r].astype(F32)
    zt[:, :HALF] = ztok[:HALF].T

    def lanes(h):
        return slice(HALF * h, HALF * h + HALF)

    def norm(h):
        zn[:, lanes(h)] = normalize(zt[:, lanes(h)], (0,)).astype(BF16)

    def push(u, h):
        def side(base):
            p = mm(wabt[u, base : base + 2 * CH, :], zn[:, lanes(h)])
            return (sigmoid(p[:CH]) * p[CH:] * keep[:, lanes(h)]).reshape(NZ, NG, HALF)

        left, right = side(0), side(2 * CH)
        s1[u, h] = jnp.concatenate([right, left] if u == 0 else [left, right], axis=1).astype(BF16)
        send_z(s1.at[u, h], r1.at[u, h], u, F1 + h)

    def constants():
        for load in loads[3:]:
            load.wait()
        wgt[0], wgt[1] = wg_ref[0].T, wg_ref[1].T
        wot[0], wot[1] = wo_ref[0].T, wo_ref[1].T
        wabt[1] = wab_ref[1].T
        o, i = iota2((256, 256))
        perm[...] = one_hot(i == lax.rem(o, 16) * 16 + o // 16)
        i, l = iota2((224, 256))
        zi, n = lax.rem(i, NZ), i // NZ
        ci = jnp.where(n < 8, n // 4, (n - 8) // 3)
        ri = jnp.where(n < 8, lax.rem(n, 4), 4 + lax.rem(n - 8, 3))
        cols[...] = one_hot(l == zi // 4 * MS + lax.rem(zi, 4) * 14 + ci * 7 + ri)

    def channels_apart(u, h, e):
        x = mm(perm[128 * e : 128 * e + 128], r1[u, h].reshape(256, HALF)).astype(BF16)
        s2[u, e, h] = x.reshape(NG, NZ, HALF)

    def send_early(u, t, a, slot):
        for d in FAR:
            h = lax.rem(g + d, NG)
            for yl_to in (yl, 1 - yl):
                send(
                    s2.at[u, EARLY, t, h], r2.at[u, EARLY, t, slot], u, F2 + t, dev(yl_to, z, a, h),
                    a == core if d == 0 and yl_to is yl else None,
                )

    def send_late(u, t, a, slot):
        for d in FAR:
            h = lax.rem(g + d, NG)
            send(
                s2.at[u, LATE, t, h], r2.at[u, LATE, t, slot], u, F2 + 2 + t, dev(a, z, core, h),
                a == yl if d == 0 else None,
            )

    def hand_over(u, t):
        own = r2.at[u, LATE, t, pl.ds(core * NG, NG)]
        wait_all(own, rsem.at[u, F2 + 2 + t])
        send(own, own, u, MATE + t, dev(yl, z, mate, g))

    def assemble(u, e, h, cs):
        n_src, n_g = (1, 8) if u == 0 else (2, 4)
        to = y0 if u == 0 else y1
        for s in range(n_src):
            for q in range(n_g // 2):
                for t in range(2):
                    at = slice(128 * t, 128 * t + 128)
                    slot, source = cs * NG + s * n_g + 2 * q, cs * n_src + s
                    even, other = r2[u, e, h, slot, :, at], r2[u, e, h, slot + 1, :, at]
                    r = 4 * h + 2 * t
                    row = (source * 4 + r if h == 0 else n_src * 8 + source * 3 + r - 4) * NZ
                    to_lanes = slice(128 * q, 128 * q + 128)
                    if not isinstance(cs, int):
                        row = pl.multiple_of(row, NZ)
                    to[e, pl.ds(row, NZ), to_lanes] = jnp.where(low, even, other)
                    if r + 1 < ROWS:
                        to[e, pl.ds(row + NZ, NZ), to_lanes] = pltpu.roll(jnp.where(low, other, even), 64, 1)

    def finish(u, h):
        x = r4[u, h].astype(F32).reshape(NZ, 2, NG, 128)
        tn = jnp.concatenate([normalize(x[:, t], (0, 1)).reshape(CH, 128) for t in range(2)], axis=1).astype(BF16)
        out = mm(wot[u], tn)
        zt[:, lanes(h)] = (zt[:, lanes(h)] + gate[:, lanes(h)] * out).astype(BF16).astype(F32)

    for u in range(2):
        a = yl if u == 0 else g // 4
        slot = core * NG + g if u == 0 else (core * 2 + yl) * 4 + lax.rem(g, 4)
        if u == 0:
            norm(0)
            pl.semaphore_wait(barrier, NZ - 1 + 4 * NG - 1)
            push(u, 0)
            zt[:, HALF:] = ztok[HALF:].T
            norm(1)
            constants()
        gate[...] = sigmoid(mm(wgt[u], zn[...]))
        if u == 0:
            wait_all(s1.at[u, 0, pl.ds(0, NZ - 1)], ssem.at[u, F1])
            push(u, 1)

        for h in range(2):
            wait_all(r1.at[u, h], rsem.at[u, F1 + h])
            channels_apart(u, h, EARLY)
            send_early(u, h, a, slot)
            channels_apart(u, h, LATE)
            send_late(u, h, a, slot)

        hand_over(u, 0)
        wait_all(r2.at[u, EARLY, 0], rsem.at[u, F2])
        assemble(u, EARLY, 0, 0)
        assemble(u, EARLY, 0, 1)
        wait_all(r2.at[u, LATE, 0, pl.ds(0, NG)], rsem.at[u, MATE])
        assemble(u, LATE, 0, 0)
        assemble(u, LATE, 0, 1)
        if u == 0:
            part0[...] = mm(y0[EARLY, :128], cols[:128], 0, 0)
        else:
            e1[:, :256] = mm(cols[...], y1[EARLY, :256], 1, 1).astype(BF16)
            part1[...] = mm(e1[:, :256], y1[LATE, :256])
        wait_all(r2.at[u, EARLY, 1], rsem.at[u, F2 + 1])
        assemble(u, EARLY, 1, 0)
        assemble(u, EARLY, 1, 1)
        if u == 0:
            e0[...] = (part0[...] + mm(y0[EARLY, 128:], cols[128:], 0, 0)).astype(BF16)
        else:
            e1[:, 256:] = mm(cols[...], y1[EARLY, 256:], 1, 1).astype(BF16)

        i_half, j_half = (yl, core) if u == 0 else (core, yl)
        for h in range(2):
            n_r = 4 - h
            rows = slice(128 * h, 128 * h + 32 * n_r)
            if h == 1 - u:
                hand_over(u, 1)
                assemble(u, LATE, 1, core)
                wait_all(r2.at[u, LATE, 1, pl.ds(0, NG)], rsem.at[u, MATE + 1])
                assemble(u, LATE, 1, mate)
            if u == 0:
                tri = mm(y0[LATE, rows, :], e0[...]).astype(BF16)
            else:
                tri = (part1[rows, :] + mm(e1[rows, 256:], y1[LATE, 256:])).astype(BF16)
            for ci in range(2):
                for t in range(2):
                    for q in range(2):
                        at = slice(128 * q, 128 * q + 128)
                        base = (ci * n_r + 2 * t) * NZ
                        c0 = tri[base : base + NZ, at]
                        c1 = tri[base + NZ : base + 2 * NZ, at] if 2 * t + 1 < n_r else jnp.zeros_like(c0)
                        c1 = pltpu.roll(c1, 64, 1)
                        s3[u, h, ci * 4 + 2 * q, :, 128 * t : 128 * t + 128] = jnp.where(low, c0, c1)
                        s3[u, h, ci * 4 + 2 * q + 1, :, 128 * t : 128 * t + 128] = jnp.where(low, c1, c0)

            for d in (2, 1, 3, 0):
                q = lax.rem(g + d, 4)
                to = 4 * j_half + q
                for ci in (mate, core):
                    send(
                        s3.at[u, h, ci * 4 + q], r3.at[u, h, g], u, B1 + h, dev(i_half, z, ci, to),
                        (i_half == yl) & (to == g) if d == 0 and ci is core else None,
                    )

        for h in range(2):
            wait_all(r3.at[u, h], rsem.at[u, B1 + h])
            x = r3[u, h].reshape(NG * NZ, HALF)
            x = jnp.concatenate([x[:, :128], x[:, 128:]], axis=0)
            s4[u, h] = mm(perm[...], x).astype(BF16).reshape(NZ, 16, 128)
            send_z(s4.at[u, h], r4.at[u, h], u, B2 + h)
        for h in range(2):
            wait_all(r4.at[u, h], rsem.at[u, B2 + h])
            finish(u, h)
            if u == 0:
                norm(h)
                push(1, h)
            else:
                ztok[lanes(h), :] = zt[:, lanes(h)].T
                for r in range(4 * h, min(4 * h + 4, ROWS)):
                    out_ref[r] = ztok[slot_rows(r), :].astype(BF16)

    def wait_sent(u, stage, ref, count, less):
        @pl.when(less)
        def _():
            wait_all(ref.at[pl.ds(0, count - 1)], ssem.at[u, stage])

        @pl.when(jnp.logical_not(less))
        def _():
            wait_all(ref.at[pl.ds(0, count)], ssem.at[u, stage])

    for u in range(2):
        a = yl if u == 0 else g // 4
        for h in range(2):
            if u == 1 or h == 1:
                wait_all(s1.at[u, h, pl.ds(0, NZ - 1)], ssem.at[u, F1 + h])
        for h in range(2):
            wait_sent(u, F2 + h, r2.at[u, EARLY, h], 2 * NG, a == core)
            wait_sent(u, F2 + 2 + h, r2.at[u, LATE, h], NG, a == yl)
            wait_all(r2.at[u, LATE, h, pl.ds(0, NG)], ssem.at[u, MATE + h])
            wait_sent(u, B1 + h, s3.at[u, h], 8, g // 4 == core if u == 0 else (core == yl) & (g // 4 == yl))
            wait_all(s4.at[u, h, pl.ds(0, NZ - 1)], ssem.at[u, B2 + h])


def body(pair, pair_mask, w_ab, w_gate, w_out):
    return pl.pallas_call(
        kernel,
        out_shape=pltpu.VMEM(pair.shape, pair.dtype),
        in_specs=[pl.BlockSpec(memory_space=pltpu.HBM)] * 5,
        out_specs=pl.BlockSpec(memory_space=pltpu.VMEM),
        scratch_shapes=[
            pltpu.VMEM((ROWS, COLS, CH), BF16),
            pltpu.VMEM((ROWS, COLS), jnp.int32),
            pltpu.VMEM((2, CH, 4 * CH), BF16),
            pltpu.VMEM((2, CH, CH), BF16),
            pltpu.VMEM((2, CH, CH), BF16),
            pltpu.VMEM((2, 4 * CH, CH), BF16),
            pltpu.VMEM((2, CH, CH), BF16),
            pltpu.VMEM((2, CH, CH), BF16),
            pltpu.VMEM((256, 256), BF16),
            pltpu.VMEM((224, 256), BF16),
            pltpu.VMEM((TOK, CH), F32),
            pltpu.VMEM((CH, TOK), F32),
            pltpu.VMEM((CH, TOK), BF16),
            pltpu.VMEM((CH, TOK), F32),
            pltpu.VMEM((2, 2, NZ, 16, HALF), BF16),
            pltpu.VMEM((2, 2, NZ, 16, HALF), BF16),
            pltpu.VMEM((2, 2, 2, NG, NZ, HALF), BF16),
            pltpu.VMEM((2, 2, 2, 16, NZ, HALF), BF16),
            pltpu.VMEM((2, 224, 512), BF16),
            pltpu.VMEM((2, 448, 256), BF16),
            pltpu.VMEM((512, 256), BF16),
            pltpu.VMEM((224, 448), BF16),
            pltpu.VMEM((512, 256), F32),
            pltpu.VMEM((224, 256), F32),
            pltpu.VMEM((2, 2, 8, NZ, HALF), BF16),
            pltpu.VMEM((2, 2, 8, NZ, HALF), BF16),
            pltpu.VMEM((2, 2, NZ, 16, 128), BF16),
            pltpu.VMEM((2, 2, NZ, 16, 128), BF16),
            pltpu.SemaphoreType.DMA((6,)),
            pltpu.SemaphoreType.DMA((2, STAGES)),
            pltpu.SemaphoreType.DMA((2, STAGES)),
        ],
        compiler_params=pltpu.CompilerParams(
            collective_id=0, has_side_effects=True, vmem_limit_bytes=32 * 1024 * 1024
        ),
        name="triangle",
    )(*(pltpu.with_memory_space_constraint(x, pltpu.HBM) for x in (pair, pair_mask, w_ab, w_gate, w_out)))


def solution(mesh):
    return jax.shard_map(
        body,
        mesh=mesh,
        in_specs=(P("row", "grp", None), P("row", "grp"), P(), P(), P()),
        out_specs=P("row", "grp", None),
        check_vma=False,
    )
```

```python
import jax
import jax.numpy as jnp
from jax import lax
from jax.experimental import pallas as pl
from jax.experimental.pallas import tpu as pltpu
from jax.sharding import PartitionSpec as P

MESH = pl.DeviceIdType.MESH
F32, BF16 = jnp.float32, jnp.bfloat16
NZ, NG, ROWS, COLS, RS, MS, CH = 16, 8, 7, 56, 8, 64, 128
TOK = RS * MS
HALF = TOK // 2
AROUND = (8, 7, 9, 6, 10, 5, 11, 4, 12, 3, 13, 2, 14, 1, 15)
FAR = (6, 5, 7, 2, 4, 1, 3, 0)
EARLY, LATE = 0, 1
F1, F2, MATE, B1, B2, TAIL, STAGES = 0, 2, 6, 8, 10, 12, 13


def mm(a, b, ca=1, cb=0):
    return lax.dot_general(a, b, (((ca,), (cb,)), ((), ())), preferred_element_type=F32)


def iota2(shape):
    return lax.broadcasted_iota(jnp.int32, shape, 0), lax.broadcasted_iota(jnp.int32, shape, 1)


def one_hot(hit):
    return jnp.where(hit, 1.0, 0.0).astype(BF16)


def normalize(x, axes):
    count = 1
    for a in axes:
        count *= x.shape[a]
    mean = jnp.sum(x, axis=axes, keepdims=True) * (1.0 / count)
    cen = x - mean
    var = jnp.sum(cen * cen, axis=axes, keepdims=True) * (1.0 / count)
    return cen * lax.rsqrt(var + 1e-05)


def sigmoid(x):
    return 0.5 * jnp.tanh(0.5 * x) + 0.5


def kernel(
    pair_hbm, mask_hbm, wab_hbm, wg_hbm, wo_hbm, out_ref,
    pair_ref, mask_ref, wab_ref, wg_ref, wo_ref, wabt, wgt, wot, perm, cols, padded, s1d, r1d, st, rt, dense0,
    ztok, zt, zn, gate, s1, r1, s2, r2, y0, y1, e0, e1, part0, part1, s3, r3, s4, r4, insem, ssem, rsem,
):
    loads = [
        pltpu.make_async_copy(src, dst, insem.at[n])
        for n, (src, dst) in enumerate(
            (
                (pair_hbm, pair_ref), (wab_hbm.at[0], wab_ref.at[0]), (mask_hbm, mask_ref), (wab_hbm.at[1], wab_ref.at[1]),
                (wg_hbm, wg_ref), (wo_hbm, wo_ref),
            )
        )
    ]
    for load in loads:
        load.start()

    row, g = lax.axis_index("row"), lax.axis_index("grp")
    core = lax.rem(row, 2)
    z = lax.rem(row // 2, NZ)
    yl = row // (2 * NZ)

    mate = 1 - core
    odd = lax.rem(g, 2)

    def dev(yl_, z_, core_, g_):
        return (yl_ * (2 * NZ) + z_ * 2 + core_, g_)

    barrier = pltpu.get_barrier_semaphore()

    def greet(device):
        pl.semaphore_signal(barrier, inc=1, device_id=device, device_id_type=MESH)

    for d in AROUND:
        greet(dev(yl, lax.rem(z + d, NZ), core, g))
    for d in FAR:
        for yl_to in (yl, 1 - yl):
            for core_to in (core, mate):
                if d or yl_to is not yl or core_to is not core:
                    greet(dev(yl_to, z, core_to, lax.rem(g + d, NG)))

    def send(src, dst, u, stage, device, is_self=None):
        def remote():
            pltpu.make_async_remote_copy(
                src_ref=src, dst_ref=dst, send_sem=ssem.at[u, stage], recv_sem=rsem.at[u, stage],
                device_id=device, device_id_type=MESH,
            ).start()

        if is_self is None:
            remote()
            return

        @pl.when(is_self)
        def _():
            pltpu.make_async_copy(src, dst, rsem.at[u, stage]).start()

        pl.when(jnp.logical_not(is_self))(remote)

    def send_z(src, dst, u, stage):
        for d in AROUND:
            to = lax.rem(z + d, NZ)
            send(src.at[to], dst.at[z], u, stage, dev(yl, to, core, g))
        pltpu.make_async_copy(src.at[z], dst.at[z], rsem.at[u, stage]).start()

    def wait_all(ref, sem):
        pltpu.make_async_copy(ref, ref, sem).wait()

    def slot_rows(r):
        return pl.ds(pl.multiple_of((r + odd * (1 - 2 * (r % 2))) * MS, MS), COLS)

    low = lax.broadcasted_iota(jnp.int32, (NZ, 128), 1) < 64
    ztok[...] = jnp.zeros_like(ztok)

    k, l = iota2((COLS, TOK))
    places = one_hot(lax.rem(l, MS) == k)
    k, l = iota2((ROWS, TOK))
    loads[2].wait()
    spread = mm(mask_ref[...].astype(F32).astype(BF16), places)
    keep = jnp.sum(jnp.where(l // MS == k + odd * (1 - 2 * lax.rem(k, 2)), spread, 0.0), axis=0, keepdims=True)
    kc, lc = iota2((COLS, TOK))
    spread = mm(mask_ref[...].astype(F32).astype(BF16), one_hot(lax.rem(lc, COLS) == kc))
    keep_dense = jnp.sum(jnp.where(l // COLS == k, spread, 0.0), axis=0, keepdims=True)

    loads[1].wait()
    wabt[0] = wab_ref[0].T
    loads[0].wait()
    for r in range(ROWS):
        ztok[r * COLS : r * COLS + COLS, :] = pair_ref[r].astype(F32)
    zn[...] = normalize(ztok[...].T, (0,)).astype(BF16)

    def lanes(h):
        return slice(HALF * h, HALF * h + HALF)

    def norm(h):
        zn[:, lanes(h)] = normalize(zt[:, lanes(h)], (0,)).astype(BF16)

    def push(u, h):
        def side(base):
            p = mm(wabt[u, base : base + 2 * CH, :], zn[:, lanes(h)])
            return (sigmoid(p[:CH]) * p[CH:] * keep[:, lanes(h)]).reshape(NZ, NG, HALF)

        left, right = side(0), side(2 * CH)
        s1[u, h] = jnp.concatenate([right, left] if u == 0 else [left, right], axis=1).astype(BF16)
        send_z(s1.at[u, h], r1.at[u, h], u, F1 + h)

    def push_dense():
        def side(base):
            p = mm(wabt[0, base : base + 2 * CH, :], zn[...])
            return sigmoid(p[:CH]) * p[CH:] * keep_dense

        both = side(2 * CH), side(0)
        s1[0, 0] = jnp.concatenate([x[:, :256].reshape(NZ, NG, 256) for x in both], axis=1).astype(BF16)
        send_z(s1.at[0, 0], r1.at[0, 0], 0, F1)
        k, l = iota2((128, 128))
        spread_out = one_hot((k < 8) & (lax.rem(l, 8) == k))
        c = lax.broadcasted_iota(jnp.int32, (NZ, NG, 128), 1)
        l = lax.broadcasted_iota(jnp.int32, (NZ, NG, 128), 2)
        tail = jnp.zeros((NZ, 1, 128), F32)
        for e in (EARLY, LATE):
            x = mm(both[e][:, 384:].astype(BF16), spread_out).reshape(NZ, NG, 128)
            tail = tail + jnp.sum(jnp.where(l // 8 == e * NG + c, x, 0.0), axis=1, keepdims=True)
        st[...] = tail
        s1d[...] = jnp.concatenate([x[:, 256:384].reshape(NZ, NG, 128) for x in both], axis=1).astype(BF16)

    def push_rest():
        send_z(st, rt, 0, TAIL)
        send_z(s1d, r1d, 0, F1 + 1)

    def tail_of(e):
        c = lax.broadcasted_iota(jnp.int32, (NG, NZ, 128), 0)
        l = lax.broadcasted_iota(jnp.int32, (NG, NZ, 128), 2)
        x = jnp.broadcast_to(rt[...].reshape(1, NZ, 128), (NG, NZ, 128))
        return jnp.where(l // 8 == e * NG + c, x, 0.0).reshape(CH, 128).astype(BF16)

    def channels_apart_dense(h):
        if h == 0:
            x = mm(perm[...], r1[0, 0].reshape(256, HALF)).astype(BF16)
            dense0[...] = x
            x = mm(x, padded[:HALF, :HALF]).astype(BF16)
        else:
            x = mm(perm[...], r1d[...].reshape(256, 128)).astype(BF16)
            tails = jnp.concatenate([tail_of(EARLY), tail_of(LATE)], axis=0)
            x = mm(jnp.concatenate([dense0[...], x, tails], axis=1), padded[:, HALF:]).astype(BF16)
        for e in (EARLY, LATE):
            s2[0, e, h] = x[128 * e : 128 * e + 128].reshape(NG, NZ, HALF)

    def constants():
        for load in loads[3:]:
            load.wait()
        wgt[0], wgt[1] = wg_ref[0].T, wg_ref[1].T
        wot[0], wot[1] = wo_ref[0].T, wo_ref[1].T
        wabt[1] = wab_ref[1].T
        o, i = iota2((256, 256))
        perm[...] = one_hot(i == lax.rem(o, 16) * 16 + o // 16)
        i, l = iota2((224, 256))
        zi, n = lax.rem(i, NZ), i // NZ
        ci = jnp.where(n < 8, n // 4, (n - 8) // 3)
        ri = jnp.where(n < 8, lax.rem(n, 4), 4 + lax.rem(n - 8, 3))
        cols[...] = one_hot(l == zi // 4 * MS + lax.rem(zi, 4) * 14 + ci * 7 + ri)
        t = lax.broadcasted_iota(jnp.int32, (TOK, 1), 0)
        t = jnp.where(t < 384, t, 384 + lax.rem(t, 8))
        r = t // COLS
        spot = (r + odd * (1 - 2 * lax.rem(r, 2))) * MS + lax.rem(t, COLS)
        padded[...] = one_hot(lax.broadcasted_iota(jnp.int32, (TOK, TOK), 1) == spot)

    def channels_apart(u, h):
        x = mm(perm[...], r1[u, h].reshape(256, HALF)).astype(BF16)
        for e in (EARLY, LATE):
            s2[u, e, h] = x[128 * e : 128 * e + 128].reshape(NG, NZ, HALF)

    def send_early(u, t, a, slot):
        for d in FAR:
            h = lax.rem(g + d, NG)
            for yl_to in (yl, 1 - yl):
                send(
                    s2.at[u, EARLY, t, h], r2.at[u, EARLY, t, slot], u, F2 + t, dev(yl_to, z, a, h),
                    a == core if d == 0 and yl_to is yl else None,
                )

    def send_late(u, t, a, slot):
        for d in FAR:
            h = lax.rem(g + d, NG)
            send(
                s2.at[u, LATE, t, h], r2.at[u, LATE, t, slot], u, F2 + 2 + t, dev(a, z, core, h),
                a == yl if d == 0 else None,
            )

    def hand_over(u, t):
        own = r2.at[u, LATE, t, pl.ds(core * NG, NG)]
        wait_all(own, rsem.at[u, F2 + 2 + t])
        send(own, own, u, MATE + t, dev(yl, z, mate, g))

    def assemble(u, e, h, cs):
        n_src, n_g = (1, 8) if u == 0 else (2, 4)
        to = y0 if u == 0 else y1
        for s in range(n_src):
            for q in range(n_g // 2):
                for t in range(2):
                    at = slice(128 * t, 128 * t + 128)
                    slot, source = cs * NG + s * n_g + 2 * q, cs * n_src + s
                    even, other = r2[u, e, h, slot, :, at], r2[u, e, h, slot + 1, :, at]
                    r = 4 * h + 2 * t
                    row = (source * 4 + r if h == 0 else n_src * 8 + source * 3 + r - 4) * NZ
                    to_lanes = slice(128 * q, 128 * q + 128)
                    if not isinstance(cs, int):
                        row = pl.multiple_of(row, NZ)
                    to[e, pl.ds(row, NZ), to_lanes] = jnp.where(low, even, other)
                    if r + 1 < ROWS:
                        to[e, pl.ds(row + NZ, NZ), to_lanes] = pltpu.roll(jnp.where(low, other, even), 64, 1)

    def finish(u, h):
        x = r4[u, h].astype(F32).reshape(NZ, 2, NG, 128)
        tn = jnp.concatenate([normalize(x[:, t], (0, 1)).reshape(CH, 128) for t in range(2)], axis=1).astype(BF16)
        out = mm(wot[u], tn)
        zt[:, lanes(h)] = (zt[:, lanes(h)] + gate[:, lanes(h)] * out).astype(BF16).astype(F32)

    for u in range(2):
        a = yl if u == 0 else g // 4
        slot = core * NG + g if u == 0 else (core * 2 + yl) * 4 + lax.rem(g, 4)
        if u == 0:
            pl.semaphore_wait(barrier, NZ - 1 + 4 * NG - 1)
            push_dense()
            constants()
            push_rest()
            ztok[...] = jnp.zeros_like(ztok)
            for r in range(ROWS):
                ztok[slot_rows(r), :] = pair_ref[r].astype(F32)
            zt[...] = ztok[...].T
            norm(0)
            norm(1)
        gate[...] = sigmoid(mm(wgt[u], zn[...]))

        for h in range(2):
            if u == 0 and h == 1:
                wait_all(rt, rsem.at[u, TAIL])
                wait_all(r1d, rsem.at[u, F1 + 1])
            else:
                wait_all(r1.at[u, h], rsem.at[u, F1 + h])
            if u == 0:
                channels_apart_dense(h)
            else:
                channels_apart(u, h)
            send_early(u, h, a, slot)
            send_late(u, h, a, slot)

        hand_over(u, 0)
        wait_all(r2.at[u, EARLY, 0], rsem.at[u, F2])
        assemble(u, EARLY, 0, 0)
        assemble(u, EARLY, 0, 1)
        wait_all(r2.at[u, LATE, 0, pl.ds(0, NG)], rsem.at[u, MATE])
        assemble(u, LATE, 0, 0)
        assemble(u, LATE, 0, 1)
        if u == 0:
            part0[...] = mm(y0[EARLY, :128], cols[:128], 0, 0)
        else:
            e1[:, :256] = mm(cols[...], y1[EARLY, :256], 1, 1).astype(BF16)
            part1[...] = mm(e1[:, :256], y1[LATE, :256])
        wait_all(r2.at[u, EARLY, 1], rsem.at[u, F2 + 1])
        assemble(u, EARLY, 1, 0)
        assemble(u, EARLY, 1, 1)
        if u == 0:
            e0[...] = (part0[...] + mm(y0[EARLY, 128:], cols[128:], 0, 0)).astype(BF16)
        else:
            e1[:, 256:] = mm(cols[...], y1[EARLY, 256:], 1, 1).astype(BF16)

        i_half, j_half = (yl, core) if u == 0 else (core, yl)
        for h in range(2):
            n_r = 4 - h
            rows = slice(128 * h, 128 * h + 32 * n_r)
            if h == 1 - u:
                hand_over(u, 1)
                assemble(u, LATE, 1, core)
                wait_all(r2.at[u, LATE, 1, pl.ds(0, NG)], rsem.at[u, MATE + 1])
                assemble(u, LATE, 1, mate)
            if u == 0:
                tri = mm(y0[LATE, rows, :], e0[...]).astype(BF16)
            else:
                tri = (part1[rows, :] + mm(e1[rows, 256:], y1[LATE, 256:])).astype(BF16)
            for ci in range(2):
                for t in range(2):
                    for q in range(2):
                        at = slice(128 * q, 128 * q + 128)
                        base = (ci * n_r + 2 * t) * NZ
                        c0 = tri[base : base + NZ, at]
                        c1 = tri[base + NZ : base + 2 * NZ, at] if 2 * t + 1 < n_r else jnp.zeros_like(c0)
                        c1 = pltpu.roll(c1, 64, 1)
                        s3[u, h, ci * 4 + 2 * q, :, 128 * t : 128 * t + 128] = jnp.where(low, c0, c1)
                        s3[u, h, ci * 4 + 2 * q + 1, :, 128 * t : 128 * t + 128] = jnp.where(low, c1, c0)

            for d in (2, 1, 3, 0):
                q = lax.rem(g + d, 4)
                to = 4 * j_half + q
                for ci in (mate, core):
                    send(
                        s3.at[u, h, ci * 4 + q], r3.at[u, h, g], u, B1 + h, dev(i_half, z, ci, to),
                        (i_half == yl) & (to == g) if d == 0 and ci is core else None,
                    )

        for h in range(2):
            wait_all(r3.at[u, h], rsem.at[u, B1 + h])
            x = r3[u, h].reshape(NG * NZ, HALF)
            x = jnp.concatenate([x[:, :128], x[:, 128:]], axis=0)
            s4[u, h] = mm(perm[...], x).astype(BF16).reshape(NZ, 16, 128)
            send_z(s4.at[u, h], r4.at[u, h], u, B2 + h)
        for h in range(2):
            wait_all(r4.at[u, h], rsem.at[u, B2 + h])
            finish(u, h)
            if u == 0:
                norm(h)
                push(1, h)
            else:
                ztok[lanes(h), :] = zt[:, lanes(h)].T
                for r in range(4 * h, min(4 * h + 4, ROWS)):
                    out_ref[r] = ztok[slot_rows(r), :].astype(BF16)

    def wait_sent(u, stage, ref, count, less):
        @pl.when(less)
        def _():
            wait_all(ref.at[pl.ds(0, count - 1)], ssem.at[u, stage])

        @pl.when(jnp.logical_not(less))
        def _():
            wait_all(ref.at[pl.ds(0, count)], ssem.at[u, stage])

    for u in range(2):
        a = yl if u == 0 else g // 4
        for h in range(2):
            if u == 0 and h == 1:
                wait_all(st.at[pl.ds(0, NZ - 1)], ssem.at[u, TAIL])
                wait_all(s1d.at[pl.ds(0, NZ - 1)], ssem.at[u, F1 + 1])
            else:
                wait_all(s1.at[u, h, pl.ds(0, NZ - 1)], ssem.at[u, F1 + h])
        for h in range(2):
            wait_sent(u, F2 + h, r2.at[u, EARLY, h], 2 * NG, a == core)
            wait_sent(u, F2 + 2 + h, r2.at[u, LATE, h], NG, a == yl)
            wait_all(r2.at[u, LATE, h, pl.ds(0, NG)], ssem.at[u, MATE + h])
            wait_sent(u, B1 + h, s3.at[u, h], 8, g // 4 == core if u == 0 else (core == yl) & (g // 4 == yl))
            wait_all(s4.at[u, h, pl.ds(0, NZ - 1)], ssem.at[u, B2 + h])


def body(pair, pair_mask, w_ab, w_gate, w_out):
    return pl.pallas_call(
        kernel,
        out_shape=pltpu.VMEM(pair.shape, pair.dtype),
        in_specs=[pl.BlockSpec(memory_space=pltpu.HBM)] * 5,
        out_specs=pl.BlockSpec(memory_space=pltpu.VMEM),
        scratch_shapes=[
            pltpu.VMEM((ROWS, COLS, CH), BF16),
            pltpu.VMEM((ROWS, COLS), jnp.int32),
            pltpu.VMEM((2, CH, 4 * CH), BF16),
            pltpu.VMEM((2, CH, CH), BF16),
            pltpu.VMEM((2, CH, CH), BF16),
            pltpu.VMEM((2, 4 * CH, CH), BF16),
            pltpu.VMEM((2, CH, CH), BF16),
            pltpu.VMEM((2, CH, CH), BF16),
            pltpu.VMEM((256, 256), BF16),
            pltpu.VMEM((224, 256), BF16),
            pltpu.VMEM((TOK, TOK), BF16),
            pltpu.VMEM((NZ, 16, 128), BF16),
            pltpu.VMEM((NZ, 16, 128), BF16),
            pltpu.VMEM((NZ, 1, 128), F32),
            pltpu.VMEM((NZ, 1, 128), F32),
            pltpu.VMEM((256, 256), BF16),
            pltpu.VMEM((TOK, CH), F32),
            pltpu.VMEM((CH, TOK), F32),
            pltpu.VMEM((CH, TOK), BF16),
            pltpu.VMEM((CH, TOK), F32),
            pltpu.VMEM((2, 2, NZ, 16, HALF), BF16),
            pltpu.VMEM((2, 2, NZ, 16, HALF), BF16),
            pltpu.VMEM((2, 2, 2, NG, NZ, HALF), BF16),
            pltpu.VMEM((2, 2, 2, 16, NZ, HALF), BF16),
            pltpu.VMEM((2, 224, 512), BF16),
            pltpu.VMEM((2, 448, 256), BF16),
            pltpu.VMEM((512, 256), BF16),
            pltpu.VMEM((224, 448), BF16),
            pltpu.VMEM((512, 256), F32),
            pltpu.VMEM((224, 256), F32),
            pltpu.VMEM((2, 2, 8, NZ, HALF), BF16),
            pltpu.VMEM((2, 2, 8, NZ, HALF), BF16),
            pltpu.VMEM((2, 2, NZ, 16, 128), BF16),
            pltpu.VMEM((2, 2, NZ, 16, 128), BF16),
            pltpu.SemaphoreType.DMA((6,)),
            pltpu.SemaphoreType.DMA((2, STAGES)),
            pltpu.SemaphoreType.DMA((2, STAGES)),
        ],
        compiler_params=pltpu.CompilerParams(
            collective_id=0, has_side_effects=True, vmem_limit_bytes=32 * 1024 * 1024
        ),
        name="triangle",
    )(*(pltpu.with_memory_space_constraint(x, pltpu.HBM) for x in (pair, pair_mask, w_ab, w_gate, w_out)))


def solution(mesh):
    return jax.shard_map(
        body,
        mesh=mesh,
        in_specs=(P("row", "grp", None), P("row", "grp"), P(), P(), P()),
        out_specs=P("row", "grp", None),
        check_vma=False,
    )
```

```python
import jax
import jax.numpy as jnp
from jax import lax
from jax.experimental import pallas as pl
from jax.experimental.pallas import tpu as pltpu
from jax.sharding import PartitionSpec as P

MESH = pl.DeviceIdType.MESH
F32, BF16 = jnp.float32, jnp.bfloat16
NZ, NG, ROWS, COLS, RS, MS, CH = 16, 8, 7, 56, 8, 64, 128
TOK = RS * MS
HALF = TOK // 2
AROUND = (8, 7, 9, 6, 10, 5, 11, 4, 12, 3, 13, 2, 14, 1, 15)
FAR = (6, 5, 7, 2, 4, 1, 3, 0)
EARLY, LATE = 0, 1
F1, F2, MATE, B1, B2, TAIL, STAGES = 0, 2, 6, 8, 10, 12, 13


def mm(a, b, ca=1, cb=0):
    return lax.dot_general(a, b, (((ca,), (cb,)), ((), ())), preferred_element_type=F32)


def iota2(shape):
    return lax.broadcasted_iota(jnp.int32, shape, 0), lax.broadcasted_iota(jnp.int32, shape, 1)


def one_hot(hit):
    return jnp.where(hit, 1.0, 0.0).astype(BF16)


def normalize(x, axes):
    count = 1
    for a in axes:
        count *= x.shape[a]
    mean = jnp.sum(x, axis=axes, keepdims=True) * (1.0 / count)
    cen = x - mean
    var = jnp.sum(cen * cen, axis=axes, keepdims=True) * (1.0 / count)
    return cen * lax.rsqrt(var + 1e-05)


def sigmoid(x):
    return 0.5 * jnp.tanh(0.5 * x) + 0.5


def kernel(
    pair_hbm, mask_hbm, wab_hbm, wg_hbm, wo_hbm, out_ref,
    pair_ref, mask_ref, wab_ref, wg_ref, wo_ref, wabt, wgt, wot, perm, cols, padded, s1d, r1d, st, rt, dense0,
    ztok, zt, zn, gate, s1, r1, s2, r2, y0, y1, e0, e1, part0, part1, s3, r3, s4, r4, insem, ssem, rsem,
):
    loads = [
        pltpu.make_async_copy(src, dst, insem.at[n])
        for n, (src, dst) in enumerate(
            (
                (pair_hbm, pair_ref), (wab_hbm.at[0], wab_ref.at[0]), (mask_hbm, mask_ref), (wab_hbm.at[1], wab_ref.at[1]),
                (wg_hbm, wg_ref), (wo_hbm, wo_ref),
            )
        )
    ]
    for load in loads:
        load.start()

    row, g = lax.axis_index("row"), lax.axis_index("grp")
    core = lax.rem(row, 2)
    z = lax.rem(row // 2, NZ)
    yl = row // (2 * NZ)

    mate = 1 - core
    odd = lax.rem(g, 2)

    def dev(yl_, z_, core_, g_):
        return (yl_ * (2 * NZ) + z_ * 2 + core_, g_)

    barrier = pltpu.get_barrier_semaphore()

    def greet(device):
        pl.semaphore_signal(barrier, inc=1, device_id=device, device_id_type=MESH)

    for d in AROUND:
        greet(dev(yl, lax.rem(z + d, NZ), core, g))
    for d in FAR:
        for yl_to in (yl, 1 - yl):
            for core_to in (core, mate):
                if d or yl_to is not yl or core_to is not core:
                    greet(dev(yl_to, z, core_to, lax.rem(g + d, NG)))

    def send(src, dst, u, stage, device, is_self=None):
        def remote():
            pltpu.make_async_remote_copy(
                src_ref=src, dst_ref=dst, send_sem=ssem.at[u, stage], recv_sem=rsem.at[u, stage],
                device_id=device, device_id_type=MESH,
            ).start()

        if is_self is None:
            remote()
            return

        @pl.when(is_self)
        def _():
            pltpu.make_async_copy(src, dst, rsem.at[u, stage]).start()

        pl.when(jnp.logical_not(is_self))(remote)

    def send_z(src, dst, u, stage):
        for d in AROUND:
            to = lax.rem(z + d, NZ)
            send(src.at[to], dst.at[z], u, stage, dev(yl, to, core, g))
        pltpu.make_async_copy(src.at[z], dst.at[z], rsem.at[u, stage]).start()

    def wait_all(ref, sem):
        pltpu.make_async_copy(ref, ref, sem).wait()

    def slot_rows(r):
        return pl.ds(pl.multiple_of((r + odd * (1 - 2 * (r % 2))) * MS, MS), COLS)

    low = lax.broadcasted_iota(jnp.int32, (NZ, 128), 1) < 64
    ztok[...] = jnp.zeros_like(ztok)

    k, l = iota2((COLS, TOK))
    places = one_hot(lax.rem(l, MS) == k)
    k, l = iota2((ROWS, TOK))
    loads[2].wait()
    spread = mm(mask_ref[...].astype(F32).astype(BF16), places)
    keep = jnp.sum(jnp.where(l // MS == k + odd * (1 - 2 * lax.rem(k, 2)), spread, 0.0), axis=0, keepdims=True)
    kc, lc = iota2((COLS, TOK))
    spread = mm(mask_ref[...].astype(F32).astype(BF16), one_hot(lax.rem(lc, COLS) == kc))
    keep_dense = jnp.sum(jnp.where(l // COLS == k, spread, 0.0), axis=0, keepdims=True)

    loads[1].wait()
    wabt[0] = wab_ref[0].T
    loads[0].wait()
    for r in range(ROWS):
        ztok[r * COLS : r * COLS + COLS, :] = pair_ref[r].astype(F32)
    zn[...] = normalize(ztok[...].T, (0,)).astype(BF16)

    def lanes(h):
        return slice(HALF * h, HALF * h + HALF)

    def norm(h):
        zn[:, lanes(h)] = normalize(zt[:, lanes(h)], (0,)).astype(BF16)

    def push(u, h):
        def side(base):
            p = mm(wabt[u, base : base + 2 * CH, :], zn[:, lanes(h)])
            return (sigmoid(p[:CH]) * p[CH:] * keep[:, lanes(h)]).reshape(NZ, NG, HALF)

        left, right = side(0), side(2 * CH)
        s1[u, h] = jnp.concatenate([right, left] if u == 0 else [left, right], axis=1).astype(BF16)
        send_z(s1.at[u, h], r1.at[u, h], u, F1 + h)

    def push_dense():
        def side(base, h):
            p = mm(wabt[0, base : base + 2 * CH, :], zn[:, lanes(h)])
            return sigmoid(p[:CH]) * p[CH:] * keep_dense[:, lanes(h)]

        both = side(2 * CH, 0), side(0, 0)
        s1[0, 0] = jnp.concatenate([x.reshape(NZ, NG, 256) for x in both], axis=1).astype(BF16)
        send_z(s1.at[0, 0], r1.at[0, 0], 0, F1)
        both = side(2 * CH, 1), side(0, 1)
        k, l = iota2((128, 128))
        spread_out = one_hot((k < 8) & (lax.rem(l, 8) == k))
        c = lax.broadcasted_iota(jnp.int32, (NZ, NG, 128), 1)
        l = lax.broadcasted_iota(jnp.int32, (NZ, NG, 128), 2)
        tail = jnp.zeros((NZ, 1, 128), F32)
        for e in (EARLY, LATE):
            x = mm(both[e][:, 128:].astype(BF16), spread_out).reshape(NZ, NG, 128)
            tail = tail + jnp.sum(jnp.where(l // 8 == e * NG + c, x, 0.0), axis=1, keepdims=True)
        st[...] = tail
        s1d[...] = jnp.concatenate([x[:, :128].reshape(NZ, NG, 128) for x in both], axis=1).astype(BF16)

    def push_rest():
        send_z(st, rt, 0, TAIL)
        send_z(s1d, r1d, 0, F1 + 1)

    def tail_of(e):
        c = lax.broadcasted_iota(jnp.int32, (NG, NZ, 128), 0)
        l = lax.broadcasted_iota(jnp.int32, (NG, NZ, 128), 2)
        x = jnp.broadcast_to(rt[...].reshape(1, NZ, 128), (NG, NZ, 128))
        return jnp.where(l // 8 == e * NG + c, x, 0.0).reshape(CH, 128).astype(BF16)

    def channels_apart_dense(h):
        if h == 0:
            x = mm(perm[...], r1[0, 0].reshape(256, HALF)).astype(BF16)
            dense0[...] = x
            x = mm(x, padded[:HALF, :HALF]).astype(BF16)
        else:
            x = mm(perm[...], r1d[...].reshape(256, 128)).astype(BF16)
            tails = jnp.concatenate([tail_of(EARLY), tail_of(LATE)], axis=0)
            x = mm(jnp.concatenate([dense0[...], x, tails], axis=1), padded[:, HALF:]).astype(BF16)
        for e in (EARLY, LATE):
            s2[0, e, h] = x[128 * e : 128 * e + 128].reshape(NG, NZ, HALF)

    def constants():
        for load in loads[3:]:
            load.wait()
        wgt[0], wgt[1] = wg_ref[0].T, wg_ref[1].T
        wot[0], wot[1] = wo_ref[0].T, wo_ref[1].T
        wabt[1] = wab_ref[1].T
        o, i = iota2((256, 256))
        perm[...] = one_hot(i == lax.rem(o, 16) * 16 + o // 16)
        i, l = iota2((224, 256))
        zi, n = lax.rem(i, NZ), i // NZ
        ci = jnp.where(n < 8, n // 4, (n - 8) // 3)
        ri = jnp.where(n < 8, lax.rem(n, 4), 4 + lax.rem(n - 8, 3))
        cols[...] = one_hot(l == zi // 4 * MS + lax.rem(zi, 4) * 14 + ci * 7 + ri)
        t = lax.broadcasted_iota(jnp.int32, (TOK, 1), 0)
        t = jnp.where(t < 384, t, 384 + lax.rem(t, 8))
        r = t // COLS
        spot = (r + odd * (1 - 2 * lax.rem(r, 2))) * MS + lax.rem(t, COLS)
        padded[...] = one_hot(lax.broadcasted_iota(jnp.int32, (TOK, TOK), 1) == spot)

    def channels_apart(u, h):
        x = mm(perm[...], r1[u, h].reshape(256, HALF)).astype(BF16)
        for e in (EARLY, LATE):
            s2[u, e, h] = x[128 * e : 128 * e + 128].reshape(NG, NZ, HALF)

    def send_early(u, t, a, slot):
        for d in FAR:
            h = lax.rem(g + d, NG)
            for yl_to in (yl, 1 - yl):
                send(
                    s2.at[u, EARLY, t, h], r2.at[u, EARLY, t, slot], u, F2 + t, dev(yl_to, z, a, h),
                    a == core if d == 0 and yl_to is yl else None,
                )

    def send_late(u, t, a, slot):
        for d in FAR:
            h = lax.rem(g + d, NG)
            send(
                s2.at[u, LATE, t, h], r2.at[u, LATE, t, slot], u, F2 + 2 + t, dev(a, z, core, h),
                a == yl if d == 0 else None,
            )

    def hand_over(u, t):
        own = r2.at[u, LATE, t, pl.ds(core * NG, NG)]
        wait_all(own, rsem.at[u, F2 + 2 + t])
        send(own, own, u, MATE + t, dev(yl, z, mate, g))

    def assemble(u, e, h, cs):
        n_src, n_g = (1, 8) if u == 0 else (2, 4)
        to = y0 if u == 0 else y1
        for s in range(n_src):
            for q in range(n_g // 2):
                for t in range(2):
                    at = slice(128 * t, 128 * t + 128)
                    slot, source = cs * NG + s * n_g + 2 * q, cs * n_src + s
                    even, other = r2[u, e, h, slot, :, at], r2[u, e, h, slot + 1, :, at]
                    r = 4 * h + 2 * t
                    row = (source * 4 + r if h == 0 else n_src * 8 + source * 3 + r - 4) * NZ
                    to_lanes = slice(128 * q, 128 * q + 128)
                    if not isinstance(cs, int):
                        row = pl.multiple_of(row, NZ)
                    to[e, pl.ds(row, NZ), to_lanes] = jnp.where(low, even, other)
                    if r + 1 < ROWS:
                        to[e, pl.ds(row + NZ, NZ), to_lanes] = pltpu.roll(jnp.where(low, other, even), 64, 1)

    def finish(u, h):
        x = r4[u, h].astype(F32).reshape(NZ, 2, NG, 128)
        tn = jnp.concatenate([normalize(x[:, t], (0, 1)).reshape(CH, 128) for t in range(2)], axis=1).astype(BF16)
        out = mm(wot[u], tn)
        zt[:, lanes(h)] = (zt[:, lanes(h)] + gate[:, lanes(h)] * out).astype(BF16).astype(F32)

    for u in range(2):
        a = yl if u == 0 else g // 4
        slot = core * NG + g if u == 0 else (core * 2 + yl) * 4 + lax.rem(g, 4)
        if u == 0:
            pl.semaphore_wait(barrier, NZ - 1 + 4 * NG - 1)
            push_dense()
            constants()
            push_rest()

        for h in range(2):
            if u == 0 and h == 1:
                wait_all(rt, rsem.at[u, TAIL])
                wait_all(r1d, rsem.at[u, F1 + 1])
            else:
                wait_all(r1.at[u, h], rsem.at[u, F1 + h])
            if u == 0:
                channels_apart_dense(h)
            else:
                channels_apart(u, h)
            send_early(u, h, a, slot)
            send_late(u, h, a, slot)
            if h == 0:
                if u == 0:
                    ztok[...] = jnp.zeros_like(ztok)
                    for r in range(ROWS):
                        ztok[slot_rows(r), :] = pair_ref[r].astype(F32)
                    zt[...] = ztok[...].T
                    norm(0)
                    norm(1)
                gate[...] = sigmoid(mm(wgt[u], zn[...]))

        hand_over(u, 0)
        wait_all(r2.at[u, EARLY, 0], rsem.at[u, F2])
        assemble(u, EARLY, 0, 0)
        assemble(u, EARLY, 0, 1)
        wait_all(r2.at[u, LATE, 0, pl.ds(0, NG)], rsem.at[u, MATE])
        assemble(u, LATE, 0, 0)
        assemble(u, LATE, 0, 1)
        if u == 0:
            part0[...] = mm(y0[EARLY, :128], cols[:128], 0, 0)
        else:
            e1[:, :256] = mm(cols[...], y1[EARLY, :256], 1, 1).astype(BF16)
            part1[...] = mm(e1[:, :256], y1[LATE, :256])
        wait_all(r2.at[u, EARLY, 1], rsem.at[u, F2 + 1])
        assemble(u, EARLY, 1, 0)
        assemble(u, EARLY, 1, 1)
        if u == 0:
            e0[...] = (part0[...] + mm(y0[EARLY, 128:], cols[128:], 0, 0)).astype(BF16)
        else:
            e1[:, 256:] = mm(cols[...], y1[EARLY, 256:], 1, 1).astype(BF16)

        i_half, j_half = (yl, core) if u == 0 else (core, yl)
        for h in range(2):
            n_r = 4 - h
            rows = slice(128 * h, 128 * h + 32 * n_r)
            if h == 1 - u:
                hand_over(u, 1)
                assemble(u, LATE, 1, core)
                wait_all(r2.at[u, LATE, 1, pl.ds(0, NG)], rsem.at[u, MATE + 1])
                assemble(u, LATE, 1, mate)
            if u == 0:
                tri = mm(y0[LATE, rows, :], e0[...]).astype(BF16)
            else:
                tri = (part1[rows, :] + mm(e1[rows, 256:], y1[LATE, 256:])).astype(BF16)
            for ci in range(2):
                for t in range(2):
                    for q in range(2):
                        at = slice(128 * q, 128 * q + 128)
                        base = (ci * n_r + 2 * t) * NZ
                        c0 = tri[base : base + NZ, at]
                        c1 = tri[base + NZ : base + 2 * NZ, at] if 2 * t + 1 < n_r else jnp.zeros_like(c0)
                        c1 = pltpu.roll(c1, 64, 1)
                        s3[u, h, ci * 4 + 2 * q, :, 128 * t : 128 * t + 128] = jnp.where(low, c0, c1)
                        s3[u, h, ci * 4 + 2 * q + 1, :, 128 * t : 128 * t + 128] = jnp.where(low, c1, c0)

            for d in (2, 1, 3, 0):
                q = lax.rem(g + d, 4)
                to = 4 * j_half + q
                for ci in (mate, core):
                    send(
                        s3.at[u, h, ci * 4 + q], r3.at[u, h, g], u, B1 + h, dev(i_half, z, ci, to),
                        (i_half == yl) & (to == g) if d == 0 and ci is core else None,
                    )

        for h in range(2):
            wait_all(r3.at[u, h], rsem.at[u, B1 + h])
            x = r3[u, h].reshape(NG * NZ, HALF)
            x = jnp.concatenate([x[:, :128], x[:, 128:]], axis=0)
            s4[u, h] = mm(perm[...], x).astype(BF16).reshape(NZ, 16, 128)
            send_z(s4.at[u, h], r4.at[u, h], u, B2 + h)
        for h in range(2):
            wait_all(r4.at[u, h], rsem.at[u, B2 + h])
            finish(u, h)
            if u == 0:
                norm(h)
                push(1, h)
            else:
                ztok[lanes(h), :] = zt[:, lanes(h)].T
                for r in range(4 * h, min(4 * h + 4, ROWS)):
                    out_ref[r] = ztok[slot_rows(r), :].astype(BF16)

    def wait_sent(u, stage, ref, count, less):
        @pl.when(less)
        def _():
            wait_all(ref.at[pl.ds(0, count - 1)], ssem.at[u, stage])

        @pl.when(jnp.logical_not(less))
        def _():
            wait_all(ref.at[pl.ds(0, count)], ssem.at[u, stage])

    for u in range(2):
        a = yl if u == 0 else g // 4
        for h in range(2):
            if u == 0 and h == 1:
                wait_all(st.at[pl.ds(0, NZ - 1)], ssem.at[u, TAIL])
                wait_all(s1d.at[pl.ds(0, NZ - 1)], ssem.at[u, F1 + 1])
            else:
                wait_all(s1.at[u, h, pl.ds(0, NZ - 1)], ssem.at[u, F1 + h])
        for h in range(2):
            wait_sent(u, F2 + h, r2.at[u, EARLY, h], 2 * NG, a == core)
            wait_sent(u, F2 + 2 + h, r2.at[u, LATE, h], NG, a == yl)
            wait_all(r2.at[u, LATE, h, pl.ds(0, NG)], ssem.at[u, MATE + h])
            wait_sent(u, B1 + h, s3.at[u, h], 8, g // 4 == core if u == 0 else (core == yl) & (g // 4 == yl))
            wait_all(s4.at[u, h, pl.ds(0, NZ - 1)], ssem.at[u, B2 + h])


def body(pair, pair_mask, w_ab, w_gate, w_out):
    return pl.pallas_call(
        kernel,
        out_shape=pltpu.VMEM(pair.shape, pair.dtype),
        in_specs=[pl.BlockSpec(memory_space=pltpu.HBM)] * 5,
        out_specs=pl.BlockSpec(memory_space=pltpu.VMEM),
        scratch_shapes=[
            pltpu.VMEM((ROWS, COLS, CH), BF16),
            pltpu.VMEM((ROWS, COLS), jnp.int32),
            pltpu.VMEM((2, CH, 4 * CH), BF16),
            pltpu.VMEM((2, CH, CH), BF16),
            pltpu.VMEM((2, CH, CH), BF16),
            pltpu.VMEM((2, 4 * CH, CH), BF16),
            pltpu.VMEM((2, CH, CH), BF16),
            pltpu.VMEM((2, CH, CH), BF16),
            pltpu.VMEM((256, 256), BF16),
            pltpu.VMEM((224, 256), BF16),
            pltpu.VMEM((TOK, TOK), BF16),
            pltpu.VMEM((NZ, 16, 128), BF16),
            pltpu.VMEM((NZ, 16, 128), BF16),
            pltpu.VMEM((NZ, 1, 128), F32),
            pltpu.VMEM((NZ, 1, 128), F32),
            pltpu.VMEM((256, 256), BF16),
            pltpu.VMEM((TOK, CH), F32),
            pltpu.VMEM((CH, TOK), F32),
            pltpu.VMEM((CH, TOK), BF16),
            pltpu.VMEM((CH, TOK), F32),
            pltpu.VMEM((2, 2, NZ, 16, HALF), BF16),
            pltpu.VMEM((2, 2, NZ, 16, HALF), BF16),
            pltpu.VMEM((2, 2, 2, NG, NZ, HALF), BF16),
            pltpu.VMEM((2, 2, 2, 16, NZ, HALF), BF16),
            pltpu.VMEM((2, 224, 512), BF16),
            pltpu.VMEM((2, 448, 256), BF16),
            pltpu.VMEM((512, 256), BF16),
            pltpu.VMEM((224, 448), BF16),
            pltpu.VMEM((512, 256), F32),
            pltpu.VMEM((224, 256), F32),
            pltpu.VMEM((2, 2, 8, NZ, HALF), BF16),
            pltpu.VMEM((2, 2, 8, NZ, HALF), BF16),
            pltpu.VMEM((2, 2, NZ, 16, 128), BF16),
            pltpu.VMEM((2, 2, NZ, 16, 128), BF16),
            pltpu.SemaphoreType.DMA((6,)),
            pltpu.SemaphoreType.DMA((2, STAGES)),
            pltpu.SemaphoreType.DMA((2, STAGES)),
        ],
        compiler_params=pltpu.CompilerParams(
            collective_id=0, has_side_effects=True, vmem_limit_bytes=32 * 1024 * 1024
        ),
        name="triangle",
    )(*(pltpu.with_memory_space_constraint(x, pltpu.HBM) for x in (pair, pair_mask, w_ab, w_gate, w_out)))


def solution(mesh):
    return jax.shard_map(
        body,
        mesh=mesh,
        in_specs=(P("row", "grp", None), P("row", "grp"), P(), P(), P()),
        out_specs=P("row", "grp", None),
        check_vma=False,
    )
```

```python
import jax
import jax.numpy as jnp
from jax import lax
from jax.experimental import pallas as pl
from jax.experimental.pallas import tpu as pltpu
from jax.sharding import PartitionSpec as P

MESH = pl.DeviceIdType.MESH
F32, BF16 = jnp.float32, jnp.bfloat16
NZ, NG, ROWS, COLS, RS, MS, CH = 16, 8, 7, 56, 8, 64, 128
TOK = RS * MS
HALF = TOK // 2
AROUND = (8, 7, 9, 6, 10, 5, 11, 4, 12, 3, 13, 2, 14, 1, 15)
FAR = (6, 5, 7, 2, 4, 1, 3, 0)
EARLY, LATE = 0, 1
F1, F2, MATE, B1, B2, TAIL, STAGES = 0, 2, 6, 8, 10, 12, 13


def mm(a, b, ca=1, cb=0):
    return lax.dot_general(a, b, (((ca,), (cb,)), ((), ())), preferred_element_type=F32)


def iota2(shape):
    return lax.broadcasted_iota(jnp.int32, shape, 0), lax.broadcasted_iota(jnp.int32, shape, 1)


def one_hot(hit):
    return jnp.where(hit, 1.0, 0.0).astype(BF16)


def normalize(x, axes):
    count = 1
    for a in axes:
        count *= x.shape[a]
    mean = jnp.sum(x, axis=axes, keepdims=True) * (1.0 / count)
    cen = x - mean
    var = jnp.sum(cen * cen, axis=axes, keepdims=True) * (1.0 / count)
    return cen * lax.rsqrt(var + 1e-05)


def sigmoid(x):
    return 0.5 * jnp.tanh(0.5 * x) + 0.5


def kernel(
    pair_hbm, mask_hbm, wab_hbm, wg_hbm, wo_hbm, out_ref,
    pair_ref, mask_ref, wab_ref, wg_ref, wo_ref, wabt, wgt, wot, perm, cols, padded, s1d, r1d, st, rt, dense0,
    ztok, zt, zn, gate, s1, r1, s2, r2, y0, y1, e0, e1, part0, part1, s3, r3, s4, r4, insem, ssem, rsem,
):
    loads = [
        pltpu.make_async_copy(src, dst, insem.at[n])
        for n, (src, dst) in enumerate(
            (
                (pair_hbm, pair_ref), (wab_hbm.at[0], wab_ref.at[0]), (mask_hbm, mask_ref), (wab_hbm.at[1], wab_ref.at[1]),
                (wg_hbm, wg_ref), (wo_hbm, wo_ref),
            )
        )
    ]
    for load in loads:
        load.start()

    row, g = lax.axis_index("row"), lax.axis_index("grp")
    core = lax.rem(row, 2)
    z = lax.rem(row // 2, NZ)
    yl = row // (2 * NZ)

    mate = 1 - core
    odd = lax.rem(g, 2)

    def dev(yl_, z_, core_, g_):
        return (yl_ * (2 * NZ) + z_ * 2 + core_, g_)

    barrier = pltpu.get_barrier_semaphore()

    def greet(device):
        pl.semaphore_signal(barrier, inc=1, device_id=device, device_id_type=MESH)

    for d in AROUND:
        greet(dev(yl, lax.rem(z + d, NZ), core, g))
    for d in FAR:
        for yl_to in (yl, 1 - yl):
            for core_to in (core, mate):
                if d or yl_to is not yl or core_to is not core:
                    greet(dev(yl_to, z, core_to, lax.rem(g + d, NG)))

    def send(src, dst, u, stage, device, is_self=None):
        def remote():
            pltpu.make_async_remote_copy(
                src_ref=src, dst_ref=dst, send_sem=ssem.at[u, stage], recv_sem=rsem.at[u, stage],
                device_id=device, device_id_type=MESH,
            ).start()

        if is_self is None:
            remote()
            return

        @pl.when(is_self)
        def _():
            pltpu.make_async_copy(src, dst, rsem.at[u, stage]).start()

        pl.when(jnp.logical_not(is_self))(remote)

    def send_z(src, dst, u, stage):
        for d in AROUND:
            to = lax.rem(z + d, NZ)
            send(src.at[to], dst.at[z], u, stage, dev(yl, to, core, g))
        pltpu.make_async_copy(src.at[z], dst.at[z], rsem.at[u, stage]).start()

    def wait_all(ref, sem):
        pltpu.make_async_copy(ref, ref, sem).wait()

    def slot_rows(r):
        return pl.ds(pl.multiple_of((r + odd * (1 - 2 * (r % 2))) * MS, MS), COLS)

    low = lax.broadcasted_iota(jnp.int32, (NZ, 128), 1) < 64
    ztok[...] = jnp.zeros_like(ztok)

    k, l = iota2((COLS, TOK))
    places = one_hot(lax.rem(l, MS) == k)
    k, l = iota2((ROWS, TOK))
    loads[2].wait()
    spread = mm(mask_ref[...].astype(F32).astype(BF16), places)
    keep = jnp.sum(jnp.where(l // MS == k + odd * (1 - 2 * lax.rem(k, 2)), spread, 0.0), axis=0, keepdims=True)
    kc, lc = iota2((COLS, TOK))
    spread = mm(mask_ref[...].astype(F32).astype(BF16), one_hot(lax.rem(lc, COLS) == kc))
    keep_dense = jnp.sum(jnp.where(l // COLS == k, spread, 0.0), axis=0, keepdims=True)

    loads[1].wait()
    wabt[0] = wab_ref[0].T
    loads[0].wait()
    for r in range(ROWS):
        ztok[r * COLS : r * COLS + COLS, :] = pair_ref[r].astype(F32)
    zn[...] = normalize(ztok[...].T, (0,)).astype(BF16)

    def lanes(h):
        return slice(HALF * h, HALF * h + HALF)

    def norm(h):
        zn[:, lanes(h)] = normalize(zt[:, lanes(h)], (0,)).astype(BF16)

    def push(u, h):
        def side(base):
            p = mm(wabt[u, base : base + 2 * CH, :], zn[:, lanes(h)])
            return (sigmoid(p[:CH]) * p[CH:] * keep[:, lanes(h)]).reshape(NZ, NG, HALF)

        left, right = side(0), side(2 * CH)
        s1[u, h] = jnp.concatenate([right, left] if u == 0 else [left, right], axis=1).astype(BF16)
        send_z(s1.at[u, h], r1.at[u, h], u, F1 + h)

    def push_dense():
        def side(base):
            p = mm(wabt[0, base : base + 2 * CH, :], zn[...])
            return sigmoid(p[:CH]) * p[CH:] * keep_dense

        both = side(2 * CH), side(0)
        s1[0, 0] = jnp.concatenate([x[:, :256].reshape(NZ, NG, 256) for x in both], axis=1).astype(BF16)
        send_z(s1.at[0, 0], r1.at[0, 0], 0, F1)
        k, l = iota2((128, 128))
        spread_out = one_hot((k < 8) & (lax.rem(l, 8) == k))
        c = lax.broadcasted_iota(jnp.int32, (NZ, NG, 128), 1)
        l = lax.broadcasted_iota(jnp.int32, (NZ, NG, 128), 2)
        tail = jnp.zeros((NZ, 1, 128), F32)
        for e in (EARLY, LATE):
            x = mm(both[e][:, 384:].astype(BF16), spread_out).reshape(NZ, NG, 128)
            tail = tail + jnp.sum(jnp.where(l // 8 == e * NG + c, x, 0.0), axis=1, keepdims=True)
        st[...] = tail
        s1d[...] = jnp.concatenate([x[:, 256:384].reshape(NZ, NG, 128) for x in both], axis=1).astype(BF16)

    def push_rest():
        send_z(st, rt, 0, TAIL)
        send_z(s1d, r1d, 0, F1 + 1)

    def tail_of(e):
        c = lax.broadcasted_iota(jnp.int32, (NG, NZ, 128), 0)
        l = lax.broadcasted_iota(jnp.int32, (NG, NZ, 128), 2)
        x = jnp.broadcast_to(rt[...].reshape(1, NZ, 128), (NG, NZ, 128))
        return jnp.where(l // 8 == e * NG + c, x, 0.0).reshape(CH, 128).astype(BF16)

    def channels_apart_dense(h):
        if h == 0:
            x = mm(perm[...], r1[0, 0].reshape(256, HALF)).astype(BF16)
            dense0[...] = x
            x = mm(x, padded[:HALF, :HALF]).astype(BF16)
        else:
            x = mm(perm[...], r1d[...].reshape(256, 128)).astype(BF16)
            tails = jnp.concatenate([tail_of(EARLY), tail_of(LATE)], axis=0)
            x = mm(jnp.concatenate([dense0[...], x, tails], axis=1), padded[:, HALF:]).astype(BF16)
        for e in (EARLY, LATE):
            s2[0, e, h] = x[128 * e : 128 * e + 128].reshape(NG, NZ, HALF)

    def constants():
        for load in loads[3:]:
            load.wait()
        wgt[0], wgt[1] = wg_ref[0].T, wg_ref[1].T
        wot[0], wot[1] = wo_ref[0].T, wo_ref[1].T
        wabt[1] = wab_ref[1].T
        o, i = iota2((256, 256))
        perm[...] = one_hot(i == lax.rem(o, 16) * 16 + o // 16)
        i, l = iota2((224, 256))
        zi, n = lax.rem(i, NZ), i // NZ
        ci = jnp.where(n < 8, n // 4, (n - 8) // 3)
        ri = jnp.where(n < 8, lax.rem(n, 4), 4 + lax.rem(n - 8, 3))
        cols[...] = one_hot(l == zi // 4 * MS + lax.rem(zi, 4) * 14 + ci * 7 + ri)
        t = lax.broadcasted_iota(jnp.int32, (TOK, 1), 0)
        t = jnp.where(t < 384, t, 384 + lax.rem(t, 8))
        r = t // COLS
        spot = (r + odd * (1 - 2 * lax.rem(r, 2))) * MS + lax.rem(t, COLS)
        padded[...] = one_hot(lax.broadcasted_iota(jnp.int32, (TOK, TOK), 1) == spot)

    def channels_apart(u, h):
        x = mm(perm[...], r1[u, h].reshape(256, HALF)).astype(BF16)
        for e in (EARLY, LATE):
            s2[u, e, h] = x[128 * e : 128 * e + 128].reshape(NG, NZ, HALF)

    def send_early(u, t, a, slot):
        for d in FAR:
            h = lax.rem(g + d, NG)
            for yl_to in (yl, 1 - yl):
                send(
                    s2.at[u, EARLY, t, h], r2.at[u, EARLY, t, slot], u, F2 + t, dev(yl_to, z, a, h),
                    a == core if d == 0 and yl_to is yl else None,
                )

    def send_late(u, t, a, slot):
        for d in FAR:
            h = lax.rem(g + d, NG)
            send(
                s2.at[u, LATE, t, h], r2.at[u, LATE, t, slot], u, F2 + 2 + t, dev(a, z, core, h),
                a == yl if d == 0 else None,
            )

    def hand_over(u, t):
        own = r2.at[u, LATE, t, pl.ds(core * NG, NG)]
        wait_all(own, rsem.at[u, F2 + 2 + t])
        send(own, own, u, MATE + t, dev(yl, z, mate, g))

    def assemble(u, e, h, cs):
        n_src, n_g = (1, 8) if u == 0 else (2, 4)
        to = y0 if u == 0 else y1
        for s in range(n_src):
            for q in range(n_g // 2):
                for t in range(2):
                    at = slice(128 * t, 128 * t + 128)
                    slot, source = cs * NG + s * n_g + 2 * q, cs * n_src + s
                    even, other = r2[u, e, h, slot, :, at], r2[u, e, h, slot + 1, :, at]
                    r = 4 * h + 2 * t
                    row = (source * 4 + r if h == 0 else n_src * 8 + source * 3 + r - 4) * NZ
                    to_lanes = slice(128 * q, 128 * q + 128)
                    if not isinstance(cs, int):
                        row = pl.multiple_of(row, NZ)
                    to[e, pl.ds(row, NZ), to_lanes] = jnp.where(low, even, other)
                    if r + 1 < ROWS:
                        to[e, pl.ds(row + NZ, NZ), to_lanes] = pltpu.roll(jnp.where(low, other, even), 64, 1)

    def finish(u, h):
        x = r4[u, h].astype(F32).reshape(NZ, 2, NG, 128)
        tn = jnp.concatenate([normalize(x[:, t], (0, 1)).reshape(CH, 128) for t in range(2)], axis=1).astype(BF16)
        out = mm(wot[u], tn)
        zt[:, lanes(h)] = (zt[:, lanes(h)] + gate[:, lanes(h)] * out).astype(BF16).astype(F32)

    for u in range(2):
        a = yl if u == 0 else g // 4
        slot = core * NG + g if u == 0 else (core * 2 + yl) * 4 + lax.rem(g, 4)
        if u == 0:
            pl.semaphore_wait(barrier, NZ - 1 + 4 * NG - 1)
            push_dense()
            push_rest()
            constants()
            ztok[...] = jnp.zeros_like(ztok)
            for r in range(ROWS):
                ztok[slot_rows(r), :] = pair_ref[r].astype(F32)
            zt[...] = ztok[...].T
            norm(0)
            norm(1)
        gate[...] = sigmoid(mm(wgt[u], zn[...]))

        for h in range(2):
            if u == 0 and h == 1:
                wait_all(rt, rsem.at[u, TAIL])
                wait_all(r1d, rsem.at[u, F1 + 1])
            else:
                wait_all(r1.at[u, h], rsem.at[u, F1 + h])
            if u == 0:
                channels_apart_dense(h)
            else:
                channels_apart(u, h)
            send_early(u, h, a, slot)
            send_late(u, h, a, slot)

        hand_over(u, 0)
        wait_all(r2.at[u, EARLY, 0], rsem.at[u, F2])
        assemble(u, EARLY, 0, 0)
        assemble(u, EARLY, 0, 1)
        wait_all(r2.at[u, LATE, 0, pl.ds(0, NG)], rsem.at[u, MATE])
        assemble(u, LATE, 0, 0)
        assemble(u, LATE, 0, 1)
        if u == 0:
            part0[...] = mm(y0[EARLY, :128], cols[:128], 0, 0)
        else:
            e1[:, :256] = mm(cols[...], y1[EARLY, :256], 1, 1).astype(BF16)
            part1[...] = mm(e1[:, :256], y1[LATE, :256])
        wait_all(r2.at[u, EARLY, 1], rsem.at[u, F2 + 1])
        assemble(u, EARLY, 1, 0)
        assemble(u, EARLY, 1, 1)
        if u == 0:
            e0[...] = (part0[...] + mm(y0[EARLY, 128:], cols[128:], 0, 0)).astype(BF16)
        else:
            e1[:, 256:] = mm(cols[...], y1[EARLY, 256:], 1, 1).astype(BF16)

        i_half, j_half = (yl, core) if u == 0 else (core, yl)
        for h in range(2):
            n_r = 4 - h
            rows = slice(128 * h, 128 * h + 32 * n_r)
            if h == 1 - u:
                hand_over(u, 1)
                assemble(u, LATE, 1, core)
                wait_all(r2.at[u, LATE, 1, pl.ds(0, NG)], rsem.at[u, MATE + 1])
                assemble(u, LATE, 1, mate)
            if u == 0:
                tri = mm(y0[LATE, rows, :], e0[...]).astype(BF16)
            else:
                tri = (part1[rows, :] + mm(e1[rows, 256:], y1[LATE, 256:])).astype(BF16)
            for ci in range(2):
                for t in range(2):
                    for q in range(2):
                        at = slice(128 * q, 128 * q + 128)
                        base = (ci * n_r + 2 * t) * NZ
                        c0 = tri[base : base + NZ, at]
                        c1 = tri[base + NZ : base + 2 * NZ, at] if 2 * t + 1 < n_r else jnp.zeros_like(c0)
                        c1 = pltpu.roll(c1, 64, 1)
                        s3[u, h, ci * 4 + 2 * q, :, 128 * t : 128 * t + 128] = jnp.where(low, c0, c1)
                        s3[u, h, ci * 4 + 2 * q + 1, :, 128 * t : 128 * t + 128] = jnp.where(low, c1, c0)

            for d in (2, 1, 3, 0):
                q = lax.rem(g + d, 4)
                to = 4 * j_half + q
                for ci in (mate, core):
                    send(
                        s3.at[u, h, ci * 4 + q], r3.at[u, h, g], u, B1 + h, dev(i_half, z, ci, to),
                        (i_half == yl) & (to == g) if d == 0 and ci is core else None,
                    )

        for h in range(2):
            wait_all(r3.at[u, h], rsem.at[u, B1 + h])
            x = r3[u, h].reshape(NG * NZ, HALF)
            x = jnp.concatenate([x[:, :128], x[:, 128:]], axis=0)
            s4[u, h] = mm(perm[...], x).astype(BF16).reshape(NZ, 16, 128)
            send_z(s4.at[u, h], r4.at[u, h], u, B2 + h)
        for h in range(2):
            wait_all(r4.at[u, h], rsem.at[u, B2 + h])
            finish(u, h)
            if u == 0:
                norm(h)
                push(1, h)
            else:
                ztok[lanes(h), :] = zt[:, lanes(h)].T
                for r in range(4 * h, min(4 * h + 4, ROWS)):
                    out_ref[r] = ztok[slot_rows(r), :].astype(BF16)

    def wait_sent(u, stage, ref, count, less):
        @pl.when(less)
        def _():
            wait_all(ref.at[pl.ds(0, count - 1)], ssem.at[u, stage])

        @pl.when(jnp.logical_not(less))
        def _():
            wait_all(ref.at[pl.ds(0, count)], ssem.at[u, stage])

    for u in range(2):
        a = yl if u == 0 else g // 4
        for h in range(2):
            if u == 0 and h == 1:
                wait_all(st.at[pl.ds(0, NZ - 1)], ssem.at[u, TAIL])
                wait_all(s1d.at[pl.ds(0, NZ - 1)], ssem.at[u, F1 + 1])
            else:
                wait_all(s1.at[u, h, pl.ds(0, NZ - 1)], ssem.at[u, F1 + h])
        for h in range(2):
            wait_sent(u, F2 + h, r2.at[u, EARLY, h], 2 * NG, a == core)
            wait_sent(u, F2 + 2 + h, r2.at[u, LATE, h], NG, a == yl)
            wait_all(r2.at[u, LATE, h, pl.ds(0, NG)], ssem.at[u, MATE + h])
            wait_sent(u, B1 + h, s3.at[u, h], 8, g // 4 == core if u == 0 else (core == yl) & (g // 4 == yl))
            wait_all(s4.at[u, h, pl.ds(0, NZ - 1)], ssem.at[u, B2 + h])


def body(pair, pair_mask, w_ab, w_gate, w_out):
    return pl.pallas_call(
        kernel,
        out_shape=pltpu.VMEM(pair.shape, pair.dtype),
        in_specs=[pl.BlockSpec(memory_space=pltpu.HBM)] * 5,
        out_specs=pl.BlockSpec(memory_space=pltpu.VMEM),
        scratch_shapes=[
            pltpu.VMEM((ROWS, COLS, CH), BF16),
            pltpu.VMEM((ROWS, COLS), jnp.int32),
            pltpu.VMEM((2, CH, 4 * CH), BF16),
            pltpu.VMEM((2, CH, CH), BF16),
            pltpu.VMEM((2, CH, CH), BF16),
            pltpu.VMEM((2, 4 * CH, CH), BF16),
            pltpu.VMEM((2, CH, CH), BF16),
            pltpu.VMEM((2, CH, CH), BF16),
            pltpu.VMEM((256, 256), BF16),
            pltpu.VMEM((224, 256), BF16),
            pltpu.VMEM((TOK, TOK), BF16),
            pltpu.VMEM((NZ, 16, 128), BF16),
            pltpu.VMEM((NZ, 16, 128), BF16),
            pltpu.VMEM((NZ, 1, 128), F32),
            pltpu.VMEM((NZ, 1, 128), F32),
            pltpu.VMEM((256, 256), BF16),
            pltpu.VMEM((TOK, CH), F32),
            pltpu.VMEM((CH, TOK), F32),
            pltpu.VMEM((CH, TOK), BF16),
            pltpu.VMEM((CH, TOK), F32),
            pltpu.VMEM((2, 2, NZ, 16, HALF), BF16),
            pltpu.VMEM((2, 2, NZ, 16, HALF), BF16),
            pltpu.VMEM((2, 2, 2, NG, NZ, HALF), BF16),
            pltpu.VMEM((2, 2, 2, 16, NZ, HALF), BF16),
            pltpu.VMEM((2, 224, 512), BF16),
            pltpu.VMEM((2, 448, 256), BF16),
            pltpu.VMEM((512, 256), BF16),
            pltpu.VMEM((224, 448), BF16),
            pltpu.VMEM((512, 256), F32),
            pltpu.VMEM((224, 256), F32),
            pltpu.VMEM((2, 2, 8, NZ, HALF), BF16),
            pltpu.VMEM((2, 2, 8, NZ, HALF), BF16),
            pltpu.VMEM((2, 2, NZ, 16, 128), BF16),
            pltpu.VMEM((2, 2, NZ, 16, 128), BF16),
            pltpu.SemaphoreType.DMA((6,)),
            pltpu.SemaphoreType.DMA((2, STAGES)),
            pltpu.SemaphoreType.DMA((2, STAGES)),
        ],
        compiler_params=pltpu.CompilerParams(
            collective_id=0, has_side_effects=True, vmem_limit_bytes=32 * 1024 * 1024
        ),
        name="triangle",
    )(*(pltpu.with_memory_space_constraint(x, pltpu.HBM) for x in (pair, pair_mask, w_ab, w_gate, w_out)))


def solution(mesh):
    return jax.shard_map(
        body,
        mesh=mesh,
        in_specs=(P("row", "grp", None), P("row", "grp"), P(), P(), P()),
        out_specs=P("row", "grp", None),
        check_vma=False,
    )
```
